32 devices in a mesh: dp: 16 (over z, y, core), blk: 2 (over x).
Axes of the slice: x: 2, y: 2, z: 4, core: 2. Of those that a mesh axis runs over, the one named last changes fastest.
Arguments:
- inputs: bfloat16 [16, 2, 1024, 768], P('dp', 'blk'), may hold values from -6 to 6
- cotangent: bfloat16 [16, 2, 1024, 768], P('dp', 'blk'), may hold values from -6 to 6
- lengths: int32 [16], P('dp'), may hold values from 1025 to 2048, as said below
- groups: int32 [16], P('dp'), may hold values from 0 to 1, as said below
- flip: int32 [16], P('dp'), may hold values from 0 to 1
- w_qkv: bfloat16 [768, 2304], replicated, may hold values from -0.21875 to 0.21875
- b_query: float32 [768], replicated, may hold values from -1.5 to 1.5
- b_value: float32 [768], replicated, may hold values from -1.5 to 1.5
- w_out: bfloat16 [768, 768], replicated, may hold values from -0.875 to 0.875
- b_out: float32 [768], replicated, may hold values from -1.5 to 1.5
- gain_one: float32 [768], replicated, may hold values from 0.5 to 1.5
- shift_one: float32 [768], replicated, may hold values from -1.5 to 1.5
- gain_two: float32 [768], replicated, may hold values from 0.5 to 1.5
- shift_two: float32 [768], replicated, may hold values from -1.5 to 1.5
- w_fc: bfloat16 [768, 3072], replicated, may hold values from -0.21875 to 0.21875
- b_fc: float32 [3072], replicated, may hold values from -1.5 to 1.5
- w_proj: bfloat16 [3072, 768], replicated, may hold values from -0.109375 to 0.109375
- b_proj: float32 [768], replicated, may hold values from -1.5 to 1.5
Outputs:
- block_out: bfloat16 [16, 2, 1024, 768], P('dp', 'blk')
- input_grad: bfloat16 [16, 2, 1024, 768], P('dp', 'blk')
- grad_w_qkv: float32 [768, 2304], replicated
- grad_b_query: float32 [768], replicated
- grad_b_value: float32 [768], replicated
- grad_w_out: float32 [768, 768], replicated
- grad_b_out: float32 [768], replicated
- grad_gain_one: float32 [768], replicated
- grad_shift_one: float32 [768], replicated
- grad_gain_two: float32 [768], replicated
- grad_shift_two: float32 [768], replicated
- grad_w_fc: float32 [768, 3072], replicated
- grad_b_fc: float32 [3072], replicated
- grad_w_proj: float32 [3072, 768], replicated
- grad_b_proj: float32 [768], replicated
- group_rms: float32 [2, 3], replicated
The draws below stay inside these ranges and needn't reach their ends.
Inputs may be any that keep to these rules, and one draw needn't show every extreme that they name: Both groups are present; group 0 lengths exceed 3 * 512 and some reaches 2048; group 1 lengths exceed 1024 and some equals 1536. Each of the two groups holds at least one sequence.
All inputs are finite; a program needn't handle non-finite values.
Results may differ from the reference program's by a relative error of at most 0.012.
Values may be sent and summed in bfloat16 or wider, within the bound.
No kernel may reach another device: no remote copies, remote signals or barrier semaphores. Data moves between devices by JAX's collectives and lax.ppermute only.
A program may use at most 320 MiB of HBM per device.

```python
import jax
import jax.numpy as jnp
from jax import lax

D = 768
H = 12
HD = 64
FF = 3072
SPAN = 1024
SEQ = 2048
SEQS = 16


def slot_tables(key):
    order = jax.random.permutation(jax.random.fold_in(key, 11), SEQS)
    member = jax.random.randint(jax.random.fold_in(key, 12), (SEQS,), 0, 2)
    member = member.at[order[0]].set(0).at[order[1]].set(1)
    long_len = jax.random.randint(jax.random.fold_in(key, 13), (SEQS,), 3 * SEQ // 4 + 1, SEQ + 1)
    short_len = jax.random.randint(jax.random.fold_in(key, 14), (SEQS,), SPAN + 1, 3 * SEQ // 4 + 1)
    sizes = jnp.where(member == 0, long_len, short_len)
    sizes = sizes.at[order[0]].set(SEQ).at[order[1]].set(3 * SEQ // 4)
    return (member.astype(jnp.int32), sizes.astype(jnp.int32))


def draw_lengths(key, part):
    member, sizes = slot_tables(key)
    return sizes


def draw_groups(key, part):
    member, sizes = slot_tables(key)
    return member


def draw_flip(key, part):
    key = jax.random.fold_in(key, 5)
    return jax.random.randint(key, (SEQS,), 0, 2).astype(jnp.int32)


def block_scale(stream_key, shape, shards, smallest, largest):
    loudness = 1.0
    for axis_at, parts in shards:
        draws = jax.random.uniform(jax.random.fold_in(jax.random.fold_in(stream_key, 6), axis_at), (parts,), jnp.float32, smallest / len(shards), largest / len(shards))
        loudness = loudness * jnp.repeat(jnp.exp(draws), shape[axis_at] // parts).reshape((-1,) + (1,) * (len(shape) - 1 - axis_at))
    return loudness


def scatter_about(key, dims, deviation, most, pieces=(), kind=jnp.bfloat16):
    array = deviation * jax.random.normal(key, dims, jnp.float32)
    if pieces:
        array = array * block_scale(key, dims, pieces, -0.22, 0.18)
    return jnp.clip(array, -most, most).astype(kind)


def setup_inputs(seed: int = 0) -> dict:
    key_of = jax.random.split(jax.random.key(seed), 19)
    return {
        "inputs": scatter_about(key_of[0], (SEQS, 2, SPAN, D), 1.0, 6.0, ((0, 16), (1, 2))),
        "cotangent": scatter_about(key_of[1], (SEQS, 2, SPAN, D), 1.0, 6.0, ((0, 16), (1, 2))),
        "lengths": draw_lengths(jax.random.fold_in(key_of[18], 71), 0),
        "groups": draw_groups(jax.random.fold_in(key_of[18], 71), 0),
        "flip": draw_flip(jax.random.fold_in(key_of[18], 71), 0),
        "w_qkv": scatter_about(key_of[5], (D, 3 * D), D ** -0.5, 0.21875),
        "b_query": scatter_about(key_of[6], (D,), 0.3, 1.5, (), jnp.float32),
        "b_value": scatter_about(key_of[7], (D,), 0.3, 1.5, (), jnp.float32),
        "w_out": scatter_about(key_of[8], (D, D), (D // 16) ** -0.5, 0.875),
        "b_out": scatter_about(key_of[9], (D,), 0.3, 1.5, (), jnp.float32),
        "gain_one": jnp.clip(1.0 + 0.1 * jax.random.normal(key_of[10], (D,), jnp.float32), 0.5, 1.5),
        "shift_one": scatter_about(key_of[11], (D,), 0.3, 1.5, (), jnp.float32),
        "gain_two": jnp.clip(1.0 + 0.1 * jax.random.normal(key_of[12], (D,), jnp.float32), 0.5, 1.5),
        "shift_two": scatter_about(key_of[13], (D,), 0.3, 1.5, (), jnp.float32),
        "w_fc": scatter_about(key_of[14], (D, FF), D ** -0.5, 0.21875),
        "b_fc": scatter_about(key_of[15], (FF,), 0.3, 1.5, (), jnp.float32),
        "w_proj": scatter_about(key_of[16], (FF, D), FF ** -0.5, 0.109375),
        "b_proj": scatter_about(key_of[17], (D,), 0.3, 1.5, (), jnp.float32),
    }


EPS = 1e-05
HIGH = lax.Precision.HIGHEST

@jax.custom_vjp
def low(v):
    return lax.optimization_barrier(v.astype(jnp.bfloat16)).astype(jnp.float32)

@jax.custom_vjp
def low_back(v):
    return v

def low_keep(v):
    return (low(v), None)

def low_pass(kept, grad):
    return (grad,)

def back_keep(v):
    return (v, None)

def back_low(kept, grad):
    return (low(grad),)
low.defvjp(low_keep, low_pass)
low_back.defvjp(back_keep, back_low)

def matmul(left, right):
    return jnp.dot(left, right, precision=HIGH, preferred_element_type=jnp.float32)

def layer_norm(values, gain, shift):
    centered = values - lax.optimization_barrier(jnp.mean(values, -1, keepdims=True))
    inv_std = lax.rsqrt(lax.optimization_barrier(jnp.mean(centered * centered, -1, keepdims=True)) + EPS)
    return centered * inv_std * gain + shift

def attention(query, key_mat, value_mat, length):
    scale = HD ** (-0.5)
    block_rows = min(512, SEQ)
    query_heads = query.reshape(SEQ, H, HD)
    key_heads = key_mat.reshape(SEQ, H, HD)
    value_heads = value_mat.reshape(SEQ, H, HD)
    key_pos = jnp.arange(SEQ, dtype=jnp.int32)

    def one_block(offset):
        q_block = lax.dynamic_slice_in_dim(query_heads, offset, block_rows, 0)
        scores = jnp.einsum('qhd,khd->hqk', q_block, key_heads, precision=HIGH) * scale
        scores = low_back(scores)
        q_pos = offset + jnp.arange(block_rows, dtype=jnp.int32)
        allowed = (key_pos[None, :] <= q_pos[:, None]) & (key_pos[None, :] < length)
        scores = jnp.where(allowed[None], scores, -1e+30)
        row_max = lax.optimization_barrier(jnp.max(scores, -1, keepdims=True))
        expo = jnp.exp(scores - row_max)
        probs = low(expo / lax.optimization_barrier(jnp.sum(expo, -1, keepdims=True)))
        return jnp.einsum('hqk,khd->qhd', probs, value_heads, precision=HIGH).reshape(block_rows, D)
    offsets = jnp.arange(SEQ // block_rows, dtype=jnp.int32) * block_rows
    return lax.map(jax.checkpoint(one_block), offsets).reshape(SEQ, D)

def forward(seq_x, length, params):
    w_qkv, b_query, b_value, w_out, b_out, gain_one, shift_one, gain_two, shift_two, w_fc, b_fc, w_proj, b_proj = params
    normed = low(layer_norm(seq_x, gain_one, shift_one))
    qkv = matmul(normed, w_qkv)
    query = low(low_back(qkv[:, :D] + b_query))
    key_mat = low(low_back(qkv[:, D:2 * D]))
    value_mat = low(low_back(qkv[:, 2 * D:] + b_value))
    attended = low(low_back(attention(query, key_mat, value_mat, length)))
    branch_att = low_back(matmul(attended, w_out) + b_out)
    middle = seq_x + branch_att
    normed_two = low(layer_norm(middle, gain_two, shift_two))
    pre_act = low_back(matmul(normed_two, w_fc) + b_fc)
    activ = low(jax.nn.gelu(pre_act, approximate=True))
    branch_mlp = low_back(matmul(activ, w_proj) + b_proj)
    return (middle + branch_mlp, (branch_att, branch_mlp))

def to_sequence(arr, flip):
    turned = jnp.where((flip == 1)[:, None, None, None], arr[:, ::-1], arr)
    return turned.reshape(SEQS, SEQ, D)

def to_spans(arr, flip):
    stacked = arr.reshape(SEQS, 2, SPAN, D)
    return jnp.where((flip == 1)[:, None, None, None], stacked[:, ::-1], stacked)

def reference(inputs, cotangent, lengths, groups, flip, w_qkv, b_query, b_value, w_out, b_out, gain_one, shift_one, gain_two, shift_two, w_fc, b_fc, w_proj, b_proj):
    seq_x = to_sequence(inputs.astype(jnp.float32), flip)
    seq_cot = to_sequence(cotangent.astype(jnp.float32), flip)
    params = (w_qkv.astype(jnp.float32), b_query, b_value, w_out.astype(jnp.float32), b_out, gain_one, shift_one, gain_two, shift_two, w_fc.astype(jnp.float32), b_fc, w_proj.astype(jnp.float32), b_proj)

    def run(all_x, weights):
        return lax.map(lambda pair: forward(pair[0], pair[1], weights), (all_x, lengths))
    outputs, pull, extras = jax.vjp(run, seq_x, params, has_aux=True)
    grad_x, grads = pull(seq_cot)
    branch_att, branch_mlp = extras
    valid = (jnp.arange(SEQ, dtype=jnp.int32)[None, :] < lengths[:, None]).astype(jnp.float32)
    member = (groups[:, None] == jnp.arange(2, dtype=jnp.int32)[None, :]).astype(jnp.float32)
    squares = jnp.stack([lax.optimization_barrier(jnp.sum(outputs * outputs, -1)), lax.optimization_barrier(jnp.sum(branch_att * branch_att, -1)), lax.optimization_barrier(jnp.sum(branch_mlp * branch_mlp, -1))], -1)
    per_seq = lax.optimization_barrier(jnp.sum(squares * valid[:, :, None], 1))
    group_sums = matmul(member.T, per_seq)
    counts = matmul(member.T, lax.optimization_barrier(jnp.sum(valid, 1))[:, None])
    group_rms = jnp.sqrt(group_sums / (counts * D))
    return (to_spans(outputs, flip).astype(jnp.bfloat16), to_spans(grad_x, flip).astype(jnp.bfloat16), grads[0], grads[1], grads[2], grads[3], grads[4], grads[5], grads[6], grads[7], grads[8], grads[9], grads[10], grads[11], grads[12], group_rms)
```

```python
import jax
import jax.numpy as jnp
from jax import lax
from jax.experimental import pallas as pl
from jax.experimental.pallas import tpu as pltpu
from jax.sharding import PartitionSpec as P

SP = 1024
W = 768
NP = 6
EPS = 1e-05
NEG=-1e30
f32 = jnp.float32
bf16 = jnp.bfloat16
def tdot(a,b): return lax.dot_general(a,b,(((1,),(1,)),((),())),preferred_element_type=f32)
def dot(a,b): return jnp.dot(a,b,preferred_element_type=f32)
def head_masks():
    lane=lax.broadcasted_iota(jnp.int32,(1,128),1)
    return [lane<64, lane>=64]
def softmax_t(s):
    m=jnp.max(s,0,keepdims=True)
    p=jnp.exp(s-m)
    l=jnp.sum(p,0,keepdims=True)
    return m,l,p.astype(bf16)
DQ=256
def diag_fwd(place_ref, klen_ref, q_ref,k_ref,v_ref,o_ref,l_ref):
    hm=head_masks(); klen=klen_ref[0]
    q=q_ref[...]*jnp.asarray(0.125,bf16)
    vt=v_ref[...].T
    z=jnp.zeros((),bf16)
    tiles=[(qi,h) for qi in range(SP//DQ) for h in range(2)]
    kpos=lax.broadcasted_iota(jnp.int32,(SP,1),0)
    low=jnp.where(kpos<klen,kpos,SP)
    def scores(t):
        qi,h=t; n=(qi+1)*DQ
        ok=(qi*DQ+lax.broadcasted_iota(jnp.int32,(n,DQ),1))>=low[:n]
        return jnp.where(ok,tdot(k_ref[:n],jnp.where(hm[h],q[qi*DQ:n],z)),NEG)
    def finish(t,m,l,p):
        qi,h=t; n=(qi+1)*DQ; sl=slice(qi*DQ,n)
        acc=dot(vt[h*64:(h+1)*64,:n],p)
        o_ref[0,h*64:(h+1)*64,sl]=acc*(1.0/l)
        l_ref[0,h:h+1,sl]=m+jnp.log(l)
    pipeline(tiles,scores,softmax_t,finish)
def pipeline(tiles,scores,mid,finish,depth=2):
    s=scores(tiles[0]); pend=None
    for i,t in enumerate(tiles):
        sn=scores(tiles[i+1]) if i+1<len(tiles) else None
        r=mid(s) if not isinstance(s,tuple) else mid(t,*s)
        if depth==2:
            if pend: finish(*pend)
            pend=(t,)+r
        else: finish(t,*r)
        s=sn
    if pend: finish(*pend)
CQ=512
def cross_fwd(place_ref, klen_ref, q_ref,k_ref,v_ref,od_ref,ld_ref,o_ref,l_ref):
    hm=head_masks()
    @pl.when(place_ref[0]==1)
    def _():
        q=q_ref[...]*jnp.asarray(0.125,bf16)
        vt=v_ref[...].T
        z=jnp.zeros((),bf16)
        tiles=[(qi,h) for qi in range(SP//CQ) for h in range(2)]
        res={}
        def scores(t):
            qi,h=t
            return tdot(k_ref[...],jnp.where(hm[h],q[qi*CQ:(qi+1)*CQ],z))
        def finish(t,m,l,p):
            qi,h=t; sl=slice(qi*CQ,(qi+1)*CQ)
            acc=dot(vt[h*64:(h+1)*64],p)
            ld=ld_ref[0,h:h+1,sl]
            lx=m+jnp.log(l)
            mx=jnp.maximum(ld,lx)
            ed=jnp.exp(ld-mx); ex=jnp.exp(lx-mx); tot=ed+ex
            l_ref[0,h:h+1,sl]=mx+jnp.log(tot)
            res[t]=od_ref[0,h*64:(h+1)*64,sl]*(ed/tot)+acc*(ex/(tot*l))
            if h==1: o_ref[sl]=jnp.concatenate([res[(qi,0)],res[(qi,1)]],0).T.astype(bf16)
        pipeline(tiles,scores,softmax_t,finish)
    @pl.when(place_ref[0]==0)
    def _():
        o_ref[...]=od_ref[0].T.astype(bf16)
        l_ref[...]=ld_ref[...]
KB=256
def bwd_prep(q_ref,do_ref,hm):
    q=q_ref[...]*jnp.asarray(0.125,bf16)
    z=jnp.zeros((),bf16)
    do=do_ref[...]
    return [jnp.where(hm[h],q,z) for h in range(2)],[jnp.where(hm[h],do,z) for h in range(2)]
def bwd_tiles(k_ref,v_ref,qm,dm,lrow,drow,dk_ref,dv_ref,dqt,start,mask):
    tiles=[(kb,h) for kb in range(SP//KB) for h in range(2)]
    acc={}
    kts={}
    def scores(t):
        kb,h=t; ks=slice(kb*KB,(kb+1)*KB); q0=start(kb)
        return tdot(k_ref[ks],qm[h][q0:]),tdot(v_ref[ks],dm[h][q0:])
    def mid(t,s,dp):
        kb,h=t; q0=start(kb)
        p=jnp.exp(s-lrow(h)[:,q0:])
        if mask is not None: p=jnp.where(mask(kb),p,0.0)
        ds=p*(dp-drow(h)[:,q0:])
        return p.astype(bf16),ds.astype(bf16)
    def finish(t,p,ds):
        kb,h=t; ks=slice(kb*KB,(kb+1)*KB); q0=start(kb)
        if h==0: kts[kb]=k_ref[ks].T
        a=dot(p,dm[h][q0:]); b=dot(ds,qm[h][q0:])
        if h==0: acc[kb]=(a,b)
        else:
            dv_ref[ks]=(acc[kb][0]+a).astype(bf16); dk_ref[ks]=(acc[kb][1]+b).astype(bf16)
        c=dot(kts[kb][h*64:(h+1)*64],ds)
        if kb==0: dqt[h*64:(h+1)*64]=c
        else: dqt[h*64:(h+1)*64,q0:]+=c
    pipeline(tiles,scores,mid,finish)
def cross_bwd(place_ref, klen_ref, q_ref,k_ref,v_ref,do_ref,o_ref,l_ref,dq_ref,dk_ref,dv_ref,dl_ref,dqt):
    hm=head_masks()
    prod=do_ref[...].astype(f32)*o_ref[...].astype(f32)
    t=prod.T
    dl_ref[0,0:1]=jnp.sum(t[:64],0,keepdims=True); dl_ref[0,1:2]=jnp.sum(t[64:],0,keepdims=True)
    @pl.when(place_ref[0]==1)
    def _():
        qm,dm=bwd_prep(q_ref,do_ref,hm)
        bwd_tiles(k_ref,v_ref,qm,dm,lambda h:l_ref[0,h:h+1],lambda h:dl_ref[0,h:h+1],dk_ref,dv_ref,dqt,lambda kb:0,None)
        dq_ref[...]=dqt[...].T*0.125
    @pl.when(place_ref[0]==0)
    def _():
        dk_ref[...]=jnp.zeros_like(dk_ref); dv_ref[...]=jnp.zeros_like(dv_ref); dq_ref[...]=jnp.zeros_like(dq_ref)
def diag_bwd(place_ref, klen_ref, q_ref,k_ref,v_ref,do_ref,l_ref,dl_ref,dqx_ref,dq_ref,dk_ref,dv_ref,dqt):
    hm=head_masks(); klen=klen_ref[0]
    qm,dm=bwd_prep(q_ref,do_ref,hm)
    kpos=lax.broadcasted_iota(jnp.int32,(SP,1),0)
    low=jnp.where(kpos<klen,kpos,SP)
    def mask(kb):
        q0=kb*KB
        return q0+lax.broadcasted_iota(jnp.int32,(KB,SP-q0),1)>=low[q0:q0+KB]
    bwd_tiles(k_ref,v_ref,qm,dm,lambda h:l_ref[0,h:h+1],lambda h:dl_ref[0,h:h+1],dk_ref,dv_ref,dqt,lambda kb:kb*KB,mask)
    dq_ref[...]=(dqt[...].T*0.125+dqx_ref[...]).astype(bf16)
def col(base): return pl.BlockSpec((SP,128),lambda j,*_:(0,base+j))
ROW=pl.BlockSpec((1,8,SP),lambda j,*_:(j,0,0))
def call(fn,place,klen,ins,in_specs,outs,out_specs,scratch=(),flops=0):
    return pl.pallas_call(fn,
        grid_spec=pltpu.PrefetchScalarGridSpec(num_scalar_prefetch=2,grid=(NP,),in_specs=in_specs,out_specs=out_specs,scratch_shapes=list(scratch)),
        out_shape=outs,
        compiler_params=pltpu.CompilerParams(vmem_limit_bytes=50*1024*1024,dimension_semantics=("arbitrary",)),
        cost_estimate=pl.CostEstimate(flops=flops,bytes_accessed=10**7,transcendentals=10**7),
        name=fn.__name__,
    )(place,klen,*ins)
S=jax.ShapeDtypeStruct
def fwd(place,klen,qkv,kvr):
    c=col(0)
    T=pl.BlockSpec((1,128,SP),lambda j,*_:(j,0,0))
    od,ld=call(diag_fwd,place,klen,(qkv,qkv,qkv),[c,col(6),col(12)],[S((NP,128,SP),f32),S((NP,8,SP),f32)],[T,ROW])
    o,l=call(cross_fwd,place,klen,(qkv,kvr,kvr,od,ld),[c,c,col(6),T,ROW],[S((SP,W),bf16),S((NP,8,SP),f32)],[c,ROW])
    return o,l
def bwd(place,klen,qkv,kvr,do,o,l):
    c=col(0)
    acc=pltpu.VMEM((128,SP),f32)
    dqx,dkr,dvr,dl=call(cross_bwd,place,klen,(qkv,kvr,kvr,do,o,l),[c,c,col(6),c,c,ROW],
        [S((SP,W),f32),S((SP,W),bf16),S((SP,W),bf16),S((NP,8,SP),f32)],[c,c,c,ROW],[acc])
    dq,dk,dv=call(diag_bwd,place,klen,(qkv,qkv,qkv,do,l,dl,dqx),[c,col(6),col(12),c,ROW,ROW,c],[S((SP,W),bf16)]*3,[c,c,c],[acc])
    return dq,dk,dv,dkr,dvr


def swap_spans(x):
    return lax.ppermute(x, "blk", [(0, 1), (1, 0)])


def normalize(values, gain, shift):
    centered = values - jnp.mean(values, -1, keepdims=True)
    inv_std = lax.rsqrt(jnp.mean(centered * centered, -1, keepdims=True) + EPS)
    x_hat = centered * inv_std
    return x_hat * gain + shift, x_hat, inv_std


def norm_back(upstream, x_hat, inv_std, gain):
    scaled = upstream * gain
    inner = (
        scaled
        - jnp.mean(scaled, -1, keepdims=True)
        - x_hat * jnp.mean(scaled * x_hat, -1, keepdims=True)
    )
    return inv_std * inner, jnp.sum(upstream * x_hat, 0), jnp.sum(upstream, 0)


def rows_dot(left, right):
    return lax.dot_general(left, right, (((0,), (0,)), ((), ())), preferred_element_type=f32)


def body(
    inputs, cotangent, lengths, groups, flip,
    w_qkv, b_query, b_value, w_out, b_out, gain_one, shift_one, gain_two, shift_two,
    w_fc, b_fc, w_proj, b_proj,
):
    place = jnp.bitwise_xor(lax.axis_index("blk"), flip[0])
    klen = jnp.minimum(lengths[0] - place * SP, SP)
    place_s = place.reshape(1).astype(jnp.int32)
    klen_s = klen.reshape(1).astype(jnp.int32)
    x_b = inputs[0, 0]
    up_b = cotangent[0, 0]
    xr_b = swap_spans(x_b)

    x_in = x_b.astype(f32)
    normed_f, x_hat_one, inv_one = normalize(x_in, gain_one, shift_one)
    normed = normed_f.astype(bf16)
    qkv_bias = jnp.concatenate([b_query, jnp.zeros_like(b_value), b_value])
    qkv = (dot(normed, w_qkv) + qkv_bias).astype(bf16)
    c = col(0)
    tall = pl.BlockSpec((1, 128, SP), lambda j, *_: (j, 0, 0))
    od, ld = call(
        diag_fwd, place_s, klen_s, (qkv, qkv, qkv), [c, col(6), col(12)],
        [S((NP, 128, SP), f32), S((NP, 8, SP), f32)], [tall, ROW],
    )
    d_act = tdot(up_b, w_proj).astype(bf16)

    normed_r = normalize(xr_b.astype(f32), gain_one, shift_one)[0].astype(bf16)
    kvr = (dot(normed_r, w_qkv[:, W:]) + qkv_bias[W:]).astype(bf16)
    attended, lse = call(
        cross_fwd, place_s, klen_s, (qkv, kvr, kvr, od, ld), [c, c, col(6), tall, ROW],
        [S((SP, W), bf16), S((NP, 8, SP), f32)], [c, ROW],
    )

    branch_att = dot(attended, w_out) + b_out
    middle = x_in + branch_att
    normed_two_f, x_hat_two, inv_two = normalize(middle, gain_two, shift_two)
    normed_two = normed_two_f.astype(bf16)
    pre_act = dot(normed_two, w_fc) + b_fc
    gelu_val, gelu_back = jax.vjp(lambda val: jax.nn.gelu(val, approximate=True), pre_act)
    activ = gelu_val.astype(bf16)
    branch_mlp = dot(activ, w_proj) + b_proj
    outputs = middle + branch_mlp
    upstream = up_b.astype(f32)
    grad_pre = gelu_back(d_act.astype(f32))[0].astype(bf16)
    grad_w_proj = rows_dot(activ, up_b).astype(bf16)
    grad_w_fc = rows_dot(normed_two, grad_pre).astype(bf16)
    grad_mid_norm, grad_gain_two, grad_shift_two = norm_back(
        tdot(grad_pre, w_fc), x_hat_two, inv_two, gain_two
    )
    grad_middle = upstream + grad_mid_norm
    grad_att = grad_middle.astype(bf16)
    grad_w_out = rows_dot(attended, grad_att).astype(bf16)
    grad_attended = tdot(grad_att, w_out).astype(bf16)
    early = lax.psum((grad_w_proj, grad_w_fc, grad_w_out), ("blk", "dp"))

    acc = pltpu.VMEM((128, SP), f32)
    dqx, dkr, dvr, delta = call(
        cross_bwd, place_s, klen_s, (qkv, kvr, kvr, grad_attended, attended, lse),
        [c, c, col(6), c, c, ROW],
        [S((SP, W), f32), S((SP, W), bf16), S((SP, W), bf16), S((NP, 8, SP), f32)],
        [c, c, c, ROW], [acc],
    )
    w_q, w_k, w_v = w_qkv[:, :W], w_qkv[:, W : 2 * W], w_qkv[:, 2 * W :]
    returned = swap_spans((tdot(dkr, w_k) + tdot(dvr, w_v)).astype(bf16))
    dq, dk, dv = call(
        diag_bwd, place_s, klen_s, (qkv, qkv, qkv, grad_attended, lse, delta, dqx),
        [c, col(6), col(12), c, ROW, ROW, c], [S((SP, W), bf16)] * 3, [c, c, c], [acc],
    )
    grad_w_q = rows_dot(normed, dq).astype(bf16)
    grad_w_k = (rows_dot(normed, dk) + rows_dot(normed_r, dkr)).astype(bf16)
    grad_w_v = (rows_dot(normed, dv) + rows_dot(normed_r, dvr)).astype(bf16)
    late = lax.psum((grad_w_q, grad_w_k, grad_w_v), ("dp", "blk"))
    grad_b_query = jnp.sum(dq.astype(f32), 0)
    grad_b_value = jnp.sum(dv.astype(f32), 0) + jnp.sum(dvr.astype(f32), 0)

    grad_normed = tdot(dq, w_q) + tdot(dk, w_k) + tdot(dv, w_v) + returned.astype(f32)
    grad_x_norm, grad_gain_one, grad_shift_one = norm_back(
        grad_normed, x_hat_one, inv_one, gain_one
    )
    input_grad = (grad_middle + grad_x_norm).astype(bf16)

    valid = (jnp.arange(SP, dtype=jnp.int32) < klen).astype(f32)
    member = (groups[0] == jnp.arange(2, dtype=jnp.int32)).astype(f32)
    sums = jnp.stack(
        [jnp.sum(valid * jnp.sum(v * v, -1)) for v in (outputs, branch_att, branch_mlp)]
        + [jnp.sum(valid)]
    )
    small = lax.psum(
        jnp.concatenate([
            grad_b_query, grad_b_value, jnp.sum(grad_att.astype(f32), 0),
            grad_gain_one, grad_shift_one, grad_gain_two, grad_shift_two,
            jnp.sum(grad_pre.astype(f32), 0), jnp.sum(upstream, 0),
            (member[:, None] * sums[None, :]).reshape(-1),
        ]),
        ("dp", "blk"),
    )
    sizes = [W] * 7 + [4 * W, W]
    pieces = []
    at = 0
    for size in sizes:
        pieces.append(small[at : at + size])
        at += size
    table = small[at : at + 8].reshape(2, 4)
    group_rms = jnp.sqrt(table[:, :3] / (table[:, 3:] * W))
    g_bq, g_bv, g_bo, g_g1, g_s1, g_g2, g_s2, g_bfc, g_bp = pieces
    return (
        outputs.astype(bf16)[None, None], input_grad[None, None],
        jnp.concatenate(late, 1).astype(f32), g_bq, g_bv, early[2].astype(f32), g_bo,
        g_g1, g_s1, g_g2, g_s2, early[1].astype(f32), g_bfc, early[0].astype(f32), g_bp, group_rms,
    )


def solution(mesh):
    span = P("dp", "blk", None, None)
    return jax.shard_map(
        body,
        mesh=mesh,
        in_specs=(span, span, P("dp"), P("dp"), P("dp")) + (P(),) * 13,
        out_specs=(span, span) + (P(),) * 14,
        check_vma=False,
    )
```

```python
import jax
import jax.numpy as jnp
from jax import lax
from jax.experimental import pallas as pl
from jax.experimental.pallas import tpu as pltpu
from jax.sharding import PartitionSpec as P

SP = 1024
W = 768
NP = 6
EPS = 1e-05
NEG=-1e30
f32=jnp.float32; bf16=jnp.bfloat16
def tdot(a,b): return lax.dot_general(a,b,(((1,),(1,)),((),())),preferred_element_type=f32)
def dot(a,b): return jnp.dot(a,b,preferred_element_type=f32)
def head_masks():
    lane=lax.broadcasted_iota(jnp.int32,(1,128),1)
    return [lane<64, lane>=64]
def softmax_t(s):
    m=jnp.max(s,0,keepdims=True)
    p=jnp.exp(s-m)
    l=jnp.sum(p,0,keepdims=True)
    return m,l,p.astype(bf16)
DQ=256
def diag_fwd(place_ref, klen_ref, q_ref,k_ref,v_ref,o_ref,l_ref):
    hm=head_masks(); klen=klen_ref[0]
    q=q_ref[...]*jnp.asarray(0.125,bf16)
    vt=v_ref[...].T
    z=jnp.zeros((),bf16)
    tiles=[(qi,h) for qi in range(SP//DQ) for h in range(2)]
    kpos=lax.broadcasted_iota(jnp.int32,(SP,1),0)
    low=jnp.where(kpos<klen,kpos,SP)
    def scores(t):
        qi,h=t; n=(qi+1)*DQ
        ok=(qi*DQ+lax.broadcasted_iota(jnp.int32,(n,DQ),1))>=low[:n]
        return jnp.where(ok,tdot(k_ref[:n],jnp.where(hm[h],q[qi*DQ:n],z)),NEG)
    def finish(t,m,l,p):
        qi,h=t; n=(qi+1)*DQ; sl=slice(qi*DQ,n)
        acc=dot(vt[h*64:(h+1)*64,:n],p)
        o_ref[0,h*64:(h+1)*64,sl]=acc*(1.0/l)
        l_ref[0,h:h+1,sl]=m+jnp.log(l)
    pipeline(tiles,scores,softmax_t,finish)
def pipeline(tiles,scores,mid,finish,depth=2):
    s=scores(tiles[0]); pend=None
    for i,t in enumerate(tiles):
        sn=scores(tiles[i+1]) if i+1<len(tiles) else None
        r=mid(s) if not isinstance(s,tuple) else mid(t,*s)
        if depth==2:
            if pend: finish(*pend)
            pend=(t,)+r
        else: finish(t,*r)
        s=sn
    if pend: finish(*pend)
CQ=512
def cross_fwd(place_ref, klen_ref, q_ref,k_ref,v_ref,od_ref,ld_ref,o_ref,l_ref):
    hm=head_masks()
    @pl.when(place_ref[0]==1)
    def _():
        q=q_ref[...]*jnp.asarray(0.125,bf16)
        vt=v_ref[...].T
        z=jnp.zeros((),bf16)
        tiles=[(qi,h) for qi in range(SP//CQ) for h in range(2)]
        res={}
        def scores(t):
            qi,h=t
            return tdot(k_ref[...],jnp.where(hm[h],q[qi*CQ:(qi+1)*CQ],z))
        def finish(t,m,l,p):
            qi,h=t; sl=slice(qi*CQ,(qi+1)*CQ)
            acc=dot(vt[h*64:(h+1)*64],p)
            ld=ld_ref[0,h:h+1,sl]
            lx=m+jnp.log(l)
            mx=jnp.maximum(ld,lx)
            ed=jnp.exp(ld-mx); ex=jnp.exp(lx-mx); tot=ed+ex
            l_ref[0,h:h+1,sl]=mx+jnp.log(tot)
            res[t]=od_ref[0,h*64:(h+1)*64,sl]*(ed/tot)+acc*(ex/(tot*l))
            if h==1: o_ref[sl]=jnp.concatenate([res[(qi,0)],res[(qi,1)]],0).T.astype(bf16)
        pipeline(tiles,scores,softmax_t,finish)
    @pl.when(place_ref[0]==0)
    def _():
        o_ref[...]=od_ref[0].T.astype(bf16)
        l_ref[...]=ld_ref[...]
KB=256
def bwd_prep(q_ref,do_ref,hm):
    q=q_ref[...]*jnp.asarray(0.125,bf16)
    z=jnp.zeros((),bf16)
    do=do_ref[...]
    return [jnp.where(hm[h],q,z) for h in range(2)],[jnp.where(hm[h],do,z) for h in range(2)]
def bwd_tiles(k_ref,v_ref,qm,dm,lrow,drow,dk_ref,dv_ref,dqt,start,mask):
    tiles=[(kb,h) for kb in range(SP//KB) for h in range(2)]
    acc={}
    kts={}
    def scores(t):
        kb,h=t; ks=slice(kb*KB,(kb+1)*KB); q0=start(kb)
        return tdot(k_ref[ks],qm[h][q0:]),tdot(v_ref[ks],dm[h][q0:])
    def mid(t,s,dp):
        kb,h=t; q0=start(kb)
        p=jnp.exp(s-lrow(h)[:,q0:])
        if mask is not None: p=jnp.where(mask(kb),p,0.0)
        ds=p*(dp-drow(h)[:,q0:])
        return p.astype(bf16),ds.astype(bf16)
    def finish(t,p,ds):
        kb,h=t; ks=slice(kb*KB,(kb+1)*KB); q0=start(kb)
        if h==0: kts[kb]=k_ref[ks].T
        a=dot(p,dm[h][q0:]); b=dot(ds,qm[h][q0:])
        if h==0: acc[kb]=(a,b)
        else:
            dv_ref[ks]=(acc[kb][0]+a).astype(bf16); dk_ref[ks]=(acc[kb][1]+b).astype(bf16)
        c=dot(kts[kb][h*64:(h+1)*64],ds)
        if kb==0: dqt[h*64:(h+1)*64]=c
        else: dqt[h*64:(h+1)*64,q0:]+=c
    pipeline(tiles,scores,mid,finish)
def cross_bwd(place_ref, klen_ref, q_ref,k_ref,v_ref,do_ref,o_ref,l_ref,dq_ref,dk_ref,dv_ref,dl_ref,dqt):
    hm=head_masks()
    prod=do_ref[...].astype(f32)*o_ref[...].astype(f32)
    t=prod.T
    dl_ref[0,0:1]=jnp.sum(t[:64],0,keepdims=True); dl_ref[0,1:2]=jnp.sum(t[64:],0,keepdims=True)
    @pl.when(place_ref[0]==1)
    def _():
        qm,dm=bwd_prep(q_ref,do_ref,hm)
        bwd_tiles(k_ref,v_ref,qm,dm,lambda h:l_ref[0,h:h+1],lambda h:dl_ref[0,h:h+1],dk_ref,dv_ref,dqt,lambda kb:0,None)
        dq_ref[...]=dqt[...].T*0.125
    @pl.when(place_ref[0]==0)
    def _():
        dk_ref[...]=jnp.zeros_like(dk_ref); dv_ref[...]=jnp.zeros_like(dv_ref); dq_ref[...]=jnp.zeros_like(dq_ref)
def diag_bwd(place_ref, klen_ref, q_ref,k_ref,v_ref,do_ref,l_ref,dl_ref,dqx_ref,dq_ref,dk_ref,dv_ref,dqt):
    hm=head_masks(); klen=klen_ref[0]
    qm,dm=bwd_prep(q_ref,do_ref,hm)
    kpos=lax.broadcasted_iota(jnp.int32,(SP,1),0)
    low=jnp.where(kpos<klen,kpos,SP)
    def mask(kb):
        q0=kb*KB
        return q0+lax.broadcasted_iota(jnp.int32,(KB,SP-q0),1)>=low[q0:q0+KB]
    bwd_tiles(k_ref,v_ref,qm,dm,lambda h:l_ref[0,h:h+1],lambda h:dl_ref[0,h:h+1],dk_ref,dv_ref,dqt,lambda kb:kb*KB,mask)
    dq_ref[...]=(dqt[...].T*0.125+dqx_ref[...]).astype(bf16)
S=jax.ShapeDtypeStruct
def col(base,rows=SP): return pl.BlockSpec((rows,128),lambda j,*_:(0,base+j))
def row(base): return pl.BlockSpec((1,8,SP),lambda j,*_:(base+j,0,0))
ROW=row(0)
def call(fn,place,klen,ins,in_specs,outs,out_specs,scratch=(),pairs=NP,into=None,after=(),held=(),flops=0,trans=0):
    into=into or {}
    extra=list(into.items())
    n=2+len(ins)
    m=len(extra)
    skip=n+m+len(held)+len(after)
    here=len(outs)
    def kern(*refs): return fn(*refs[:n],*refs[skip:skip+here],*refs[skip+here+len(held):])
    specs=list(in_specs)+[pl.BlockSpec(memory_space=pl.ANY)]*(m+len(held)+len(after))
    return pl.pallas_call(kern,
        grid_spec=pltpu.PrefetchScalarGridSpec(num_scalar_prefetch=2,grid=(pairs,),in_specs=specs,out_specs=list(out_specs)+[pl.BlockSpec(memory_space=pl.ANY)]*len(held),scratch_shapes=list(scratch)),
        out_shape=list(outs)+[S(x.shape,x.dtype) for x in held],
        input_output_aliases={n+i:o for i,(o,_) in enumerate(extra)}|{n+m+i:here+i for i in range(len(held))},
        compiler_params=pltpu.CompilerParams(vmem_limit_bytes=50*1024*1024,dimension_semantics=("arbitrary",)),
        cost_estimate=pl.CostEstimate(flops=flops,bytes_accessed=pairs*10**4,transcendentals=trans),
        name=fn.__name__,
    )(place,klen,*ins,*[x for _,x in extra],*held,*after)


BITS = {"c": ("dp", 1), "y": ("dp", 2), "u": ("dp", 4), "v": ("dp", 8), "x": ("blk", 1)}
LOW = "xyuv"
ORDERS = ("xyuv", "yuxv", "uxyv")
RB = 48


def swap(a, bit):
    axis, step = BITS[bit] if isinstance(bit, str) else ("dp", bit)
    return lax.ppermute(a, axis, [(i, i ^ step) for i in range(lax.axis_size(axis))])


def outer_steps():
    size = lax.axis_size("dp")
    return [1 << k for k in range(4, 16) if (1 << k) < size]


def my_id():
    place = 0
    for bit in "c" + LOW:
        axis, step = BITS[bit]
        place = 2 * place + (lax.axis_index(axis) // step) % 2
    return place.astype(jnp.int32).reshape(1)


def add(a, b):
    return (a.astype(f32) + b.astype(f32)).astype(bf16)


def core_step(keeps, sends):
    state = []
    for keep, send in zip(keeps, sends):
        a = add(keep, swap(send, "c"))
        state.append((a.reshape((2,) * 4 + a.shape[1:]), LOW))
    return state


def low_step(state, step):
    waiting = []
    for (a, bits), order in zip(state, ORDERS):
        at = bits.index(order[step])
        keep, send = lax.index_in_dim(a, 0, at, False), lax.index_in_dim(a, 1, at, False)
        waiting.append((keep, swap(send, order[step]), bits.replace(order[step], "")))
    return [(add(keep, got), bits) for keep, got, bits in waiting]


def outer_sum(blocks):
    for step in outer_steps():
        blocks = [add(a, swap(a, step)) for a in blocks]
    return blocks


def reduce_parts(keeps, sends):
    state = core_step(keeps, sends)
    for step in range(4):
        state = low_step(state, step)
    return outer_sum([a for a, _ in state])


def spread_parts(blocks):
    state = [a[None] for a in blocks]
    for step in (3, 2, 1, 0):
        state = [jnp.concatenate([a, swap(a, o[step])], 0) for a, o in zip(state, ORDERS)]
    return state, [swap(a, "c") for a in state]


def sum_small(a):
    for bit in "c" + LOW:
        a = a + swap(a, bit)
    for step in outer_steps():
        a = a + swap(a, step)
    return a


def low_index(p, order):
    r = 0
    for bit in order:
        r = 2 * r + (p // (1 << (3 - LOW.index(bit)))) % 2
    return r


def pack(me, arrays, blocks, layout, widths, name):
    n = len(widths)

    def kern(me_ref, *refs):
        ins, keeps, sends = refs[: len(arrays)], refs[len(arrays) :][:n], refs[len(arrays) + n :]
        step = pl.program_id(0)

        def fill(outs):
            for part, pieces in enumerate(layout):
                at = 0
                for which, row, lane, lanes in pieces:
                    outs[part][0, :, at : at + lanes] = ins[which][row : row + RB, lane : lane + lanes]
                    at += lanes

        @pl.when(step < 16)
        def _():
            fill(keeps)

        @pl.when(step >= 16)
        def _():
            fill(sends)

    def source(p, me_ref, wide):
        block = p ^ me_ref[0]
        return (block % 16, block // 16) if wide else (block, 0)

    in_specs = [
        pl.BlockSpec(shape, lambda p, me_ref, wide=wide: source(p, me_ref, wide)) for shape, wide in blocks
    ]
    outs = [pl.BlockSpec((1, RB, w), lambda p, me_ref: (jnp.minimum(p, 15), 0, 0)) for w in widths]
    outs += [pl.BlockSpec((1, RB, w), lambda p, me_ref: (jnp.maximum(p - 16, 0), 0, 0)) for w in widths]
    res = pl.pallas_call(
        kern,
        grid_spec=pltpu.PrefetchScalarGridSpec(
            num_scalar_prefetch=1, grid=(32,), in_specs=in_specs, out_specs=outs
        ),
        out_shape=[S((16, RB, w), bf16) for w in widths + widths],
        compiler_params=pltpu.CompilerParams(vmem_limit_bytes=32 * 1024 * 1024),
        cost_estimate=pl.CostEstimate(flops=0, bytes_accessed=2 * 32 * RB * sum(widths) * 2, transcendentals=0),
        name=name,
    )(me, *arrays)
    return res[:n], res[n:]


def unpack(me, mine, other, shapes, blocks, layout, widths, name):
    n = len(widths)

    def kern(me_ref, *refs):
        own, far, outs = refs[:n], refs[n : 2 * n], refs[2 * n :]
        core = me_ref[0] // 16
        half = pl.program_id(0) // 16

        def fill(ins):
            for part, pieces in enumerate(layout):
                at = 0
                for which, row, lane, lanes in pieces:
                    outs[which][row : row + RB, lane : lane + lanes] = ins[part][0, :, at : at + lanes].astype(f32)
                    at += lanes

        @pl.when(half == core)
        def _():
            fill(own)

        @pl.when(half != core)
        def _():
            fill(far)

    def pick(block, me_ref, order, near):
        me = me_ref[0]
        first = me // 16 if near else 1 - me // 16
        hold = jnp.where(first == 0, 15, 0)
        low = jnp.where(block // 16 == first, block % 16, hold) ^ (me % 16)
        return (low_index(low, order), 0, 0)

    specs = []
    for near in (True, False):
        specs += [
            pl.BlockSpec((1, RB, w), lambda b, me_ref, o=o, near=near: pick(b, me_ref, o, near))
            for w, o in zip(widths, ORDERS)
        ]
    outs = [
        pl.BlockSpec(shape, (lambda b, me_ref: (b % 16, b // 16)) if wide else (lambda b, me_ref: (b, 0)))
        for shape, wide in blocks
    ]
    return pl.pallas_call(
        kern,
        grid_spec=pltpu.PrefetchScalarGridSpec(
            num_scalar_prefetch=1, grid=(32,), in_specs=specs, out_specs=outs
        ),
        out_shape=[S(shape, f32) for shape in shapes],
        compiler_params=pltpu.CompilerParams(vmem_limit_bytes=32 * 1024 * 1024),
        cost_estimate=pl.CostEstimate(flops=0, bytes_accessed=6 * 32 * RB * sum(widths), transcendentals=0),
        name=name,
    )(me, *mine, *other)


def gather_all(blocks):
    a = lax.all_gather(jnp.stack(blocks), ("dp", "blk"), axis=0, tiled=False)
    return a[:32]


def unpack_gathered(gathered, shapes, blocks, layout, name):
    def kern(ins, *outs):
        for part, pieces in enumerate(layout):
            at = 0
            for which, row, lane, lanes in pieces:
                outs[which][row : row + RB, lane : lane + lanes] = ins[0, part, :, at : at + lanes].astype(f32)
                at += lanes

    def device(block):
        bits = [(block // (1 << (4 - i))) % 2 for i in range(5)]
        c, x, y, u, v = bits
        return (v * 8 + u * 4 + y * 2 + c) * 2 + x

    outs = [
        pl.BlockSpec(shape, (lambda b: (b % 16, b // 16)) if wide else (lambda b: (b, 0)))
        for shape, wide in blocks
    ]
    return pl.pallas_call(
        kern,
        grid=(32,),
        in_specs=[pl.BlockSpec((1,) + gathered.shape[1:], lambda b: (device(b), 0, 0, 0))],
        out_specs=outs,
        out_shape=[S(shape, f32) for shape in shapes],
        compiler_params=pltpu.CompilerParams(vmem_limit_bytes=32 * 1024 * 1024),
        cost_estimate=pl.CostEstimate(flops=0, bytes_accessed=3 * gathered.size * 2, transcendentals=0),
        name=name,
    )(gathered)


EARLY_BLOCKS = [((48, 1536), True), ((96, 768), False), ((48, 384), True)]
EARLY_LAYOUT = [
    [(0, 0, 0, 1152)],
    [(0, 0, 1152, 384), (1, 0, 0, 768)],
    [(1, 48, 0, 768), (2, 0, 0, 384)],
]
EARLY_SHAPES = [(W, 4 * W), (4 * W, W), (W, W)]
LATE_BLOCKS = [((48, 1152), True)]
LATE_LAYOUT = [[(0, 0, 0, 384)], [(0, 0, 384, 384)], [(0, 0, 768, 384)]]
LATE_SHAPES = [(W, 3 * W)]


def swap_spans(x):
    return lax.ppermute(x, "blk", [(0, 1), (1, 0)])


def normalize(values, gain, shift):
    centered = values - jnp.mean(values, -1, keepdims=True)
    inv_std = lax.rsqrt(jnp.mean(centered * centered, -1, keepdims=True) + EPS)
    x_hat = centered * inv_std
    return x_hat * gain + shift, x_hat, inv_std


def norm_back(upstream, x_hat, inv_std, gain):
    scaled = upstream * gain
    inner = (
        scaled
        - jnp.mean(scaled, -1, keepdims=True)
        - x_hat * jnp.mean(scaled * x_hat, -1, keepdims=True)
    )
    return inv_std * inner, jnp.sum(upstream * x_hat, 0), jnp.sum(upstream, 0)


def rows_dot(left, right):
    return lax.dot_general(left, right, (((0,), (0,)), ((), ())), preferred_element_type=f32)


def body(
    inputs, cotangent, lengths, groups, flip,
    w_qkv, b_query, b_value, w_out, b_out, gain_one, shift_one, gain_two, shift_two,
    w_fc, b_fc, w_proj, b_proj,
):
    place = jnp.bitwise_xor(lax.axis_index("blk"), flip[0])
    klen = jnp.minimum(lengths[0] - place * SP, SP)
    place_s = place.reshape(1).astype(jnp.int32)
    klen_s = klen.reshape(1).astype(jnp.int32)
    x_b = inputs[0, 0]
    up_b = cotangent[0, 0]
    xr_b = swap_spans(x_b)

    x_in = x_b.astype(f32)
    normed_f, x_hat_one, inv_one = normalize(x_in, gain_one, shift_one)
    normed = normed_f.astype(bf16)
    qkv_bias = jnp.concatenate([b_query, jnp.zeros_like(b_value), b_value])
    qkv = (dot(normed, w_qkv) + qkv_bias).astype(bf16)
    c = col(0)
    tall = pl.BlockSpec((1, 128, SP), lambda j, *_: (j, 0, 0))
    od, ld = call(
        diag_fwd, place_s, klen_s, (qkv, qkv, qkv), [c, col(6), col(12)],
        [S((NP, 128, SP), f32), S((NP, 8, SP), f32)], [tall, ROW],
    )
    d_act = tdot(up_b, w_proj).astype(bf16)

    normed_rf, x_hat_r, _ = normalize(xr_b.astype(f32), gain_one, shift_one)
    normed_r = normed_rf.astype(bf16)
    kvr = (dot(normed_r, w_qkv[:, W:]) + qkv_bias[W:]).astype(bf16)
    attended, lse = call(
        cross_fwd, place_s, klen_s, (qkv, kvr, kvr, od, ld), [c, c, col(6), tall, ROW],
        [S((SP, W), bf16), S((NP, 8, SP), f32)], [c, ROW],
    )

    branch_att = dot(attended, w_out) + b_out
    middle = x_in + branch_att
    normed_two_f, x_hat_two, inv_two = normalize(middle, gain_two, shift_two)
    normed_two = normed_two_f.astype(bf16)
    pre_act = dot(normed_two, w_fc) + b_fc
    gelu_val, gelu_back = jax.vjp(lambda val: jax.nn.gelu(val, approximate=True), pre_act)
    activ = gelu_val.astype(bf16)
    branch_mlp = dot(activ, w_proj) + b_proj
    outputs = middle + branch_mlp
    upstream = up_b.astype(f32)
    grad_pre = gelu_back(d_act.astype(f32))[0].astype(bf16)
    grad_w_proj = rows_dot(activ, up_b).astype(bf16)
    grad_w_fc = rows_dot(normed_two, grad_pre).astype(bf16)
    grad_mid_norm, grad_gain_two, grad_shift_two = norm_back(
        tdot(grad_pre, w_fc), x_hat_two, inv_two, gain_two
    )
    grad_middle = upstream + grad_mid_norm
    grad_att = grad_middle.astype(bf16)
    grad_w_out = rows_dot(attended, grad_att).astype(bf16)
    grad_attended = tdot(grad_att, w_out).astype(bf16)
    me = my_id()
    keeps, sends = pack(
        me, [grad_w_fc, grad_w_proj, grad_w_out], EARLY_BLOCKS, EARLY_LAYOUT, [1152] * 3, "pack_early"
    )
    acc = pltpu.VMEM((128, SP), f32)
    flops = 16 * 10**9
    crossed = []
    dkr = dvr = None
    w_q, w_k, w_v = w_qkv[:, :W], w_qkv[:, W : 2 * W], w_qkv[:, 2 * W :]

    def cross_piece(g, dep):
        nonlocal dkr, dvr
        at = 2 * g
        dqx, dkr, dvr, delta = call(
            cross_bwd, place_s, klen_s, (qkv, kvr, kvr, grad_attended, attended, lse),
            [col(at), col(at), col(6 + at), col(at), col(at), row(at)],
            [S((SP, 256), f32), S((SP, W), bf16), S((SP, W), bf16), S((2, 8, SP), f32)],
            [col(0), col(at), col(at), row(0)], [acc], pairs=2,
            into={1: dkr, 2: dvr} if g else None, after=dep, flops=flops,
        )
        crossed.append((dqx, delta))

    dq = dk = dv = None

    def diag_piece(g, dep):
        nonlocal dq, dk, dv, dkr, dvr
        at = 2 * g
        dqx, delta = crossed[g]
        dq, dk, dv, *held = call(
            diag_bwd, place_s, klen_s, (qkv, qkv, qkv, grad_attended, lse, delta, dqx),
            [col(at), col(6 + at), col(12 + at), col(at), row(at), row(0), col(0)],
            [S((SP, W), bf16)] * 3, [col(at)] * 3, [acc], pairs=2,
            into={0: dq, 1: dk, 2: dv} if g else None, after=dep, flops=flops // 2,
            held=(),
        )
        if held:
            dkr, dvr = held

    arrays = lambda state: [a for a, _ in state]
    cross_piece(0, keeps)
    state = core_step(keeps, sends)
    cross_piece(1, arrays(state))
    cross_piece(2, ())
    state = low_step(state, 0)
    diag_piece(0, arrays(state))
    state = low_step(state, 1)
    part_r = tdot(dkr, w_k) + tdot(dvr, w_v)
    part_rb = part_r.astype(bf16)
    returned = swap_spans(part_rb)
    diag_piece(1, arrays(state) + [part_rb])
    state = low_step(state, 2)
    diag_piece(2, arrays(state))
    state = low_step(state, 3)
    early = outer_sum(arrays(state))
    early = unpack_gathered(gather_all(early), EARLY_SHAPES, EARLY_BLOCKS, EARLY_LAYOUT, "unpack_early")
    grad_w_q = rows_dot(normed, dq).astype(bf16)
    grad_w_k = (rows_dot(normed, dk) + rows_dot(normed_r, dkr)).astype(bf16)
    grad_w_v = (rows_dot(normed, dv) + rows_dot(normed_r, dvr)).astype(bf16)
    grad_w_qkv = jnp.concatenate([grad_w_q, grad_w_k, grad_w_v], 1)
    late = reduce_parts(*pack(me, [grad_w_qkv], LATE_BLOCKS, LATE_LAYOUT, [384] * 3, "pack_late"))
    late = unpack(
        me, *spread_parts(late), LATE_SHAPES, LATE_BLOCKS, LATE_LAYOUT, [384] * 3, "unpack_late"
    )
    grad_b_query = jnp.sum(dq.astype(f32), 0)
    grad_b_value = jnp.sum(dv.astype(f32), 0) + jnp.sum(dvr.astype(f32), 0)

    part_own = tdot(dq, w_q) + tdot(dk, w_k) + tdot(dv, w_v)
    grad_shift_one = jnp.sum(part_own, 0) + jnp.sum(part_r, 0)
    grad_gain_one = jnp.sum(part_own * x_hat_one, 0) + jnp.sum(part_r * x_hat_r, 0)
    grad_x_norm = norm_back(part_own + returned.astype(f32), x_hat_one, inv_one, gain_one)[0]
    input_grad = (grad_middle + grad_x_norm).astype(bf16)

    valid = (jnp.arange(SP, dtype=jnp.int32) < klen).astype(f32)
    member = (groups[0] == jnp.arange(2, dtype=jnp.int32)).astype(f32)
    sums = jnp.stack(
        [jnp.sum(valid * jnp.sum(v * v, -1)) for v in (outputs, branch_att, branch_mlp)]
        + [jnp.sum(valid)]
    )
    small = jnp.concatenate([
        grad_b_query, grad_b_value, jnp.sum(grad_att.astype(f32), 0),
        grad_gain_one, grad_shift_one, grad_gain_two, grad_shift_two,
        jnp.sum(grad_pre.astype(f32), 0), jnp.sum(upstream, 0),
        (member[:, None] * sums[None, :]).reshape(-1), jnp.zeros((1016,), f32),
    ])
    small = sum_small(small.reshape(80, 128)).reshape(-1)
    sizes = [W] * 7 + [4 * W, W]
    pieces = []
    at = 0
    for size in sizes:
        pieces.append(small[at : at + size])
        at += size
    table = small[at : at + 8].reshape(2, 4)
    group_rms = jnp.sqrt(table[:, :3] / (table[:, 3:] * W))
    g_bq, g_bv, g_bo, g_g1, g_s1, g_g2, g_s2, g_bfc, g_bp = pieces
    return (
        outputs.astype(bf16)[None, None], input_grad[None, None],
        late[0], g_bq, g_bv, early[2], g_bo, g_g1, g_s1, g_g2, g_s2, early[0], g_bfc, early[1], g_bp, group_rms,
    )


def solution(mesh):
    span = P("dp", "blk", None, None)
    return jax.shard_map(
        body,
        mesh=mesh,
        in_specs=(span, span, P("dp"), P("dp"), P("dp")) + (P(),) * 13,
        out_specs=(span, span) + (P(),) * 14,
        check_vma=False,
    )
```

```python
import jax
import jax.numpy as jnp
from jax import lax
from jax.experimental import pallas as pl
from jax.experimental.pallas import tpu as pltpu
from jax.sharding import PartitionSpec as P

SP = 1024
W = 768
NP = 6
EPS = 1e-05
NEG=-1e30
f32=jnp.float32; bf16=jnp.bfloat16
def tdot(a,b): return lax.dot_general(a,b,(((1,),(1,)),((),())),preferred_element_type=f32)
def dot(a,b): return jnp.dot(a,b,preferred_element_type=f32)
def head_masks():
    lane=lax.broadcasted_iota(jnp.int32,(1,128),1)
    return [lane<64, lane>=64]
def softmax_t(s):
    m=jnp.max(s,0,keepdims=True)
    p=jnp.exp(s-m)
    l=jnp.sum(p,0,keepdims=True)
    return m,l,p.astype(bf16)
DQ=256
def diag_fwd(place_ref, klen_ref, q_ref,k_ref,v_ref,o_ref,l_ref):
    hm=head_masks(); klen=klen_ref[0]
    q=q_ref[...]*jnp.asarray(0.125,bf16)
    vt=v_ref[...].T
    z=jnp.zeros((),bf16)
    tiles=[(qi,h) for qi in range(SP//DQ) for h in range(2)]
    kpos=lax.broadcasted_iota(jnp.int32,(SP,1),0)
    low=jnp.where(kpos<klen,kpos,SP)
    def scores(t):
        qi,h=t; n=(qi+1)*DQ
        ok=(qi*DQ+lax.broadcasted_iota(jnp.int32,(n,DQ),1))>=low[:n]
        return jnp.where(ok,tdot(k_ref[:n],jnp.where(hm[h],q[qi*DQ:n],z)),NEG)
    def finish(t,m,l,p):
        qi,h=t; n=(qi+1)*DQ; sl=slice(qi*DQ,n)
        acc=dot(vt[h*64:(h+1)*64,:n],p)
        o_ref[0,h*64:(h+1)*64,sl]=acc*(1.0/l)
        l_ref[0,h:h+1,sl]=m+jnp.log(l)
    pipeline(tiles,scores,softmax_t,finish)
def pipeline(tiles,scores,mid,finish,depth=2):
    s=scores(tiles[0]); pend=None
    for i,t in enumerate(tiles):
        sn=scores(tiles[i+1]) if i+1<len(tiles) else None
        r=mid(s) if not isinstance(s,tuple) else mid(t,*s)
        if depth==2:
            if pend: finish(*pend)
            pend=(t,)+r
        else: finish(t,*r)
        s=sn
    if pend: finish(*pend)
CQ=512
def cross_fwd(place_ref, klen_ref, q_ref,k_ref,v_ref,od_ref,ld_ref,o_ref,l_ref):
    hm=head_masks()
    @pl.when(place_ref[0]==1)
    def _():
        q=q_ref[...]*jnp.asarray(0.125,bf16)
        vt=v_ref[...].T
        z=jnp.zeros((),bf16)
        tiles=[(qi,h) for qi in range(SP//CQ) for h in range(2)]
        res={}
        def scores(t):
            qi,h=t
            return tdot(k_ref[...],jnp.where(hm[h],q[qi*CQ:(qi+1)*CQ],z))
        def finish(t,m,l,p):
            qi,h=t; sl=slice(qi*CQ,(qi+1)*CQ)
            acc=dot(vt[h*64:(h+1)*64],p)
            ld=ld_ref[0,h:h+1,sl]
            lx=m+jnp.log(l)
            mx=jnp.maximum(ld,lx)
            ed=jnp.exp(ld-mx); ex=jnp.exp(lx-mx); tot=ed+ex
            l_ref[0,h:h+1,sl]=mx+jnp.log(tot)
            res[t]=od_ref[0,h*64:(h+1)*64,sl]*(ed/tot)+acc*(ex/(tot*l))
            if h==1: o_ref[sl]=jnp.concatenate([res[(qi,0)],res[(qi,1)]],0).T.astype(bf16)
        pipeline(tiles,scores,softmax_t,finish)
    @pl.when(place_ref[0]==0)
    def _():
        o_ref[...]=od_ref[0].T.astype(bf16)
        l_ref[...]=ld_ref[...]
KB=256
def bwd_prep(q_ref,do_ref,hm):
    q=q_ref[...]*jnp.asarray(0.125,bf16)
    z=jnp.zeros((),bf16)
    do=do_ref[...]
    return [jnp.where(hm[h],q,z) for h in range(2)],[jnp.where(hm[h],do,z) for h in range(2)]
def bwd_tiles(k_ref,v_ref,qm,dm,lrow,drow,put,dqt,start,mask):
    tiles=[(kb,h) for kb in range(SP//KB) for h in range(2)]
    acc={}
    kts={}
    def scores(t):
        kb,h=t; ks=slice(kb*KB,(kb+1)*KB); q0=start(kb)
        return tdot(k_ref[ks],qm[h][q0:]),tdot(v_ref[ks],dm[h][q0:])
    def mid(t,s,dp):
        kb,h=t; q0=start(kb)
        p=jnp.exp(s-lrow(h)[:,q0:])
        if mask is not None: p=jnp.where(mask(kb),p,0.0)
        ds=p*(dp-drow(h)[:,q0:])
        return p.astype(bf16),ds.astype(bf16)
    def finish(t,p,ds):
        kb,h=t; ks=slice(kb*KB,(kb+1)*KB); q0=start(kb)
        if h==0: kts[kb]=k_ref[ks].T
        a=dot(p,dm[h][q0:]); b=dot(ds,qm[h][q0:])
        if h==0: acc[kb]=(a,b)
        else:
            put(ks,(acc[kb][1]+b).astype(bf16),(acc[kb][0]+a).astype(bf16))
        c=dot(kts[kb][h*64:(h+1)*64],ds)
        if kb==0: dqt[h*64:(h+1)*64]=c
        else: dqt[h*64:(h+1)*64,q0:]+=c
    pipeline(tiles,scores,mid,finish)
def cross_bwd(place_ref, klen_ref, q_ref,k_ref,v_ref,do_ref,o_ref,l_ref,dq_ref,dkv_ref,dl_ref,dqt):
    hm=head_masks()
    prod=do_ref[...].astype(f32)*o_ref[...].astype(f32)
    t=prod.T
    dl_ref[0,0:1]=jnp.sum(t[:64],0,keepdims=True); dl_ref[0,1:2]=jnp.sum(t[64:],0,keepdims=True)
    @pl.when(place_ref[0]==1)
    def _():
        def put(ks,dk,dv):
            dkv_ref[0,ks]=dk
            dkv_ref[1,ks]=dv
        qm,dm=bwd_prep(q_ref,do_ref,hm)
        bwd_tiles(k_ref,v_ref,qm,dm,lambda h:l_ref[0,h:h+1],lambda h:dl_ref[0,h:h+1],put,dqt,lambda kb:0,None)
        dq_ref[...]=dqt[...].T*0.125
    @pl.when(place_ref[0]==0)
    def _():
        dkv_ref[...]=jnp.zeros_like(dkv_ref); dq_ref[...]=jnp.zeros_like(dq_ref)
def diag_bwd(place_ref, klen_ref, q_ref,k_ref,v_ref,do_ref,l_ref,dl_ref,dqx_ref,out_ref,dqt):
    hm=head_masks(); klen=klen_ref[0]
    qm,dm=bwd_prep(q_ref,do_ref,hm)
    def put(ks,dk,dv):
        out_ref[1,ks]=dk
        out_ref[2,ks]=dv
    kpos=lax.broadcasted_iota(jnp.int32,(SP,1),0)
    low=jnp.where(kpos<klen,kpos,SP)
    def mask(kb):
        q0=kb*KB
        return q0+lax.broadcasted_iota(jnp.int32,(KB,SP-q0),1)>=low[q0:q0+KB]
    bwd_tiles(k_ref,v_ref,qm,dm,lambda h:l_ref[0,h:h+1],lambda h:dl_ref[0,h:h+1],put,dqt,lambda kb:kb*KB,mask)
    out_ref[0]=(dqt[...].T*0.125+dqx_ref[...]).astype(bf16)
S=jax.ShapeDtypeStruct
def col(base,rows=SP): return pl.BlockSpec((rows,128),lambda j,*_:(0,base+j))
def cols(n,base): return pl.BlockSpec((n,SP,128),lambda j,*_:(0,0,base+j))
def row(base): return pl.BlockSpec((1,8,SP),lambda j,*_:(base+j,0,0))
ROW=row(0)
def call(fn,place,klen,ins,in_specs,outs,out_specs,scratch=(),pairs=NP,into=None,after=(),flops=0,trans=0):
    into=into or {}
    extra=list(into.items())
    n=2+len(ins)
    m=len(extra)
    skip=n+m+len(after)
    def kern(*refs): return fn(*refs[:n],*refs[skip:])
    specs=list(in_specs)+[pl.BlockSpec(memory_space=pl.ANY)]*(m+len(after))
    return pl.pallas_call(kern,
        grid_spec=pltpu.PrefetchScalarGridSpec(num_scalar_prefetch=2,grid=(pairs,),in_specs=specs,out_specs=out_specs,scratch_shapes=list(scratch)),
        out_shape=outs,
        input_output_aliases={n+i:o for i,(o,_) in enumerate(extra)},
        compiler_params=pltpu.CompilerParams(vmem_limit_bytes=50*1024*1024,dimension_semantics=("arbitrary",)),
        cost_estimate=pl.CostEstimate(flops=flops,bytes_accessed=pairs*10**4,transcendentals=trans),
        name=fn.__name__,
    )(place,klen,*ins,*[x for _,x in extra],*after)


BITS = {"c": ("dp", 1), "y": ("dp", 2), "u": ("dp", 4), "v": ("dp", 8), "x": ("blk", 1)}
LOW = "xyuv"
ORDERS = ("xyuv", "yuxv", "uxyv")
RB = 48


def swap(a, bit):
    axis, step = BITS[bit] if isinstance(bit, str) else ("dp", bit)
    return lax.ppermute(a, axis, [(i, i ^ step) for i in range(lax.axis_size(axis))])


def outer_steps():
    size = lax.axis_size("dp")
    return [1 << k for k in range(4, 16) if (1 << k) < size]


def my_id():
    place = 0
    for bit in "c" + LOW:
        axis, step = BITS[bit]
        place = 2 * place + (lax.axis_index(axis) // step) % 2
    return place.astype(jnp.int32).reshape(1)


def add(a, b):
    return (a.astype(f32) + b.astype(f32)).astype(bf16)


def core_step(keeps, sends):
    state = []
    for keep, send in zip(keeps, sends):
        a = add(keep, swap(send, "c"))
        state.append((a.reshape((2,) * 4 + a.shape[1:]), LOW))
    return state


def low_step(state, step, after=None):
    waiting = []
    for (a, bits), order in zip(state, ORDERS):
        at = bits.index(order[step])
        keep, send = lax.index_in_dim(a, 0, at, False), lax.index_in_dim(a, 1, at, False)
        waiting.append((keep, swap(send, order[step]), bits.replace(order[step], "")))
    if after is not None:
        flat = lambda a: a.reshape(-1, a.shape[-1])
        sums = sum_kernel([(flat(keep), flat(got)) for keep, got, _ in waiting], after, "step_sum")
        return [(a.reshape(keep.shape), bits) for a, (keep, _, bits) in zip(sums, waiting)]
    return [(add(keep, got), bits) for keep, got, bits in waiting]


def sum_kernel(pairs, after, name):
    n = len(pairs)

    def kern(*refs):
        for i in range(n):
            refs[i - n][...] = add(refs[i][...], refs[n + i][...])

    vmem = pl.BlockSpec(memory_space=pltpu.VMEM)
    return pl.pallas_call(
        kern,
        in_specs=[vmem] * (2 * n) + [pl.BlockSpec(memory_space=pl.ANY)] * len(after),
        out_specs=[vmem] * n,
        out_shape=[S(a.shape, bf16) for a, _ in pairs],
        name=name,
    )(*[a for a, _ in pairs], *[b for _, b in pairs], *after)


def last_step(state, after):
    pairs = [(a[0], swap(a[1], order[3])) for (a, _), order in zip(state, ORDERS)]
    total = jnp.stack(sum_kernel(pairs, after, "last_sum"))
    for step in outer_steps():
        total = add(total, swap(total, step))
    return total


def outer_sum(blocks):
    for step in outer_steps():
        blocks = [add(a, swap(a, step)) for a in blocks]
    return blocks


def reduce_parts(keeps, sends):
    state = core_step(keeps, sends)
    for step in range(4):
        state = low_step(state, step)
    return outer_sum([a for a, _ in state])


def spread_parts(blocks):
    state = [a[None] for a in blocks]
    for step in (3, 2, 1, 0):
        state = [jnp.concatenate([a, swap(a, o[step])], 0) for a, o in zip(state, ORDERS)]
    return state, [swap(a, "c") for a in state]


def sum_small(a):
    for bit in "c" + LOW:
        a = a + swap(a, bit)
    for step in outer_steps():
        a = a + swap(a, step)
    return a


def low_index(p, order):
    r = 0
    for bit in order:
        r = 2 * r + (p // (1 << (3 - LOW.index(bit)))) % 2
    return r


def gather_all(blocks):
    a = lax.all_gather(blocks, ("dp", "blk"), axis=0, tiled=False)
    return a[:32]


def device_of(block):
    c, x, y, u, v = [(block // (1 << (4 - i))) % 2 for i in range(5)]
    return (v * 8 + u * 4 + y * 2 + c) * 2 + x


def unpack_early(gathered):
    rows = 2

    def kern(*refs):
        ins, (fc, proj, out) = refs[: 2 * rows], refs[2 * rows :]
        for core in range(2):
            for r in range(rows):
                a = ins[core * rows + r]
                at = slice(r * RB, (r + 1) * RB)
                fc[at, core * 1536 : core * 1536 + 1152] = a[0, 0].astype(f32)
                fc[at, core * 1536 + 1152 : (core + 1) * 1536] = a[0, 1, :, :384].astype(f32)
                proj[core, 2 * r * RB : (2 * r + 1) * RB] = a[0, 1, :, 384:].astype(f32)
                proj[core, (2 * r + 1) * RB : (2 * r + 2) * RB] = a[0, 2, :, :768].astype(f32)
                out[at, core * 384 : (core + 1) * 384] = a[0, 2, :, 768:].astype(f32)

    block = (1,) + gathered.shape[1:]
    return pl.pallas_call(
        kern,
        grid=(16 // rows,),
        in_specs=[
            pl.BlockSpec(block, lambda b, core=core, r=r: (device_of(core * 16 + b * rows + r), 0, 0, 0))
            for core in range(2) for r in range(rows)
        ],
        out_specs=[
            pl.BlockSpec((rows * RB, 4 * W), lambda b: (b, 0)),
            pl.BlockSpec((2, 2 * rows * RB, W), lambda b: (0, b, 0)),
            pl.BlockSpec((rows * RB, W), lambda b: (b, 0)),
        ],
        out_shape=[S((W, 4 * W), f32), S((2, 2 * W, W), f32), S((W, W), f32)],
        compiler_params=pltpu.CompilerParams(vmem_limit_bytes=56 * 1024 * 1024),
        cost_estimate=pl.CostEstimate(flops=0, bytes_accessed=3 * gathered.size * 2, transcendentals=0),
        name="unpack_early",
    )(*[gathered] * (2 * rows))


def unpack_late(me, mine, other):
    n = len(mine)
    rows = 4
    lanes = mine[0].shape[2]

    def kern(me_ref, *refs):
        own, far, out = refs[:n], refs[n : 2 * n], refs[-1]
        core, low = me_ref[0] // 16, me_ref[0] % 16
        step = pl.program_id(0)

        def fill(half, ins):
            for r in range(rows):
                place = (step * rows + r) ^ low
                for part in range(n):
                    at = (half * n + part) * lanes
                    out[r * RB : (r + 1) * RB, at : at + lanes] = ins[part][low_index(place, ORDERS[part])].astype(f32)

        for half in range(2):
            @pl.when(core == half)
            def _():
                fill(half, own)

            @pl.when(core != half)
            def _():
                fill(half, far)

    whole = pl.BlockSpec(mine[0].shape, lambda b, *_: (0, 0, 0))
    return pl.pallas_call(
        kern,
        grid_spec=pltpu.PrefetchScalarGridSpec(
            num_scalar_prefetch=1, grid=(16 // rows,), in_specs=[whole] * (2 * n),
            out_specs=pl.BlockSpec((rows * RB, 3 * W), lambda b, *_: (b, 0)),
        ),
        out_shape=S((W, 3 * W), f32),
        compiler_params=pltpu.CompilerParams(vmem_limit_bytes=56 * 1024 * 1024),
        cost_estimate=pl.CostEstimate(flops=0, bytes_accessed=10**7, transcendentals=0),
        name="unpack_late",
    )(me, *mine, *other)


MR = 256
FC = 768
C0 = 0.7978845608028654
C1 = C0 * 0.044715


def rowmean(a):
    return jnp.sum(a, -1, keepdims=True) * (1.0 / W)


def block_kernel(
    klen_ref, x_ref, att_ref, up_ref, w_out_ref, w_fc_ref, w_proj_ref, vec_ref, b_fc_ref,
    y_ref, act_ref, pre_ref, mid_ref, gatt_ref, do_ref, sums_ref, bsum_ref,
):
    step = pl.program_id(0)

    @pl.when(step == 0)
    def _():
        sums_ref[...] = jnp.zeros_like(sums_ref)
        bsum_ref[...] = jnp.zeros_like(bsum_ref)

    up_b = up_ref[...]
    up = up_b.astype(f32)
    branch_att = dot(att_ref[...], w_out_ref[...]) + vec_ref[0:1]
    middle = x_ref[...].astype(f32) + branch_att
    centered = middle - rowmean(middle)
    inv = lax.rsqrt(rowmean(centered * centered) + EPS)
    x_hat = centered * inv
    normed = (x_hat * vec_ref[1:2] + vec_ref[2:3]).astype(bf16)
    mid_ref[...] = normed
    chunks = range(4 * W // FC)
    sl = lambda c: slice(c * FC, (c + 1) * FC)

    def first(c):
        return dot(normed, w_fc_ref[:, sl(c)]), tdot(up_b, w_proj_ref[sl(c)])

    mlp = None
    back = None
    ahead = first(0)
    for c in chunks:
        u, dz = ahead
        if c + 1 < len(chunks):
            ahead = first(c + 1)
        u = u + b_fc_ref[0:1, sl(c)]
        v = u * u
        h = 0.5 + 0.5 * jnp.tanh(u * (C0 + C1 * v))
        z = (u * h).astype(bf16)
        d = dz * (h + (u * (2 * C0 + 6 * C1 * v)) * (h * (1.0 - h)))
        bsum_ref[0:1, sl(c)] += jnp.sum(d, 0, keepdims=True)
        d = d.astype(bf16)
        act_ref[:, sl(c)] = z
        pre_ref[:, sl(c)] = d
        a = dot(z, w_proj_ref[sl(c)])
        b = tdot(d, w_fc_ref[:, sl(c)])
        mlp = a if mlp is None else mlp + a
        back = b if back is None else back + b
    branch_mlp = mlp + vec_ref[3:4]
    out = middle + branch_mlp
    y_ref[...] = out.astype(bf16)
    scaled = back * vec_ref[1:2]
    grad = up + inv * (scaled - rowmean(scaled) - x_hat * rowmean(scaled * x_hat))
    gatt = grad.astype(bf16)
    gatt_ref[...] = gatt
    do_ref[...] = tdot(gatt, w_out_ref[...]).astype(bf16)
    valid = step * MR + lax.broadcasted_iota(jnp.int32, (MR, 1), 0) < klen_ref[0]
    total = lambda a: jnp.sum(a, 0, keepdims=True)
    kept = lambda a: total(jnp.where(valid, a * a, 0.0))
    sums_ref[...] += jnp.concatenate(
        [total(back * x_hat), total(back), total(grad), total(up), kept(out), kept(branch_att), kept(branch_mlp),
         jnp.zeros((1, W), f32)], 0,
    )


def block_call(klen, x, att, up, w_out, w_fc, w_proj, vec, b_fc):
    once = pl.Buffered(1)
    rows = lambda width: pl.BlockSpec((MR, width), lambda i, *_: (i, 0))
    whole = lambda shape: pl.BlockSpec(shape, lambda i, *_: (0, 0), pipeline_mode=once)
    const = lambda shape: pl.BlockSpec(shape, lambda i, *_: (0, 0))
    return pl.pallas_call(
        block_kernel,
        grid_spec=pltpu.PrefetchScalarGridSpec(
            num_scalar_prefetch=1,
            grid=(SP // MR,),
            in_specs=[rows(W)] * 3 + [whole((W, W)), whole((W, 4 * W)), whole((4 * W, W)), const((8, W)), const((1, 4 * W))],
            out_specs=[rows(W), rows(4 * W), rows(4 * W), rows(W), rows(W), rows(W), const((8, W)), const((1, 4 * W))],
        ),
        out_shape=[
            S((SP, W), bf16), S((SP, 4 * W), bf16), S((SP, 4 * W), bf16), S((SP, W), bf16),
            S((SP, W), bf16), S((SP, W), bf16), S((8, W), f32), S((1, 4 * W), f32),
        ],
        compiler_params=pltpu.CompilerParams(vmem_limit_bytes=56 * 1024 * 1024),
        cost_estimate=pl.CostEstimate(flops=22 * 10**9, bytes_accessed=35 * 10**6, transcendentals=3 * 10**6),
        name="block_mlp",
    )(klen, x, att, up, w_out, w_fc, w_proj, vec, b_fc)


def grads_kernel(me_ref, mid_ref, pre_ref, act_ref, up_ref, att_ref, gatt_ref, k0, k1, k2, s0, s1, s2, mid_t):
    step = pl.program_id(0)
    core, low = me_ref[0] // 16, me_ref[0] % 16

    @pl.when(step == 0)
    def _():
        mid_t[...] = mid_ref[...].T

    def by_core(half, fill, keep, send):
        @pl.when(half == core)
        def _():
            fill(*keep)

        @pl.when(half != core)
        def _():
            fill(*send)

    @pl.when(step < 4)
    def _():
        tile = dot(mid_t[...], pre_ref[...]).astype(bf16)

        def left(one):
            for i in range(16):
                one[i ^ low, :, :768] = tile[i * RB : (i + 1) * RB]

        def right(one, two):
            for i in range(16):
                one[i ^ low, :, 768:] = tile[i * RB : (i + 1) * RB, :384]
                two[i ^ low, :, :384] = tile[i * RB : (i + 1) * RB, 384:]

        @pl.when(step % 2 == 0)
        def _():
            by_core(step // 2, left, (k0,), (s0,))

        @pl.when(step % 2 == 1)
        def _():
            by_core(step // 2, right, (k0, k1), (s0, s1))

    @pl.when((step >= 4) & (step < 8))
    def _():
        tile = rows_dot(act_ref[...], up_ref[...]).astype(bf16)
        first = (step - 4) % 2 * 8

        def fill(one, two):
            for i in range(8):
                at = (first + i) ^ low
                one[at, :, 384:] = tile[2 * i * RB : (2 * i + 1) * RB]
                two[at, :, :768] = tile[(2 * i + 1) * RB : (2 * i + 2) * RB]

        by_core((step - 4) // 2, fill, (k1, k2), (s1, s2))

    @pl.when(step == 8)
    def _():
        tile = rows_dot(att_ref[...], gatt_ref[...]).astype(bf16)

        def fill(one, two):
            for i in range(16):
                one[i ^ low, :, 768:] = tile[i * RB : (i + 1) * RB, :384]
                two[i ^ low, :, 768:] = tile[i * RB : (i + 1) * RB, 384:]

        by_core(0, fill, (k2, s2), (s2, k2))


def grads_call(me, mid, pre, act, up, att, gatt):
    clip = lambda i, lo, hi: jnp.clip(i, lo, hi) - lo
    whole = pl.BlockSpec((SP, W), lambda i, *_: (0, 0))
    part = pl.BlockSpec((16, RB, 1152), lambda i, *_: (0, 0, 0))
    res = pl.pallas_call(
        grads_kernel,
        grid_spec=pltpu.PrefetchScalarGridSpec(
            num_scalar_prefetch=1,
            grid=(9,),
            in_specs=[
                whole,
                pl.BlockSpec((SP, W), lambda i, *_: (0, clip(i, 0, 3))),
                pl.BlockSpec((SP, W), lambda i, *_: (0, clip(i, 4, 7))),
                whole,
                whole,
                whole,
            ],
            out_specs=[part] * 6,
            scratch_shapes=[pltpu.VMEM((W, SP), bf16)],
        ),
        out_shape=[S((16, RB, 1152), bf16)] * 6,
        compiler_params=pltpu.CompilerParams(vmem_limit_bytes=56 * 1024 * 1024),
        cost_estimate=pl.CostEstimate(flops=11 * 10**9, bytes_accessed=30 * 10**6, transcendentals=0),
        name="block_grads",
    )(me, mid, pre, act, up, att, gatt)
    return res[:3], res[3:]


def late_kernel(me_ref, a_ref, ar_ref, d_ref, dr_ref, k0, k1, k2, s0, s1, s2, a_t, ar_t):
    step = pl.program_id(0)
    core, low = me_ref[0] // 16, me_ref[0] % 16

    def put(keep, send, tile):
        def fill(ref):
            for i in range(16):
                ref[i ^ low] = tile[i * RB : (i + 1) * RB]

        return lambda half: (
            pl.when(core == half)(lambda: fill(keep)),
            pl.when(core != half)(lambda: fill(send)),
        )

    @pl.when(step == 0)
    def _():
        a_t[...] = a_ref[...].T
        ar_t[...] = ar_ref[...].T
        tile = dot(a_t[...], d_ref[0]).astype(bf16)
        put(k0, s0, tile[:, :384])(0)
        put(k1, s1, tile[:, 384:])(0)

    @pl.when(step == 1)
    def _():
        tile = (dot(a_t[...], d_ref[0]) + dot(ar_t[...], dr_ref[0])).astype(bf16)
        put(k2, s2, tile[:, :384])(0)
        put(k0, s0, tile[:, 384:])(1)

    @pl.when(step == 2)
    def _():
        tile = (dot(a_t[...], d_ref[0]) + dot(ar_t[...], dr_ref[0])).astype(bf16)
        put(k1, s1, tile[:, :384])(1)
        put(k2, s2, tile[:, 384:])(1)


def late_call(me, a, ar, d, dr, after):
    def kern(*refs):
        return late_kernel(*refs[:5], *refs[5 + len(after) :])

    whole = pl.BlockSpec((SP, W), lambda i, *_: (0, 0))
    part = pl.BlockSpec((16, RB, 384), lambda i, *_: (0, 0, 0))
    res = pl.pallas_call(
        kern,
        grid_spec=pltpu.PrefetchScalarGridSpec(
            num_scalar_prefetch=1,
            grid=(3,),
            in_specs=[
                whole,
                whole,
                pl.BlockSpec((1, SP, W), lambda i, *_: (i, 0, 0)),
                pl.BlockSpec((1, SP, W), lambda i, *_: (jnp.maximum(i - 1, 0), 0, 0)),
            ] + [pl.BlockSpec(memory_space=pl.ANY)] * len(after),
            out_specs=[part] * 6,
            scratch_shapes=[pltpu.VMEM((W, SP), bf16)] * 2,
        ),
        out_shape=[S((16, RB, 384), bf16)] * 6,
        compiler_params=pltpu.CompilerParams(vmem_limit_bytes=56 * 1024 * 1024),
        cost_estimate=pl.CostEstimate(flops=6 * 10**9, bytes_accessed=14 * 10**6, transcendentals=0),
        name="late_grads",
    )(me, a, ar, d, dr, *after)
    return res[:3], res[3:]


def qkv_call(x, w_qkv, bias, vec, n, after, name):
    def kern(x_ref, w_ref, bias_ref, vec_ref, *refs):
        a_ref, out_ref = refs[len(after) :]
        a = (norm_one(x_ref)[0] * vec_ref[0:1] + vec_ref[1:2]).astype(bf16)
        a_ref[...] = a
        out_ref[...] = (dot(a, w_ref[:, (3 - n) * W :]) + bias_ref[0:1, (3 - n) * W :]).astype(bf16)

    rows = lambda width: pl.BlockSpec((MR, width), lambda i: (i, 0))
    return pl.pallas_call(
        kern,
        grid=(SP // MR,),
        in_specs=[
            rows(W),
            pl.BlockSpec((W, 3 * W), lambda i: (0, 0)),
            pl.BlockSpec((1, 3 * W), lambda i: (0, 0)),
            pl.BlockSpec((2, W), lambda i: (0, 0)),
        ] + [pl.BlockSpec(memory_space=pl.ANY)] * len(after),
        out_specs=[rows(W), rows(n * W)],
        out_shape=[S((SP, W), bf16), S((SP, n * W), bf16)],
        compiler_params=pltpu.CompilerParams(vmem_limit_bytes=56 * 1024 * 1024),
        cost_estimate=pl.CostEstimate(flops=n * 12 * 10**8, bytes_accessed=10**7, transcendentals=0),
        name=name,
    )(x, w_qkv, bias, vec, *after)


def norm_one(x_ref):
    x = x_ref[...].astype(f32)
    centered = x - rowmean(x)
    inv = lax.rsqrt(rowmean(centered * centered) + EPS)
    return centered * inv, inv


def input_kernel(x_ref, d_ref, w_ref, gain_ref, *refs):
    n = d_ref.shape[0]
    sums_ref = refs[-1]

    @pl.when(pl.program_id(0) == 0)
    def _():
        sums_ref[...] = jnp.zeros_like(sums_ref)

    x_hat, inv = norm_one(x_ref)
    part = None
    for i in range(n):
        a = tdot(d_ref[i], w_ref[:, (3 - n + i) * W : (4 - n + i) * W])
        part = a if part is None else part + a
    total = lambda a: jnp.sum(a.astype(f32), 0, keepdims=True)
    first = total(d_ref[0]) if n == 3 else jnp.zeros((1, W), f32)
    sums_ref[...] += jnp.concatenate(
        [first, total(d_ref[n - 1]), total(part * x_hat), total(part), jnp.zeros((4, W), f32)], 0
    )
    if n == 2:
        refs[0][...] = part.astype(bf16)
    else:
        returned_ref, gatt_ref = refs[:2]
        scaled = (part + returned_ref[0].astype(f32)) * gain_ref[0:1]
        inner = scaled - rowmean(scaled) - x_hat * rowmean(scaled * x_hat)
        refs[-2][...] = (gatt_ref[...].astype(f32) + inv * inner).astype(bf16)


def input_call(side, x, d, w_qkv, gain, extra, after, name):
    n = d.shape[0]
    rows = pl.BlockSpec((MR, W), lambda i, *_: (i, 0))
    more = [pl.BlockSpec((1, MR, W), lambda i, side_ref: (side_ref[0], i, 0)), rows] if extra else []
    skip = 5 + len(extra)

    def kern(*refs):
        return input_kernel(*refs[1:skip], *refs[skip + len(after) :])

    return pl.pallas_call(
        kern,
        grid_spec=pltpu.PrefetchScalarGridSpec(
            num_scalar_prefetch=1,
            grid=(SP // MR,),
            in_specs=[
                rows,
                pl.BlockSpec((n, MR, W), lambda i, *_: (0, i, 0)),
                pl.BlockSpec((W, 3 * W), lambda i, *_: (0, 0)),
                pl.BlockSpec((1, W), lambda i, *_: (0, 0)),
            ] + more + [pl.BlockSpec(memory_space=pl.ANY)] * len(after),
            out_specs=[rows, pl.BlockSpec((8, W), lambda i, *_: (0, 0))],
        ),
        out_shape=[S((SP, W), bf16), S((8, W), f32)],
        compiler_params=pltpu.CompilerParams(vmem_limit_bytes=56 * 1024 * 1024),
        cost_estimate=pl.CostEstimate(flops=n * 12 * 10**8, bytes_accessed=10**7, transcendentals=0),
        name=name,
    )(side, x, d, w_qkv, gain, *extra, *after)


def swap_spans(x):
    return lax.ppermute(x, "blk", [(0, 1), (1, 0)])


def rows_dot(left, right):
    return lax.dot_general(left, right, (((0,), (0,)), ((), ())), preferred_element_type=f32)


def body(
    inputs, cotangent, lengths, groups, flip,
    w_qkv, b_query, b_value, w_out, b_out, gain_one, shift_one, gain_two, shift_two,
    w_fc, b_fc, w_proj, b_proj,
):
    place = jnp.bitwise_xor(lax.axis_index("blk"), flip[0])
    klen = jnp.minimum(lengths[0] - place * SP, SP)
    place_s = place.reshape(1).astype(jnp.int32)
    klen_s = klen.reshape(1).astype(jnp.int32)
    x_b = inputs[0, 0]
    up_b = cotangent[0, 0]
    xr_b = swap_spans(x_b)

    qkv_bias = jnp.concatenate([b_query, jnp.zeros_like(b_value), b_value])[None]
    vec_one = jnp.stack([gain_one, shift_one])
    normed, qkv = qkv_call(x_b, w_qkv, qkv_bias, vec_one, 3, (), "own_qkv")
    c = col(0)
    tall = pl.BlockSpec((1, 128, SP), lambda j, *_: (j, 0, 0))
    od, ld = call(
        diag_fwd, place_s, klen_s, (qkv, qkv, qkv), [c, col(6), col(12)],
        [S((NP, 128, SP), f32), S((NP, 8, SP), f32)], [tall, ROW],
    )

    normed_r, kvr = qkv_call(xr_b, w_qkv, qkv_bias, vec_one, 2, (ld,), "other_kv")
    attended, lse = call(
        cross_fwd, place_s, klen_s, (qkv, kvr, kvr, od, ld), [c, c, col(6), tall, ROW],
        [S((SP, W), bf16), S((NP, 8, SP), f32)], [c, ROW],
    )

    zero = jnp.zeros_like(b_out)
    vec = jnp.stack([b_out, gain_two, shift_two, b_proj, zero, zero, zero, zero])
    outputs, activ, grad_pre, normed_two, grad_att, grad_attended, sums, grad_b_fc = block_call(
        klen_s, x_b, attended, up_b, w_out, w_fc, w_proj, vec, b_fc[None]
    )
    me = my_id()
    keeps, sends = grads_call(me, normed_two, grad_pre, activ, up_b, attended, grad_att)
    acc = pltpu.VMEM((128, SP), f32)
    flops = 8 * 10**9
    dqx = dkvr = delta = dqkv = None

    def cross_piece(at, pairs, dep):
        nonlocal dqx, dkvr, delta
        dqx, dkvr, delta = call(
            cross_bwd, place_s, klen_s, (qkv, kvr, kvr, grad_attended, attended, lse),
            [col(at), col(at), col(6 + at), col(at), col(at), row(at)],
            [S((SP, W), f32), S((2, SP, W), bf16), S((NP, 8, SP), f32)],
            [col(at), cols(2, at), row(at)], [acc], pairs=pairs,
            into={0: dqx, 1: dkvr, 2: delta} if at else None, after=dep, flops=flops * pairs,
        )

    def diag_piece(at, pairs, dep):
        nonlocal dqkv
        (dqkv,) = call(
            diag_bwd, place_s, klen_s, (qkv, qkv, qkv, grad_attended, lse, delta, dqx),
            [col(at), col(6 + at), col(12 + at), col(at), row(at), row(at), col(at)],
            [S((3, SP, W), bf16)], [cols(3, at)], [acc], pairs=pairs,
            into={0: dqkv} if at else None, after=dep, flops=flops * pairs // 2,
        )

    arrays = lambda state: [a for a, _ in state]
    gain = gain_one[None]
    side = (1 - lax.axis_index("blk")).astype(jnp.int32).reshape(1)
    cross_piece(0, 1, keeps)
    state = core_step(keeps, sends)
    cross_piece(1, 3, arrays(state))
    state = low_step(state, 0)
    cross_piece(4, 2, arrays(state))
    state = low_step(state, 1)
    part_r, sums_r = input_call(side, xr_b, dkvr, w_qkv, gain, (), arrays(state), "other_span")
    returned = lax.all_gather(part_r, "blk", axis=0, tiled=False)
    state = low_step(state, 2)
    diag_piece(0, 3, arrays(state) + [part_r])
    early_sum = last_step(state, [dqkv])
    diag_piece(3, 3, [early_sum])
    early = unpack_early(gather_all(early_sum))

    state = core_step(*late_call(me, normed, normed_r, dqkv, dkvr, []))
    input_grad, sums_o = input_call(
        side, x_b, dqkv, w_qkv, gain, (returned, grad_att), arrays(state), "input_grad"
    )
    state = low_step(state, 0, [sums_o])
    for step in (1, 2, 3):
        state = low_step(state, step)
    late = unpack_late(me, *spread_parts(outer_sum(arrays(state))))

    member = (groups[0] == jnp.arange(2, dtype=jnp.int32)).astype(f32)
    squares = jnp.concatenate([jnp.sum(sums[4:7], 1), klen.astype(f32)[None]])
    sums_one = sums_o + sums_r
    small = jnp.concatenate([
        sums_one[0], sums_one[1], sums[2], sums_one[2], sums_one[3], sums[0], sums[1], grad_b_fc[0], sums[3],
        (member[:, None] * squares[None, :]).reshape(-1), jnp.zeros((1016,), f32),
    ])
    small = sum_small(small.reshape(80, 128)).reshape(-1)
    sizes = [W] * 7 + [4 * W, W]
    pieces = []
    at = 0
    for size in sizes:
        pieces.append(small[at : at + size])
        at += size
    table = small[at : at + 8].reshape(2, 4)
    group_rms = jnp.sqrt(table[:, :3] / (table[:, 3:] * W))
    g_bq, g_bv, g_bo, g_g1, g_s1, g_g2, g_s2, g_bfc, g_bp = pieces
    return (
        outputs[None, None], input_grad[None, None], late, g_bq, g_bv, early[2], g_bo, g_g1, g_s1, g_g2, g_s2,
        early[0], g_bfc, early[1].reshape(4 * W, W), g_bp, group_rms,
    )


def solution(mesh):
    span = P("dp", "blk", None, None)
    return jax.shard_map(
        body,
        mesh=mesh,
        in_specs=(span, span, P("dp"), P("dp"), P("dp")) + (P(),) * 13,
        out_specs=(span, span) + (P(),) * 14,
        check_vma=False,
    )
```

```python
import jax
import jax.numpy as jnp
from jax import lax
from jax.experimental import pallas as pl
from jax.experimental.pallas import tpu as pltpu
from jax.sharding import PartitionSpec as P

SP = 1024
W = 768
NP = 6
EPS = 1e-05
NEG=-1e30
f32=jnp.float32; bf16=jnp.bfloat16
def tdot(a,b): return lax.dot_general(a,b,(((1,),(1,)),((),())),preferred_element_type=f32)
def dot(a,b): return jnp.dot(a,b,preferred_element_type=f32)
def head_masks():
    lane=lax.broadcasted_iota(jnp.int32,(1,128),1)
    return [lane<64, lane>=64]
def softmax_t(s):
    m=jnp.max(s,0,keepdims=True)
    p=jnp.exp(s-m)
    l=jnp.sum(p,0,keepdims=True)
    return m,l,p.astype(bf16)
DQ=256
def diag_fwd(place_ref, klen_ref, q_ref,k_ref,v_ref,o_ref,l_ref):
    hm=head_masks(); klen=klen_ref[0]
    q=q_ref[...]*jnp.asarray(0.125,bf16)
    vt=v_ref[...].T
    z=jnp.zeros((),bf16)
    tiles=[(qi,h) for qi in range(SP//DQ) for h in range(2)]
    kpos=lax.broadcasted_iota(jnp.int32,(SP,1),0)
    low=jnp.where(kpos<klen,kpos,SP)
    def scores(t):
        qi,h=t; n=(qi+1)*DQ
        ok=(qi*DQ+lax.broadcasted_iota(jnp.int32,(n,DQ),1))>=low[:n]
        return jnp.where(ok,tdot(k_ref[:n],jnp.where(hm[h],q[qi*DQ:n],z)),NEG)
    def finish(t,m,l,p):
        qi,h=t; n=(qi+1)*DQ; sl=slice(qi*DQ,n)
        acc=dot(vt[h*64:(h+1)*64,:n],p)
        o_ref[0,h*64:(h+1)*64,sl]=acc*(1.0/l)
        l_ref[0,h:h+1,sl]=m+jnp.log(l)
    pipeline(tiles,scores,softmax_t,finish)
def pipeline(tiles,scores,mid,finish,depth=2):
    s=scores(tiles[0]); pend=None
    for i,t in enumerate(tiles):
        sn=scores(tiles[i+1]) if i+1<len(tiles) else None
        r=mid(s) if not isinstance(s,tuple) else mid(t,*s)
        if depth==2:
            if pend: finish(*pend)
            pend=(t,)+r
        else: finish(t,*r)
        s=sn
    if pend: finish(*pend)
CQ=512
def cross_fwd(place_ref, klen_ref, q_ref,k_ref,v_ref,od_ref,ld_ref,o_ref,l_ref):
    hm=head_masks()
    @pl.when(place_ref[0]==1)
    def _():
        q=q_ref[...]*jnp.asarray(0.125,bf16)
        vt=v_ref[...].T
        z=jnp.zeros((),bf16)
        tiles=[(qi,h) for qi in range(SP//CQ) for h in range(2)]
        res={}
        def scores(t):
            qi,h=t
            return tdot(k_ref[...],jnp.where(hm[h],q[qi*CQ:(qi+1)*CQ],z))
        def finish(t,m,l,p):
            qi,h=t; sl=slice(qi*CQ,(qi+1)*CQ)
            acc=dot(vt[h*64:(h+1)*64],p)
            ld=ld_ref[0,h:h+1,sl]
            lx=m+jnp.log(l)
            mx=jnp.maximum(ld,lx)
            ed=jnp.exp(ld-mx); ex=jnp.exp(lx-mx); tot=ed+ex
            l_ref[0,h:h+1,sl]=mx+jnp.log(tot)
            res[t]=od_ref[0,h*64:(h+1)*64,sl]*(ed/tot)+acc*(ex/(tot*l))
            if h==1: o_ref[sl]=jnp.concatenate([res[(qi,0)],res[(qi,1)]],0).T.astype(bf16)
        pipeline(tiles,scores,softmax_t,finish)
    @pl.when(place_ref[0]==0)
    def _():
        o_ref[...]=od_ref[0].T.astype(bf16)
        l_ref[...]=ld_ref[...]
KB=256
def bwd_prep(q_ref,do_ref,hm):
    q=q_ref[...]*jnp.asarray(0.125,bf16)
    z=jnp.zeros((),bf16)
    do=do_ref[...]
    return [jnp.where(hm[h],q,z) for h in range(2)],[jnp.where(hm[h],do,z) for h in range(2)]
def bwd_tiles(k_ref,v_ref,qm,dm,lrow,drow,put,dqt,start,mask,KB):
    tiles=[(kb,h) for kb in range(SP//KB) for h in range(2)]
    acc={}
    kts={}
    def scores(t):
        kb,h=t; ks=slice(kb*KB,(kb+1)*KB); q0=start(kb)
        return tdot(k_ref[ks],qm[h][q0:]),tdot(v_ref[ks],dm[h][q0:])
    def mid(t,s,dp):
        kb,h=t; q0=start(kb)
        p=jnp.exp(s-lrow(h)[:,q0:])
        if mask is not None: p=jnp.where(mask(kb),p,0.0)
        ds=p*(dp-drow(h)[:,q0:])
        return p.astype(bf16),ds.astype(bf16)
    def finish(t,p,ds):
        kb,h=t; ks=slice(kb*KB,(kb+1)*KB); q0=start(kb)
        if h==0: kts[kb]=k_ref[ks].T
        a=dot(p,dm[h][q0:]); b=dot(ds,qm[h][q0:])
        if h==0: acc[kb]=(a,b)
        else:
            put(ks,(acc[kb][1]+b).astype(bf16),(acc[kb][0]+a).astype(bf16))
        c=dot(kts[kb][h*64:(h+1)*64],ds)
        if kb==0: dqt[h*64:(h+1)*64]=c
        else: dqt[h*64:(h+1)*64,q0:]+=c
    pipeline(tiles,scores,mid,finish)
def cross_bwd(place_ref, klen_ref, q_ref,k_ref,v_ref,do_ref,o_ref,l_ref,dq_ref,dkv_ref,dl_ref,dqt):
    hm=head_masks()
    prod=do_ref[...].astype(f32)*o_ref[...].astype(f32)
    t=prod.T
    dl_ref[0,0:1]=jnp.sum(t[:64],0,keepdims=True); dl_ref[0,1:2]=jnp.sum(t[64:],0,keepdims=True)
    @pl.when(place_ref[0]==1)
    def _():
        def put(ks,dk,dv):
            dkv_ref[0,ks]=dk
            dkv_ref[1,ks]=dv
        qm,dm=bwd_prep(q_ref,do_ref,hm)
        bwd_tiles(k_ref,v_ref,qm,dm,lambda h:l_ref[0,h:h+1],lambda h:dl_ref[0,h:h+1],put,dqt,lambda kb:0,None,512)
        dq_ref[...]=dqt[...].T*0.125
    @pl.when(place_ref[0]==0)
    def _():
        dkv_ref[...]=jnp.zeros_like(dkv_ref); dq_ref[...]=jnp.zeros_like(dq_ref)
def diag_bwd(place_ref, klen_ref, q_ref,k_ref,v_ref,do_ref,l_ref,dl_ref,dqx_ref,out_ref,dqt):
    hm=head_masks(); klen=klen_ref[0]
    qm,dm=bwd_prep(q_ref,do_ref,hm)
    def put(ks,dk,dv):
        out_ref[1,ks]=dk
        out_ref[2,ks]=dv
    kpos=lax.broadcasted_iota(jnp.int32,(SP,1),0)
    low=jnp.where(kpos<klen,kpos,SP)
    def mask(kb):
        q0=kb*KB
        return q0+lax.broadcasted_iota(jnp.int32,(KB,SP-q0),1)>=low[q0:q0+KB]
    bwd_tiles(k_ref,v_ref,qm,dm,lambda h:l_ref[0,h:h+1],lambda h:dl_ref[0,h:h+1],put,dqt,lambda kb:kb*KB,mask,KB)
    out_ref[0]=(dqt[...].T*0.125+dqx_ref[...]).astype(bf16)
S=jax.ShapeDtypeStruct
def col(base,rows=SP): return pl.BlockSpec((rows,128),lambda j,*_:(0,base+j))
def cols(n,base): return pl.BlockSpec((n,SP,128),lambda j,*_:(0,0,base+j))
def row(base): return pl.BlockSpec((1,8,SP),lambda j,*_:(base+j,0,0))
ROW=row(0)
def call(fn,place,klen,ins,in_specs,outs,out_specs,scratch=(),pairs=NP,into=None,after=(),flops=0,trans=0):
    into=into or {}
    extra=list(into.items())
    n=2+len(ins)
    m=len(extra)
    skip=n+m+len(after)
    def kern(*refs): return fn(*refs[:n],*refs[skip:])
    specs=list(in_specs)+[pl.BlockSpec(memory_space=pl.ANY)]*(m+len(after))
    return pl.pallas_call(kern,
        grid_spec=pltpu.PrefetchScalarGridSpec(num_scalar_prefetch=2,grid=(pairs,),in_specs=specs,out_specs=out_specs,scratch_shapes=list(scratch)),
        out_shape=outs,
        input_output_aliases={n+i:o for i,(o,_) in enumerate(extra)},
        compiler_params=pltpu.CompilerParams(vmem_limit_bytes=50*1024*1024,dimension_semantics=("arbitrary",)),
        cost_estimate=pl.CostEstimate(flops=flops,bytes_accessed=pairs*10**4,transcendentals=trans),
        name=fn.__name__,
    )(place,klen,*ins,*[x for _,x in extra],*after)


BITS = {"c": ("dp", 1), "y": ("dp", 2), "u": ("dp", 4), "v": ("dp", 8), "x": ("blk", 1)}
LOW = "xyuv"
ORDERS = ("xyuv", "yuxv", "uxyv")
RB = 48


def swap(a, bit):
    axis, step = BITS[bit] if isinstance(bit, str) else ("dp", bit)
    return lax.ppermute(a, axis, [(i, i ^ step) for i in range(lax.axis_size(axis))])


def outer_steps():
    size = lax.axis_size("dp")
    return [1 << k for k in range(4, 16) if (1 << k) < size]


def my_id():
    place = 0
    for bit in "c" + LOW:
        axis, step = BITS[bit]
        place = 2 * place + (lax.axis_index(axis) // step) % 2
    return place.astype(jnp.int32).reshape(1)


def add(a, b):
    return (a.astype(f32) + b.astype(f32)).astype(bf16)


def core_step(keeps, sends):
    state = []
    for keep, send in zip(keeps, sends):
        a = add(keep, swap(send, "c"))
        state.append((a.reshape((2,) * 4 + a.shape[1:]), LOW))
    return state


def low_step(state, step, after=None):
    waiting = []
    for (a, bits), order in zip(state, ORDERS):
        at = bits.index(order[step])
        keep, send = lax.index_in_dim(a, 0, at, False), lax.index_in_dim(a, 1, at, False)
        waiting.append((keep, swap(send, order[step]), bits.replace(order[step], "")))
    if after is not None:
        flat = lambda a: a.reshape(-1, a.shape[-1])
        sums = sum_kernel([(flat(keep), flat(got)) for keep, got, _ in waiting], after, "step_sum")
        return [(a.reshape(keep.shape), bits) for a, (keep, _, bits) in zip(sums, waiting)]
    return [(add(keep, got), bits) for keep, got, bits in waiting]


def sum_kernel(pairs, after, name):
    n = len(pairs)

    def kern(*refs):
        for i in range(n):
            a, b = refs[i][...], refs[n + i][...]
            refs[i - n][...] = (a.astype(f32) + b.astype(f32)).astype(a.dtype)

    vmem = pl.BlockSpec(memory_space=pltpu.VMEM)
    return pl.pallas_call(
        kern,
        in_specs=[vmem] * (2 * n) + [pl.BlockSpec(memory_space=pl.ANY)] * len(after),
        out_specs=[vmem] * n,
        out_shape=[S(a.shape, a.dtype) for a, _ in pairs],
        name=name,
    )(*[a for a, _ in pairs], *[b for _, b in pairs], *after)


def last_step(state, after):
    keep = jnp.stack([a[0] for a, _ in state])
    got = swap(jnp.stack([a[1] for a, _ in state]), ORDERS[0][3])
    (total,) = sum_kernel([(keep, got)], after, "last_sum")
    for step in outer_steps():
        total = add(total, swap(total, step))
    return total


def outer_sum(blocks):
    for step in outer_steps():
        blocks = [add(a, swap(a, step)) for a in blocks]
    return blocks


def reduce_parts(keeps, sends):
    state = core_step(keeps, sends)
    for step in range(4):
        state = low_step(state, step)
    return outer_sum([a for a, _ in state])


def spread_parts(blocks):
    state = [a[None] for a in blocks]
    for step in (3, 2, 1, 0):
        state = [jnp.concatenate([a, swap(a, o[step])], 0) for a, o in zip(state, ORDERS)]
    return state, [swap(a, "c") for a in state]


def sum_small(a):
    for bit in "c" + LOW:
        a = a + swap(a, bit)
    for step in outer_steps():
        a = a + swap(a, step)
    return a


def low_index(p, order):
    r = 0
    for bit in order:
        r = 2 * r + (p // (1 << (3 - LOW.index(bit)))) % 2
    return r


def gather_all(blocks):
    a = lax.all_gather(blocks, ("dp", "blk"), axis=0, tiled=False)
    return a[:32]


def device_of(block):
    c, x, y, u, v = [(block // (1 << (4 - i))) % 2 for i in range(5)]
    return (v * 8 + u * 4 + y * 2 + c) * 2 + x


def unpack_early(gathered):
    rows = 2

    def kern(*refs):
        ins, (fc, proj, out) = refs[: 2 * rows], refs[2 * rows :]
        for core in range(2):
            for r in range(rows):
                a = ins[core * rows + r]
                at = slice(r * RB, (r + 1) * RB)
                fc[at, core * 1536 : core * 1536 + 1152] = a[0, 0].astype(f32)
                fc[at, core * 1536 + 1152 : (core + 1) * 1536] = a[0, 1, :, :384].astype(f32)
                proj[core, 2 * r * RB : (2 * r + 1) * RB] = a[0, 1, :, 384:].astype(f32)
                proj[core, (2 * r + 1) * RB : (2 * r + 2) * RB] = a[0, 2, :, :768].astype(f32)
                out[at, core * 384 : (core + 1) * 384] = a[0, 2, :, 768:].astype(f32)

    block = (1,) + gathered.shape[1:]
    return pl.pallas_call(
        kern,
        grid=(16 // rows,),
        in_specs=[
            pl.BlockSpec(block, lambda b, core=core, r=r: (device_of(core * 16 + b * rows + r), 0, 0, 0))
            for core in range(2) for r in range(rows)
        ],
        out_specs=[
            pl.BlockSpec((rows * RB, 4 * W), lambda b: (b, 0)),
            pl.BlockSpec((2, 2 * rows * RB, W), lambda b: (0, b, 0)),
            pl.BlockSpec((rows * RB, W), lambda b: (b, 0)),
        ],
        out_shape=[S((W, 4 * W), f32), S((2, 2 * W, W), f32), S((W, W), f32)],
        compiler_params=pltpu.CompilerParams(vmem_limit_bytes=56 * 1024 * 1024),
        cost_estimate=pl.CostEstimate(flops=0, bytes_accessed=3 * gathered.size * 2, transcendentals=0),
        name="unpack_early",
    )(*[gathered] * (2 * rows))


def unpack_late(me, mine, other, after):
    n = len(mine)
    rows = 4
    lanes = mine[0].shape[2]

    def kern(me_ref, *refs):
        own, far, out = refs[:n], refs[n : 2 * n], refs[-1]
        core, low = me_ref[0] // 16, me_ref[0] % 16
        step = pl.program_id(0)

        def fill(half, ins):
            for r in range(rows):
                place = (step * rows + r) ^ low
                for part in range(n):
                    at = (half * n + part) * lanes
                    out[r * RB : (r + 1) * RB, at : at + lanes] = ins[part][low_index(place, ORDERS[part])].astype(f32)

        for half in range(2):
            @pl.when(core == half)
            def _():
                fill(half, own)

            @pl.when(core != half)
            def _():
                fill(half, far)

    whole = pl.BlockSpec(mine[0].shape, lambda b, *_: (0, 0, 0))
    return pl.pallas_call(
        kern,
        grid_spec=pltpu.PrefetchScalarGridSpec(
            num_scalar_prefetch=1, grid=(16 // rows,), in_specs=[whole] * (2 * n) + [pl.BlockSpec(memory_space=pl.ANY)] * len(after),
            out_specs=pl.BlockSpec((rows * RB, 3 * W), lambda b, *_: (b, 0)),
        ),
        out_shape=S((W, 3 * W), f32),
        compiler_params=pltpu.CompilerParams(vmem_limit_bytes=56 * 1024 * 1024),
        cost_estimate=pl.CostEstimate(flops=0, bytes_accessed=10**7, transcendentals=0),
        name="unpack_late",
    )(me, *mine, *other, *after)


MR = 256
QR = 512
FC = 1536
C0 = 0.7978845608028654
C1 = C0 * 0.044715


def rowmean(a):
    return jnp.sum(a, -1, keepdims=True) * (1.0 / W)


def block_kernel(
    klen_ref, x_ref, att_ref, up_ref, w_out_ref, w_fc_ref, w_proj_ref, b_out_ref, gain_ref, shift_ref, b_proj_ref, b_fc_ref,
    y_ref, act_ref, pre_ref, mid_ref, gatt_ref, do_ref, sums_ref, bsum_ref,
):
    step = pl.program_id(0)

    @pl.when(step == 0)
    def _():
        sums_ref[...] = jnp.zeros_like(sums_ref)
        bsum_ref[...] = jnp.zeros_like(bsum_ref)

    up_b = up_ref[...]
    up = up_b.astype(f32)
    branch_att = dot(att_ref[...], w_out_ref[...]) + b_out_ref[...][None]
    middle = x_ref[...].astype(f32) + branch_att
    centered = middle - rowmean(middle)
    inv = lax.rsqrt(rowmean(centered * centered) + EPS)
    x_hat = centered * inv
    gain = gain_ref[...][None]
    normed = (x_hat * gain + shift_ref[...][None]).astype(bf16)
    mid_ref[...] = normed
    chunks = range(4 * W // FC)
    sl = lambda c: slice(c * FC, (c + 1) * FC)

    def first(c):
        return dot(normed, w_fc_ref[:, sl(c)]), tdot(up_b, w_proj_ref[sl(c)])

    mlp = None
    back = None
    ahead = first(0)
    for c in chunks:
        u, dz = ahead
        if c + 1 < len(chunks):
            ahead = first(c + 1)
        u = u + b_fc_ref[sl(c)][None]
        v = u * u
        h = 0.5 + 0.5 * jnp.tanh(u * (C0 + C1 * v))
        z = (u * h).astype(bf16)
        d = dz * (h + (u * (2 * C0 + 6 * C1 * v)) * (h * (1.0 - h)))
        bsum_ref[0:1, sl(c)] += jnp.sum(d, 0, keepdims=True)
        d = d.astype(bf16)
        act_ref[:, sl(c)] = z
        pre_ref[:, sl(c)] = d
        a = dot(z, w_proj_ref[sl(c)])
        b = tdot(d, w_fc_ref[:, sl(c)])
        mlp = a if mlp is None else mlp + a
        back = b if back is None else back + b
    branch_mlp = mlp + b_proj_ref[...][None]
    out = middle + branch_mlp
    y_ref[...] = out.astype(bf16)
    scaled = back * gain
    grad = up + inv * (scaled - rowmean(scaled) - x_hat * rowmean(scaled * x_hat))
    gatt = grad.astype(bf16)
    gatt_ref[...] = gatt
    do_ref[...] = tdot(gatt, w_out_ref[...]).astype(bf16)
    valid = step * MR + lax.broadcasted_iota(jnp.int32, (MR, 1), 0) < klen_ref[0]
    total = lambda a: jnp.sum(a, 0, keepdims=True)
    kept = lambda a: total(jnp.where(valid, a * a, 0.0))
    sums_ref[...] += jnp.concatenate(
        [total(back * x_hat), total(back), total(grad), total(up), kept(out), kept(branch_att), kept(branch_mlp),
         jnp.zeros((1, W), f32)], 0,
    )


def block_call(klen, x, att, up, w_out, w_fc, w_proj, b_out, gain, shift, b_proj, b_fc):
    once = pl.Buffered(1)
    rows = lambda width: pl.BlockSpec((MR, width), lambda i, *_: (i, 0))
    whole = lambda shape: pl.BlockSpec(shape, lambda i, *_: (0, 0), pipeline_mode=once)
    const = lambda shape: pl.BlockSpec(shape, lambda i, *_: (0, 0))
    line = lambda size: pl.BlockSpec((size,), lambda i, *_: (0,))
    return pl.pallas_call(
        block_kernel,
        grid_spec=pltpu.PrefetchScalarGridSpec(
            num_scalar_prefetch=1,
            grid=(SP // MR,),
            in_specs=[rows(W)] * 3 + [whole((W, W)), whole((W, 4 * W)), whole((4 * W, W)), line(W), line(W), line(W), line(W), line(4 * W)],
            out_specs=[rows(W), rows(4 * W), rows(4 * W), rows(W), rows(W), rows(W), const((8, W)), const((1, 4 * W))],
        ),
        out_shape=[
            S((SP, W), bf16), S((SP, 4 * W), bf16), S((SP, 4 * W), bf16), S((SP, W), bf16),
            S((SP, W), bf16), S((SP, W), bf16), S((8, W), f32), S((1, 4 * W), f32),
        ],
        compiler_params=pltpu.CompilerParams(vmem_limit_bytes=56 * 1024 * 1024),
        cost_estimate=pl.CostEstimate(flops=22 * 10**9, bytes_accessed=35 * 10**6, transcendentals=3 * 10**6),
        name="block_mlp",
    )(klen, x, att, up, w_out, w_fc, w_proj, b_out, gain, shift, b_proj, b_fc)


def grads_kernel(me_ref, mid_ref, pre_ref, act_ref, up_ref, att_ref, gatt_ref, k0, k1, k2, s0, s1, s2, mid_t):
    step = pl.program_id(0)
    core, low = me_ref[0] // 16, me_ref[0] % 16

    @pl.when(step == 0)
    def _():
        mid_t[...] = mid_ref[...].T

    def by_core(half, fill, keep, send):
        @pl.when(half == core)
        def _():
            fill(*keep)

        @pl.when(half != core)
        def _():
            fill(*send)

    @pl.when(step < 4)
    def _():
        tile = dot(mid_t[...], pre_ref[...]).astype(bf16)

        def left(one):
            for i in range(16):
                one[i ^ low, :, :768] = tile[i * RB : (i + 1) * RB]

        def right(one, two):
            for i in range(16):
                one[i ^ low, :, 768:] = tile[i * RB : (i + 1) * RB, :384]
                two[i ^ low, :, :384] = tile[i * RB : (i + 1) * RB, 384:]

        @pl.when(step % 2 == 0)
        def _():
            by_core(step // 2, left, (k0,), (s0,))

        @pl.when(step % 2 == 1)
        def _():
            by_core(step // 2, right, (k0, k1), (s0, s1))

    @pl.when((step >= 4) & (step < 8))
    def _():
        tile = rows_dot(act_ref[...], up_ref[...]).astype(bf16)
        first = (step - 4) % 2 * 8

        def fill(one, two):
            for i in range(8):
                at = (first + i) ^ low
                one[at, :, 384:] = tile[2 * i * RB : (2 * i + 1) * RB]
                two[at, :, :768] = tile[(2 * i + 1) * RB : (2 * i + 2) * RB]

        by_core((step - 4) // 2, fill, (k1, k2), (s1, s2))

    @pl.when(step == 8)
    def _():
        tile = rows_dot(att_ref[...], gatt_ref[...]).astype(bf16)

        def fill(one, two):
            for i in range(16):
                one[i ^ low, :, 768:] = tile[i * RB : (i + 1) * RB, :384]
                two[i ^ low, :, 768:] = tile[i * RB : (i + 1) * RB, 384:]

        by_core(0, fill, (k2, s2), (s2, k2))


def grads_call(me, mid, pre, act, up, att, gatt):
    clip = lambda i, lo, hi: jnp.clip(i, lo, hi) - lo
    whole = pl.BlockSpec((SP, W), lambda i, *_: (0, 0))
    part = pl.BlockSpec((16, RB, 1152), lambda i, *_: (0, 0, 0))
    res = pl.pallas_call(
        grads_kernel,
        grid_spec=pltpu.PrefetchScalarGridSpec(
            num_scalar_prefetch=1,
            grid=(9,),
            in_specs=[
                whole,
                pl.BlockSpec((SP, W), lambda i, *_: (0, clip(i, 0, 3))),
                pl.BlockSpec((SP, W), lambda i, *_: (0, clip(i, 4, 7))),
                whole,
                whole,
                whole,
            ],
            out_specs=[part] * 6,
            scratch_shapes=[pltpu.VMEM((W, SP), bf16)],
        ),
        out_shape=[S((16, RB, 1152), bf16)] * 6,
        compiler_params=pltpu.CompilerParams(vmem_limit_bytes=56 * 1024 * 1024),
        cost_estimate=pl.CostEstimate(flops=11 * 10**9, bytes_accessed=30 * 10**6, transcendentals=0),
        name="block_grads",
    )(me, mid, pre, act, up, att, gatt)
    return res[:3], res[3:]


def late_kernel(me_ref, a_ref, ar_ref, d_ref, dr_ref, k0, k1, k2, s0, s1, s2, a_t, ar_t):
    step = pl.program_id(0)
    core, low = me_ref[0] // 16, me_ref[0] % 16

    def put(keep, send, tile):
        def fill(ref):
            for i in range(16):
                ref[i ^ low] = tile[i * RB : (i + 1) * RB]

        return lambda half: (
            pl.when(core == half)(lambda: fill(keep)),
            pl.when(core != half)(lambda: fill(send)),
        )

    @pl.when(step == 0)
    def _():
        a_t[...] = a_ref[...].T
        ar_t[...] = ar_ref[...].T
        tile = dot(a_t[...], d_ref[0]).astype(bf16)
        put(k0, s0, tile[:, :384])(0)
        put(k1, s1, tile[:, 384:])(0)

    @pl.when(step == 1)
    def _():
        tile = (dot(a_t[...], d_ref[0]) + dot(ar_t[...], dr_ref[0])).astype(bf16)
        put(k2, s2, tile[:, :384])(0)
        put(k0, s0, tile[:, 384:])(1)

    @pl.when(step == 2)
    def _():
        tile = (dot(a_t[...], d_ref[0]) + dot(ar_t[...], dr_ref[0])).astype(bf16)
        put(k1, s1, tile[:, :384])(1)
        put(k2, s2, tile[:, 384:])(1)


def late_call(me, a, ar, d, dr, after):
    def kern(*refs):
        return late_kernel(*refs[:5], *refs[5 + len(after) :])

    whole = pl.BlockSpec((SP, W), lambda i, *_: (0, 0))
    part = pl.BlockSpec((16, RB, 384), lambda i, *_: (0, 0, 0))
    res = pl.pallas_call(
        kern,
        grid_spec=pltpu.PrefetchScalarGridSpec(
            num_scalar_prefetch=1,
            grid=(3,),
            in_specs=[
                whole,
                whole,
                pl.BlockSpec((1, SP, W), lambda i, *_: (i, 0, 0)),
                pl.BlockSpec((1, SP, W), lambda i, *_: (jnp.maximum(i - 1, 0), 0, 0)),
            ] + [pl.BlockSpec(memory_space=pl.ANY)] * len(after),
            out_specs=[part] * 6,
            scratch_shapes=[pltpu.VMEM((W, SP), bf16)] * 2,
        ),
        out_shape=[S((16, RB, 384), bf16)] * 6,
        compiler_params=pltpu.CompilerParams(vmem_limit_bytes=56 * 1024 * 1024),
        cost_estimate=pl.CostEstimate(flops=6 * 10**9, bytes_accessed=14 * 10**6, transcendentals=0),
        name="late_grads",
    )(me, a, ar, d, dr, *after)
    return res[:3], res[3:]


def qkv_call(x, w_qkv, b_query, b_value, gain, shift, n, after, name):
    def kern(x_ref, w_ref, bq_ref, bv_ref, gain_ref, shift_ref, *refs):
        a_ref, out_ref = refs[len(after) :]
        a = (norm_one(x_ref)[0] * gain_ref[...][None] + shift_ref[...][None]).astype(bf16)
        a_ref[...] = a
        if n == 3:
            out_ref[:, :W] = (dot(a, w_ref[:, :W]) + bq_ref[...][None]).astype(bf16)
        out_ref[:, (n - 2) * W : (n - 1) * W] = dot(a, w_ref[:, W : 2 * W]).astype(bf16)
        out_ref[:, (n - 1) * W :] = (dot(a, w_ref[:, 2 * W :]) + bv_ref[...][None]).astype(bf16)

    rows = lambda width: pl.BlockSpec((QR, width), lambda i: (i, 0))
    return pl.pallas_call(
        kern,
        grid=(SP // QR,),
        in_specs=[
            rows(W),
            pl.BlockSpec((W, 3 * W), lambda i: (0, 0)),
        ] + [pl.BlockSpec((W,), lambda i: (0,))] * 4 + [pl.BlockSpec(memory_space=pl.ANY)] * len(after),
        out_specs=[rows(W), rows(n * W)],
        out_shape=[S((SP, W), bf16), S((SP, n * W), bf16)],
        compiler_params=pltpu.CompilerParams(vmem_limit_bytes=56 * 1024 * 1024),
        cost_estimate=pl.CostEstimate(flops=n * 12 * 10**8, bytes_accessed=10**7, transcendentals=0),
        name=name,
    )(x, w_qkv, b_query, b_value, gain, shift, *after)


def norm_one(x_ref):
    x = x_ref[...].astype(f32)
    centered = x - rowmean(x)
    inv = lax.rsqrt(rowmean(centered * centered) + EPS)
    return centered * inv, inv


def input_kernel(x_ref, d_ref, w_ref, gain_ref, *refs):
    n = d_ref.shape[0]
    sums_ref = refs[-1]

    @pl.when(pl.program_id(0) == 0)
    def _():
        sums_ref[...] = jnp.zeros_like(sums_ref)

    x_hat, inv = norm_one(x_ref)
    part = None
    for i in range(n):
        a = tdot(d_ref[i], w_ref[:, (3 - n + i) * W : (4 - n + i) * W])
        part = a if part is None else part + a
    total = lambda a: jnp.sum(a.astype(f32), 0, keepdims=True)
    first = total(d_ref[0]) if n == 3 else jnp.zeros((1, W), f32)
    sums_ref[...] += jnp.concatenate(
        [first, total(d_ref[n - 1]), total(part * x_hat), total(part), jnp.zeros((4, W), f32)], 0
    )
    if n == 2:
        refs[0][...] = part.astype(bf16)
    else:
        returned_ref, gatt_ref = refs[:2]
        scaled = (part + returned_ref[0].astype(f32)) * gain_ref[...][None]
        inner = scaled - rowmean(scaled) - x_hat * rowmean(scaled * x_hat)
        refs[-2][...] = (gatt_ref[...].astype(f32) + inv * inner).astype(bf16)


def input_call(side, x, d, w_qkv, gain, extra, after, name):
    n = d.shape[0]
    rows = pl.BlockSpec((QR, W), lambda i, *_: (i, 0))
    more = [pl.BlockSpec((1, QR, W), lambda i, side_ref: (side_ref[0], i, 0)), rows] if extra else []
    skip = 5 + len(extra)

    def kern(*refs):
        return input_kernel(*refs[1:skip], *refs[skip + len(after) :])

    return pl.pallas_call(
        kern,
        grid_spec=pltpu.PrefetchScalarGridSpec(
            num_scalar_prefetch=1,
            grid=(SP // QR,),
            in_specs=[
                rows,
                pl.BlockSpec((n, QR, W), lambda i, *_: (0, i, 0)),
                pl.BlockSpec((W, 3 * W), lambda i, *_: (0, 0)),
                pl.BlockSpec((W,), lambda i, *_: (0,)),
            ] + more + [pl.BlockSpec(memory_space=pl.ANY)] * len(after),
            out_specs=[rows, pl.BlockSpec((8, W), lambda i, *_: (0, 0))],
        ),
        out_shape=[S((SP, W), bf16), S((8, W), f32)],
        compiler_params=pltpu.CompilerParams(vmem_limit_bytes=56 * 1024 * 1024),
        cost_estimate=pl.CostEstimate(flops=n * 12 * 10**8, bytes_accessed=10**7, transcendentals=0),
        name=name,
    )(side, x, d, w_qkv, gain, *extra, *after)


def swap_spans(x):
    return lax.ppermute(x, "blk", [(0, 1), (1, 0)])


def rows_dot(left, right):
    return lax.dot_general(left, right, (((0,), (0,)), ((), ())), preferred_element_type=f32)


def body(
    inputs, cotangent, lengths, groups, flip,
    w_qkv, b_query, b_value, w_out, b_out, gain_one, shift_one, gain_two, shift_two,
    w_fc, b_fc, w_proj, b_proj,
):
    place = jnp.bitwise_xor(lax.axis_index("blk"), flip[0])
    klen = jnp.minimum(lengths[0] - place * SP, SP)
    place_s = place.reshape(1).astype(jnp.int32)
    klen_s = klen.reshape(1).astype(jnp.int32)
    x_b = inputs[0, 0]
    up_b = cotangent[0, 0]
    xr_b = swap_spans(x_b)

    normed, qkv = qkv_call(x_b, w_qkv, b_query, b_value, gain_one, shift_one, 3, (), "own_qkv")
    c = col(0)
    tall = pl.BlockSpec((1, 128, SP), lambda j, *_: (j, 0, 0))
    od, ld = call(
        diag_fwd, place_s, klen_s, (qkv, qkv, qkv), [c, col(6), col(12)],
        [S((NP, 128, SP), f32), S((NP, 8, SP), f32)], [tall, ROW],
    )

    normed_r, kvr = qkv_call(xr_b, w_qkv, b_query, b_value, gain_one, shift_one, 2, (ld,), "other_kv")
    attended, lse = call(
        cross_fwd, place_s, klen_s, (qkv, kvr, kvr, od, ld), [c, c, col(6), tall, ROW],
        [S((SP, W), bf16), S((NP, 8, SP), f32)], [c, ROW],
    )

    outputs, activ, grad_pre, normed_two, grad_att, grad_attended, sums, grad_b_fc = block_call(
        klen_s, x_b, attended, up_b, w_out, w_fc, w_proj, b_out, gain_two, shift_two, b_proj, b_fc
    )
    me = my_id()
    keeps, sends = grads_call(me, normed_two, grad_pre, activ, up_b, attended, grad_att)
    acc = pltpu.VMEM((128, SP), f32)
    flops = 8 * 10**9
    dqx = dkvr = delta = dqkv = None

    def cross_piece(at, pairs, dep):
        nonlocal dqx, dkvr, delta
        dqx, dkvr, delta = call(
            cross_bwd, place_s, klen_s, (qkv, kvr, kvr, grad_attended, attended, lse),
            [col(at), col(at), col(6 + at), col(at), col(at), row(at)],
            [S((SP, W), f32), S((2, SP, W), bf16), S((NP, 8, SP), f32)],
            [col(at), cols(2, at), row(at)], [acc], pairs=pairs,
            into={0: dqx, 1: dkvr, 2: delta} if at else None, after=dep, flops=flops * pairs,
        )

    def diag_piece(at, pairs, dep):
        nonlocal dqkv
        (dqkv,) = call(
            diag_bwd, place_s, klen_s, (qkv, qkv, qkv, grad_attended, lse, delta, dqx),
            [col(at), col(6 + at), col(12 + at), col(at), row(at), row(at), col(at)],
            [S((3, SP, W), bf16)], [cols(3, at)], [acc], pairs=pairs,
            into={0: dqkv} if at else None, after=dep, flops=flops * pairs // 2,
        )

    arrays = lambda state: [a for a, _ in state]
    gain = gain_one
    side = (1 - lax.axis_index("blk")).astype(jnp.int32).reshape(1)
    cross_piece(0, 1, keeps)
    state = core_step(keeps, sends)
    cross_piece(1, 3, arrays(state))
    state = low_step(state, 0)
    cross_piece(4, 2, arrays(state))
    part_r, sums_r = input_call(side, xr_b, dkvr, w_qkv, gain, (), (), "other_span")
    returned = lax.all_gather(part_r, "blk", axis=0, tiled=False)
    state = low_step(state, 1)
    state = low_step(state, 2)
    diag_piece(0, 3, arrays(state) + [part_r])
    early_sum = last_step(state, [dqkv])
    diag_piece(3, 3, [early_sum])
    early = unpack_early(gather_all(early_sum))

    state = core_step(*late_call(me, normed, normed_r, dqkv, dkvr, []))
    input_grad, sums_o = input_call(
        side, x_b, dqkv, w_qkv, gain, (returned, grad_att), arrays(state), "input_grad"
    )
    state = low_step(state, 0, [sums_o])
    state = low_step(state, 1)
    state = low_step(state, 2)
    state = low_step(state, 3)
    late = unpack_late(me, *spread_parts(outer_sum(arrays(state))), [early[0]])

    member = (groups[0] == jnp.arange(2, dtype=jnp.int32)).astype(f32)
    squares = jnp.concatenate([jnp.sum(sums[4:7], 1), klen.astype(f32)[None]])
    sums_one = sums_o + sums_r
    small = jnp.concatenate([
        sums_one[0], sums_one[1], sums[2], sums_one[2], sums_one[3], sums[0], sums[1], grad_b_fc[0], sums[3],
        (member[:, None] * squares[None, :]).reshape(-1), jnp.zeros((1016,), f32),
    ])
    small = sum_small(small.reshape(80, 128)).reshape(-1)
    sizes = [W] * 7 + [4 * W, W]
    pieces = []
    at = 0
    for size in sizes:
        pieces.append(small[at : at + size])
        at += size
    table = small[at : at + 8].reshape(2, 4)
    group_rms = jnp.sqrt(table[:, :3] / (table[:, 3:] * W))
    g_bq, g_bv, g_bo, g_g1, g_s1, g_g2, g_s2, g_bfc, g_bp = pieces
    return (
        outputs[None, None], input_grad[None, None], late, g_bq, g_bv, early[2], g_bo, g_g1, g_s1, g_g2, g_s2,
        early[0], g_bfc, early[1].reshape(4 * W, W), g_bp, group_rms,
    )


def solution(mesh):
    span = P("dp", "blk", None, None)
    return jax.shard_map(
        body,
        mesh=mesh,
        in_specs=(span, span, P("dp"), P("dp"), P("dp")) + (P(),) * 13,
        out_specs=(span, span) + (P(),) * 14,
        check_vma=False,
    )
```

```python
import jax
import jax.numpy as jnp
from jax import lax
from jax.experimental import pallas as pl
from jax.experimental.pallas import tpu as pltpu
from jax.sharding import PartitionSpec as P

SP = 1024
W = 768
NP = 6
EPS = 1e-05
NEG=-1e30
f32=jnp.float32; bf16=jnp.bfloat16
def tdot(a,b): return lax.dot_general(a,b,(((1,),(1,)),((),())),preferred_element_type=f32)
def dot(a,b): return jnp.dot(a,b,preferred_element_type=f32)
def head_masks():
    lane=lax.broadcasted_iota(jnp.int32,(1,128),1)
    return [lane<64, lane>=64]
def softmax_t(s):
    m=jnp.max(s,0,keepdims=True)
    p=jnp.exp(s-m)
    l=jnp.sum(p,0,keepdims=True)
    return m,l,p.astype(bf16)
DQ=256
def diag_fwd(place_ref, klen_ref, q_ref,k_ref,v_ref,o_ref,l_ref):
    hm=head_masks(); klen=klen_ref[0]
    q=q_ref[...]*jnp.asarray(0.125,bf16)
    vt=v_ref[...].T
    z=jnp.zeros((),bf16)
    tiles=[(qi,h) for qi in range(SP//DQ) for h in range(2)]
    kpos=lax.broadcasted_iota(jnp.int32,(SP,1),0)
    low=jnp.where(kpos<klen,kpos,SP)
    def scores(t):
        qi,h=t; n=(qi+1)*DQ
        ok=(qi*DQ+lax.broadcasted_iota(jnp.int32,(n,DQ),1))>=low[:n]
        return jnp.where(ok,tdot(k_ref[:n],jnp.where(hm[h],q[qi*DQ:n],z)),NEG)
    def finish(t,m,l,p):
        qi,h=t; n=(qi+1)*DQ; sl=slice(qi*DQ,n)
        acc=dot(vt[h*64:(h+1)*64,:n],p)
        o_ref[0,h*64:(h+1)*64,sl]=acc*(1.0/l)
        l_ref[0,h:h+1,sl]=m+jnp.log(l)
    pipeline(tiles,scores,softmax_t,finish)
def pipeline(tiles,scores,mid,finish,depth=2):
    s=scores(tiles[0]); pend=None
    for i,t in enumerate(tiles):
        sn=scores(tiles[i+1]) if i+1<len(tiles) else None
        r=mid(s) if not isinstance(s,tuple) else mid(t,*s)
        if depth==2:
            if pend: finish(*pend)
            pend=(t,)+r
        else: finish(t,*r)
        s=sn
    if pend: finish(*pend)
CQ=512
def cross_fwd(place_ref, klen_ref, q_ref,k_ref,v_ref,od_ref,ld_ref,o_ref,l_ref):
    hm=head_masks()
    @pl.when(place_ref[0]==1)
    def _():
        q=q_ref[...]*jnp.asarray(0.125,bf16)
        vt=v_ref[...].T
        z=jnp.zeros((),bf16)
        tiles=[(qi,h) for qi in range(SP//CQ) for h in range(2)]
        res={}
        def scores(t):
            qi,h=t
            return tdot(k_ref[...],jnp.where(hm[h],q[qi*CQ:(qi+1)*CQ],z))
        def finish(t,m,l,p):
            qi,h=t; sl=slice(qi*CQ,(qi+1)*CQ)
            acc=dot(vt[h*64:(h+1)*64],p)
            ld=ld_ref[0,h:h+1,sl]
            lx=m+jnp.log(l)
            mx=jnp.maximum(ld,lx)
            ed=jnp.exp(ld-mx); ex=jnp.exp(lx-mx); tot=ed+ex
            l_ref[0,h:h+1,sl]=mx+jnp.log(tot)
            res[t]=od_ref[0,h*64:(h+1)*64,sl]*(ed/tot)+acc*(ex/(tot*l))
            if h==1: o_ref[sl]=jnp.concatenate([res[(qi,0)],res[(qi,1)]],0).T.astype(bf16)
        pipeline(tiles,scores,softmax_t,finish)
    @pl.when(place_ref[0]==0)
    def _():
        o_ref[...]=od_ref[0].T.astype(bf16)
        l_ref[...]=ld_ref[...]
KB=256
def bwd_prep(q_ref,do_ref,hm):
    q=q_ref[...]*jnp.asarray(0.125,bf16)
    z=jnp.zeros((),bf16)
    do=do_ref[...]
    return [jnp.where(hm[h],q,z) for h in range(2)],[jnp.where(hm[h],do,z) for h in range(2)]
def bwd_tiles(k_ref,v_ref,qm,dm,lrow,drow,put,dqt,start,mask,KB):
    tiles=[(kb,h) for kb in range(SP//KB) for h in range(2)]
    acc={}
    kts={}
    def scores(t):
        kb,h=t; ks=slice(kb*KB,(kb+1)*KB); q0=start(kb)
        return tdot(k_ref[ks],qm[h][q0:]),tdot(v_ref[ks],dm[h][q0:])
    def mid(t,s,dp):
        kb,h=t; q0=start(kb)
        p=jnp.exp(s-lrow(h)[:,q0:])
        if mask is not None: p=jnp.where(mask(kb),p,0.0)
        ds=p*(dp-drow(h)[:,q0:])
        return p.astype(bf16),ds.astype(bf16)
    def finish(t,p,ds):
        kb,h=t; ks=slice(kb*KB,(kb+1)*KB); q0=start(kb)
        if h==0: kts[kb]=k_ref[ks].T
        a=dot(p,dm[h][q0:]); b=dot(ds,qm[h][q0:])
        if h==0: acc[kb]=(a,b)
        else:
            put(ks,(acc[kb][1]+b).astype(bf16),(acc[kb][0]+a).astype(bf16))
        c=dot(kts[kb][h*64:(h+1)*64],ds)
        if kb==0: dqt[h*64:(h+1)*64]=c
        else: dqt[h*64:(h+1)*64,q0:]+=c
    pipeline(tiles,scores,mid,finish)
def cross_bwd(place_ref, klen_ref, q_ref,k_ref,v_ref,do_ref,o_ref,l_ref,dq_ref,dkv_ref,dl_ref,dqt):
    hm=head_masks()
    prod=do_ref[...].astype(f32)*o_ref[...].astype(f32)
    t=prod.T
    dl_ref[0,0:1]=jnp.sum(t[:64],0,keepdims=True); dl_ref[0,1:2]=jnp.sum(t[64:],0,keepdims=True)
    @pl.when(place_ref[0]==1)
    def _():
        def put(ks,dk,dv):
            dkv_ref[0,ks]=dk
            dkv_ref[1,ks]=dv
        qm,dm=bwd_prep(q_ref,do_ref,hm)
        bwd_tiles(k_ref,v_ref,qm,dm,lambda h:l_ref[0,h:h+1],lambda h:dl_ref[0,h:h+1],put,dqt,lambda kb:0,None,512)
        dq_ref[...]=dqt[...].T*0.125
    @pl.when(place_ref[0]==0)
    def _():
        dkv_ref[...]=jnp.zeros_like(dkv_ref); dq_ref[...]=jnp.zeros_like(dq_ref)
def diag_bwd(place_ref, klen_ref, q_ref,k_ref,v_ref,do_ref,l_ref,dl_ref,dqx_ref,out_ref,dqt):
    hm=head_masks(); klen=klen_ref[0]
    qm,dm=bwd_prep(q_ref,do_ref,hm)
    def put(ks,dk,dv):
        out_ref[1,ks]=dk
        out_ref[2,ks]=dv
    kpos=lax.broadcasted_iota(jnp.int32,(SP,1),0)
    low=jnp.where(kpos<klen,kpos,SP)
    def mask(kb):
        q0=kb*KB
        return q0+lax.broadcasted_iota(jnp.int32,(KB,SP-q0),1)>=low[q0:q0+KB]
    bwd_tiles(k_ref,v_ref,qm,dm,lambda h:l_ref[0,h:h+1],lambda h:dl_ref[0,h:h+1],put,dqt,lambda kb:kb*KB,mask,KB)
    out_ref[0]=(dqt[...].T*0.125+dqx_ref[...]).astype(bf16)
S=jax.ShapeDtypeStruct
def col(base,rows=SP): return pl.BlockSpec((rows,128),lambda j,*_:(0,base+j))
def cols(n,base): return pl.BlockSpec((n,SP,128),lambda j,*_:(0,0,base+j))
def row(base): return pl.BlockSpec((1,8,SP),lambda j,*_:(base+j,0,0))
ROW=row(0)
def call(fn,place,klen,ins,in_specs,outs,out_specs,scratch=(),pairs=NP,into=None,after=(),flops=0,trans=0):
    into=into or {}
    extra=list(into.items())
    n=2+len(ins)
    m=len(extra)
    skip=n+m+len(after)
    def kern(*refs): return fn(*refs[:n],*refs[skip:])
    specs=list(in_specs)+[pl.BlockSpec(memory_space=pl.ANY)]*(m+len(after))
    return pl.pallas_call(kern,
        grid_spec=pltpu.PrefetchScalarGridSpec(num_scalar_prefetch=2,grid=(pairs,),in_specs=specs,out_specs=out_specs,scratch_shapes=list(scratch)),
        out_shape=outs,
        input_output_aliases={n+i:o for i,(o,_) in enumerate(extra)},
        compiler_params=pltpu.CompilerParams(vmem_limit_bytes=50*1024*1024,dimension_semantics=("arbitrary",)),
        cost_estimate=pl.CostEstimate(flops=flops,bytes_accessed=pairs*10**4,transcendentals=trans),
        name=fn.__name__,
    )(place,klen,*ins,*[x for _,x in extra],*after)


BITS = {"c": ("dp", 1), "y": ("dp", 2), "u": ("dp", 4), "v": ("dp", 8), "x": ("blk", 1)}
LOW = "xyuv"
ORDERS = ("xyuv", "yuxv", "uxyv")
RB = 48


def swap(a, bit):
    axis, step = BITS[bit] if isinstance(bit, str) else ("dp", bit)
    return lax.ppermute(a, axis, [(i, i ^ step) for i in range(lax.axis_size(axis))])


def outer_steps():
    size = lax.axis_size("dp")
    return [1 << k for k in range(4, 16) if (1 << k) < size]


def my_id():
    place = 0
    for bit in "c" + LOW:
        axis, step = BITS[bit]
        place = 2 * place + (lax.axis_index(axis) // step) % 2
    return place.astype(jnp.int32).reshape(1)


def add(a, b):
    return (a.astype(f32) + b.astype(f32)).astype(bf16)


def core_step(keeps, sends):
    state = []
    for keep, send in zip(keeps, sends):
        a = add(keep, swap(send, "c"))
        state.append((a.reshape((2,) * 4 + a.shape[1:]), LOW))
    return state


def low_step(state, step, after=None):
    waiting = []
    for (a, bits), order in zip(state, ORDERS):
        at = bits.index(order[step])
        keep, send = lax.index_in_dim(a, 0, at, False), lax.index_in_dim(a, 1, at, False)
        waiting.append((keep, swap(send, order[step]), bits.replace(order[step], "")))
    if after is not None:
        flat = lambda a: a.reshape(-1, a.shape[-1])
        sums = sum_kernel([(flat(keep), flat(got)) for keep, got, _ in waiting], after, "step_sum")
        return [(a.reshape(keep.shape), bits) for a, (keep, _, bits) in zip(sums, waiting)]
    return [(add(keep, got), bits) for keep, got, bits in waiting]


def sum_kernel(pairs, after, name):
    n = len(pairs)

    def kern(*refs):
        for i in range(n):
            a, b = refs[i][...], refs[n + i][...]
            refs[i - n][...] = (a.astype(f32) + b.astype(f32)).astype(a.dtype)

    vmem = pl.BlockSpec(memory_space=pltpu.VMEM)
    return pl.pallas_call(
        kern,
        in_specs=[vmem] * (2 * n) + [pl.BlockSpec(memory_space=pl.ANY)] * len(after),
        out_specs=[vmem] * n,
        out_shape=[S(a.shape, a.dtype) for a, _ in pairs],
        name=name,
    )(*[a for a, _ in pairs], *[b for _, b in pairs], *after)


def last_step(state, after):
    keep = jnp.stack([a[0] for a, _ in state])
    got = swap(jnp.stack([a[1] for a, _ in state]), ORDERS[0][3])
    (total,) = sum_kernel([(keep, got)], after, "last_sum")
    for step in outer_steps():
        total = add(total, swap(total, step))
    return total


def outer_sum(blocks):
    for step in outer_steps():
        blocks = [add(a, swap(a, step)) for a in blocks]
    return blocks


def reduce_parts(keeps, sends):
    state = core_step(keeps, sends)
    for step in range(4):
        state = low_step(state, step)
    return outer_sum([a for a, _ in state])


def spread_parts(blocks):
    state = [a[None] for a in blocks]
    for step in (3, 2, 1, 0):
        state = [jnp.concatenate([a, swap(a, o[step])], 0) for a, o in zip(state, ORDERS)]
    return state, [swap(a, "c") for a in state]


def sum_small(a):
    for bit in "c" + LOW:
        a = a + swap(a, bit)
    for step in outer_steps():
        a = a + swap(a, step)
    return a


def low_index(p, order):
    r = 0
    for bit in order:
        r = 2 * r + (p // (1 << (3 - LOW.index(bit)))) % 2
    return r


def gather_all(blocks):
    a = lax.all_gather(blocks, ("dp", "blk"), axis=0, tiled=False)
    return a[:32]


def device_of(block):
    c, x, y, u, v = [(block // (1 << (4 - i))) % 2 for i in range(5)]
    return (v * 8 + u * 4 + y * 2 + c) * 2 + x


def unpack_early(gathered):
    rows = 2

    def kern(*refs):
        ins, (fc, proj, out) = refs[: 2 * rows], refs[2 * rows :]
        for core in range(2):
            for r in range(rows):
                a = ins[core * rows + r]
                at = slice(r * RB, (r + 1) * RB)
                fc[at, core * 1536 : core * 1536 + 1152] = a[0, 0].astype(f32)
                fc[at, core * 1536 + 1152 : (core + 1) * 1536] = a[0, 1, :, :384].astype(f32)
                proj[core, 2 * r * RB : (2 * r + 1) * RB] = a[0, 1, :, 384:].astype(f32)
                proj[core, (2 * r + 1) * RB : (2 * r + 2) * RB] = a[0, 2, :, :768].astype(f32)
                out[at, core * 384 : (core + 1) * 384] = a[0, 2, :, 768:].astype(f32)

    block = (1,) + gathered.shape[1:]
    return pl.pallas_call(
        kern,
        grid=(16 // rows,),
        in_specs=[
            pl.BlockSpec(block, lambda b, core=core, r=r: (device_of(core * 16 + b * rows + r), 0, 0, 0))
            for core in range(2) for r in range(rows)
        ],
        out_specs=[
            pl.BlockSpec((rows * RB, 4 * W), lambda b: (b, 0)),
            pl.BlockSpec((2, 2 * rows * RB, W), lambda b: (0, b, 0)),
            pl.BlockSpec((rows * RB, W), lambda b: (b, 0)),
        ],
        out_shape=[S((W, 4 * W), f32), S((2, 2 * W, W), f32), S((W, W), f32)],
        compiler_params=pltpu.CompilerParams(vmem_limit_bytes=56 * 1024 * 1024),
        cost_estimate=pl.CostEstimate(flops=0, bytes_accessed=3 * gathered.size * 2, transcendentals=0),
        name="unpack_early",
    )(*[gathered] * (2 * rows))


def unpack_late(me, mine, other, after):
    n = len(mine)
    rows = 4
    lanes = mine[0].shape[2]

    def kern(me_ref, *refs):
        own, far, out = refs[:n], refs[n : 2 * n], refs[-1]
        core, low = me_ref[0] // 16, me_ref[0] % 16
        step = pl.program_id(0)

        def fill(half, ins):
            for r in range(rows):
                place = (step * rows + r) ^ low
                for part in range(n):
                    at = (half * n + part) * lanes
                    out[r * RB : (r + 1) * RB, at : at + lanes] = ins[part][low_index(place, ORDERS[part])].astype(f32)

        for half in range(2):
            @pl.when(core == half)
            def _():
                fill(half, own)

            @pl.when(core != half)
            def _():
                fill(half, far)

    whole = pl.BlockSpec(mine[0].shape, lambda b, *_: (0, 0, 0))
    return pl.pallas_call(
        kern,
        grid_spec=pltpu.PrefetchScalarGridSpec(
            num_scalar_prefetch=1, grid=(16 // rows,), in_specs=[whole] * (2 * n) + [pl.BlockSpec(memory_space=pl.ANY)] * len(after),
            out_specs=pl.BlockSpec((rows * RB, 3 * W), lambda b, *_: (b, 0)),
        ),
        out_shape=S((W, 3 * W), f32),
        compiler_params=pltpu.CompilerParams(vmem_limit_bytes=56 * 1024 * 1024),
        cost_estimate=pl.CostEstimate(flops=0, bytes_accessed=10**7, transcendentals=0),
        name="unpack_late",
    )(me, *mine, *other, *after)


MR = 256
QR = 512
FC = 1536
C0 = 0.7978845608028654
C1 = C0 * 0.044715


def rowmean(a):
    return jnp.sum(a, -1, keepdims=True) * (1.0 / W)


def block_kernel(
    klen_ref, x_ref, att_ref, up_ref, d_act_ref, w_out_ref, w_fc_ref, w_proj_ref, b_out_ref, gain_ref, shift_ref, b_proj_ref, b_fc_ref,
    y_ref, act_ref, pre_ref, mid_ref, gatt_ref, do_ref, sums_ref, bsum_ref,
):
    step = pl.program_id(0)

    @pl.when(step == 0)
    def _():
        sums_ref[...] = jnp.zeros_like(sums_ref)
        bsum_ref[...] = jnp.zeros_like(bsum_ref)

    up = up_ref[...].astype(f32)
    branch_att = dot(att_ref[...], w_out_ref[...]) + b_out_ref[...][None]
    middle = x_ref[...].astype(f32) + branch_att
    centered = middle - rowmean(middle)
    inv = lax.rsqrt(rowmean(centered * centered) + EPS)
    x_hat = centered * inv
    gain = gain_ref[...][None]
    normed = (x_hat * gain + shift_ref[...][None]).astype(bf16)
    mid_ref[...] = normed
    chunks = range(4 * W // FC)
    sl = lambda c: slice(c * FC, (c + 1) * FC)

    def first(c):
        return dot(normed, w_fc_ref[:, sl(c)])

    mlp = None
    back = None
    ahead = first(0)
    for c in chunks:
        u = ahead
        if c + 1 < len(chunks):
            ahead = first(c + 1)
        u = u + b_fc_ref[sl(c)][None]
        v = u * u
        h = 0.5 + 0.5 * jnp.tanh(u * (C0 + C1 * v))
        z = (u * h).astype(bf16)
        d = d_act_ref[:, sl(c)].astype(f32) * (h + (u * (2 * C0 + 6 * C1 * v)) * (h * (1.0 - h)))
        bsum_ref[0:1, sl(c)] += jnp.sum(d, 0, keepdims=True)
        d = d.astype(bf16)
        act_ref[:, sl(c)] = z
        pre_ref[:, sl(c)] = d
        a = dot(z, w_proj_ref[sl(c)])
        b = tdot(d, w_fc_ref[:, sl(c)])
        mlp = a if mlp is None else mlp + a
        back = b if back is None else back + b
    branch_mlp = mlp + b_proj_ref[...][None]
    out = middle + branch_mlp
    y_ref[...] = out.astype(bf16)
    scaled = back * gain
    grad = up + inv * (scaled - rowmean(scaled) - x_hat * rowmean(scaled * x_hat))
    gatt = grad.astype(bf16)
    gatt_ref[...] = gatt
    do_ref[...] = tdot(gatt, w_out_ref[...]).astype(bf16)
    valid = step * MR + lax.broadcasted_iota(jnp.int32, (MR, 1), 0) < klen_ref[0]
    total = lambda a: jnp.sum(a, 0, keepdims=True)
    kept = lambda a: total(jnp.where(valid, a * a, 0.0))
    sums_ref[...] += jnp.concatenate(
        [total(back * x_hat), total(back), total(grad), total(up), kept(out), kept(branch_att), kept(branch_mlp),
         jnp.zeros((1, W), f32)], 0,
    )


def block_call(klen, x, att, up, d_act, w_out, w_fc, w_proj, b_out, gain, shift, b_proj, b_fc):
    once = pl.Buffered(1)
    rows = lambda width: pl.BlockSpec((MR, width), lambda i, *_: (i, 0))
    whole = lambda shape: pl.BlockSpec(shape, lambda i, *_: (0, 0), pipeline_mode=once)
    const = lambda shape: pl.BlockSpec(shape, lambda i, *_: (0, 0))
    line = lambda size: pl.BlockSpec((size,), lambda i, *_: (0,))
    return pl.pallas_call(
        block_kernel,
        grid_spec=pltpu.PrefetchScalarGridSpec(
            num_scalar_prefetch=1,
            grid=(SP // MR,),
            in_specs=[rows(W)] * 3 + [rows(4 * W), whole((W, W)), whole((W, 4 * W)), whole((4 * W, W)), line(W), line(W), line(W), line(W), line(4 * W)],
            out_specs=[rows(W), rows(4 * W), rows(4 * W), rows(W), rows(W), rows(W), const((8, W)), const((1, 4 * W))],
        ),
        out_shape=[
            S((SP, W), bf16), S((SP, 4 * W), bf16), S((SP, 4 * W), bf16), S((SP, W), bf16),
            S((SP, W), bf16), S((SP, W), bf16), S((8, W), f32), S((1, 4 * W), f32),
        ],
        compiler_params=pltpu.CompilerParams(vmem_limit_bytes=56 * 1024 * 1024),
        cost_estimate=pl.CostEstimate(flops=17 * 10**9, bytes_accessed=41 * 10**6, transcendentals=3 * 10**6),
        name="block_mlp",
    )(klen, x, att, up, d_act, w_out, w_fc, w_proj, b_out, gain, shift, b_proj, b_fc)


def grads_kernel(me_ref, mid_ref, pre_ref, act_ref, up_ref, att_ref, gatt_ref, k0, k1, k2, s0, s1, s2, mid_t):
    step = pl.program_id(0)
    core, low = me_ref[0] // 16, me_ref[0] % 16

    @pl.when(step == 0)
    def _():
        mid_t[...] = mid_ref[...].T

    def by_core(half, fill, keep, send):
        @pl.when(half == core)
        def _():
            fill(*keep)

        @pl.when(half != core)
        def _():
            fill(*send)

    @pl.when(step < 4)
    def _():
        tile = dot(mid_t[...], pre_ref[...]).astype(bf16)

        def left(one):
            for i in range(16):
                one[i ^ low, :, :768] = tile[i * RB : (i + 1) * RB]

        def right(one, two):
            for i in range(16):
                one[i ^ low, :, 768:] = tile[i * RB : (i + 1) * RB, :384]
                two[i ^ low, :, :384] = tile[i * RB : (i + 1) * RB, 384:]

        @pl.when(step % 2 == 0)
        def _():
            by_core(step // 2, left, (k0,), (s0,))

        @pl.when(step % 2 == 1)
        def _():
            by_core(step // 2, right, (k0, k1), (s0, s1))

    @pl.when((step >= 4) & (step < 8))
    def _():
        tile = rows_dot(act_ref[...], up_ref[...]).astype(bf16)
        first = (step - 4) % 2 * 8

        def fill(one, two):
            for i in range(8):
                at = (first + i) ^ low
                one[at, :, 384:] = tile[2 * i * RB : (2 * i + 1) * RB]
                two[at, :, :768] = tile[(2 * i + 1) * RB : (2 * i + 2) * RB]

        by_core((step - 4) // 2, fill, (k1, k2), (s1, s2))

    @pl.when(step == 8)
    def _():
        tile = rows_dot(att_ref[...], gatt_ref[...]).astype(bf16)

        def fill(one, two):
            for i in range(16):
                one[i ^ low, :, 768:] = tile[i * RB : (i + 1) * RB, :384]
                two[i ^ low, :, 768:] = tile[i * RB : (i + 1) * RB, 384:]

        by_core(0, fill, (k2, s2), (s2, k2))


def grads_call(me, mid, pre, act, up, att, gatt):
    clip = lambda i, lo, hi: jnp.clip(i, lo, hi) - lo
    whole = pl.BlockSpec((SP, W), lambda i, *_: (0, 0))
    part = pl.BlockSpec((16, RB, 1152), lambda i, *_: (0, 0, 0))
    res = pl.pallas_call(
        grads_kernel,
        grid_spec=pltpu.PrefetchScalarGridSpec(
            num_scalar_prefetch=1,
            grid=(9,),
            in_specs=[
                whole,
                pl.BlockSpec((SP, W), lambda i, *_: (0, clip(i, 0, 3))),
                pl.BlockSpec((SP, W), lambda i, *_: (0, clip(i, 4, 7))),
                whole,
                whole,
                whole,
            ],
            out_specs=[part] * 6,
            scratch_shapes=[pltpu.VMEM((W, SP), bf16)],
        ),
        out_shape=[S((16, RB, 1152), bf16)] * 6,
        compiler_params=pltpu.CompilerParams(vmem_limit_bytes=56 * 1024 * 1024),
        cost_estimate=pl.CostEstimate(flops=11 * 10**9, bytes_accessed=30 * 10**6, transcendentals=0),
        name="block_grads",
    )(me, mid, pre, act, up, att, gatt)
    return res[:3], res[3:]


def late_kernel(me_ref, a_ref, ar_ref, d_ref, dr_ref, k0, k1, k2, s0, s1, s2, a_t, ar_t):
    step = pl.program_id(0)
    core, low = me_ref[0] // 16, me_ref[0] % 16

    def put(keep, send, tile):
        def fill(ref):
            for i in range(16):
                ref[i ^ low] = tile[i * RB : (i + 1) * RB]

        return lambda half: (
            pl.when(core == half)(lambda: fill(keep)),
            pl.when(core != half)(lambda: fill(send)),
        )

    @pl.when(step == 0)
    def _():
        a_t[...] = a_ref[...].T
        ar_t[...] = ar_ref[...].T
        tile = dot(a_t[...], d_ref[0]).astype(bf16)
        put(k0, s0, tile[:, :384])(0)
        put(k1, s1, tile[:, 384:])(0)

    @pl.when(step == 1)
    def _():
        tile = (dot(a_t[...], d_ref[0]) + dot(ar_t[...], dr_ref[0])).astype(bf16)
        put(k2, s2, tile[:, :384])(0)
        put(k0, s0, tile[:, 384:])(1)

    @pl.when(step == 2)
    def _():
        tile = (dot(a_t[...], d_ref[0]) + dot(ar_t[...], dr_ref[0])).astype(bf16)
        put(k1, s1, tile[:, :384])(1)
        put(k2, s2, tile[:, 384:])(1)


def late_call(me, a, ar, d, dr, after):
    def kern(*refs):
        return late_kernel(*refs[:5], *refs[5 + len(after) :])

    whole = pl.BlockSpec((SP, W), lambda i, *_: (0, 0))
    part = pl.BlockSpec((16, RB, 384), lambda i, *_: (0, 0, 0))
    res = pl.pallas_call(
        kern,
        grid_spec=pltpu.PrefetchScalarGridSpec(
            num_scalar_prefetch=1,
            grid=(3,),
            in_specs=[
                whole,
                whole,
                pl.BlockSpec((1, SP, W), lambda i, *_: (i, 0, 0)),
                pl.BlockSpec((1, SP, W), lambda i, *_: (jnp.maximum(i - 1, 0), 0, 0)),
            ] + [pl.BlockSpec(memory_space=pl.ANY)] * len(after),
            out_specs=[part] * 6,
            scratch_shapes=[pltpu.VMEM((W, SP), bf16)] * 2,
        ),
        out_shape=[S((16, RB, 384), bf16)] * 6,
        compiler_params=pltpu.CompilerParams(vmem_limit_bytes=56 * 1024 * 1024),
        cost_estimate=pl.CostEstimate(flops=6 * 10**9, bytes_accessed=14 * 10**6, transcendentals=0),
        name="late_grads",
    )(me, a, ar, d, dr, *after)
    return res[:3], res[3:]


def qkv_call(x, w_qkv, b_query, b_value, gain, shift, n, after, name):
    def kern(x_ref, w_ref, bq_ref, bv_ref, gain_ref, shift_ref, *refs):
        a_ref, out_ref = refs[len(after) :]
        a = (norm_one(x_ref)[0] * gain_ref[...][None] + shift_ref[...][None]).astype(bf16)
        a_ref[...] = a
        if n == 3:
            out_ref[:, :W] = (dot(a, w_ref[:, :W]) + bq_ref[...][None]).astype(bf16)
        out_ref[:, (n - 2) * W : (n - 1) * W] = dot(a, w_ref[:, W : 2 * W]).astype(bf16)
        out_ref[:, (n - 1) * W :] = (dot(a, w_ref[:, 2 * W :]) + bv_ref[...][None]).astype(bf16)

    rows = lambda width: pl.BlockSpec((QR, width), lambda i: (i, 0))
    return pl.pallas_call(
        kern,
        grid=(SP // QR,),
        in_specs=[
            rows(W),
            pl.BlockSpec((W, 3 * W), lambda i: (0, 0)),
        ] + [pl.BlockSpec((W,), lambda i: (0,))] * 4 + [pl.BlockSpec(memory_space=pl.ANY)] * len(after),
        out_specs=[rows(W), rows(n * W)],
        out_shape=[S((SP, W), bf16), S((SP, n * W), bf16)],
        compiler_params=pltpu.CompilerParams(vmem_limit_bytes=56 * 1024 * 1024),
        cost_estimate=pl.CostEstimate(flops=n * 12 * 10**8, bytes_accessed=10**7, transcendentals=0),
        name=name,
    )(x, w_qkv, b_query, b_value, gain, shift, *after)


def norm_one(x_ref):
    x = x_ref[...].astype(f32)
    centered = x - rowmean(x)
    inv = lax.rsqrt(rowmean(centered * centered) + EPS)
    return centered * inv, inv


def input_kernel(x_ref, d_ref, w_ref, gain_ref, *refs):
    n = d_ref.shape[0]
    sums_ref = refs[-1]

    @pl.when(pl.program_id(0) == 0)
    def _():
        sums_ref[...] = jnp.zeros_like(sums_ref)

    x_hat, inv = norm_one(x_ref)
    part = None
    for i in range(n):
        a = tdot(d_ref[i], w_ref[:, (3 - n + i) * W : (4 - n + i) * W])
        part = a if part is None else part + a
    total = lambda a: jnp.sum(a.astype(f32), 0, keepdims=True)
    first = total(d_ref[0]) if n == 3 else jnp.zeros((1, W), f32)
    sums_ref[...] += jnp.concatenate(
        [first, total(d_ref[n - 1]), total(part * x_hat), total(part), jnp.zeros((4, W), f32)], 0
    )
    if n == 2:
        refs[0][...] = part.astype(bf16)
    else:
        returned_ref, gatt_ref = refs[:2]
        scaled = (part + returned_ref[0].astype(f32)) * gain_ref[...][None]
        inner = scaled - rowmean(scaled) - x_hat * rowmean(scaled * x_hat)
        refs[-2][...] = (gatt_ref[...].astype(f32) + inv * inner).astype(bf16)


def input_call(side, x, d, w_qkv, gain, extra, after, name):
    n = d.shape[0]
    rows = pl.BlockSpec((QR, W), lambda i, *_: (i, 0))
    more = [pl.BlockSpec((1, QR, W), lambda i, side_ref: (side_ref[0], i, 0)), rows] if extra else []
    skip = 5 + len(extra)

    def kern(*refs):
        return input_kernel(*refs[1:skip], *refs[skip + len(after) :])

    return pl.pallas_call(
        kern,
        grid_spec=pltpu.PrefetchScalarGridSpec(
            num_scalar_prefetch=1,
            grid=(SP // QR,),
            in_specs=[
                rows,
                pl.BlockSpec((n, QR, W), lambda i, *_: (0, i, 0)),
                pl.BlockSpec((W, 3 * W), lambda i, *_: (0, 0)),
                pl.BlockSpec((W,), lambda i, *_: (0,)),
            ] + more + [pl.BlockSpec(memory_space=pl.ANY)] * len(after),
            out_specs=[rows, pl.BlockSpec((8, W), lambda i, *_: (0, 0))],
        ),
        out_shape=[S((SP, W), bf16), S((8, W), f32)],
        compiler_params=pltpu.CompilerParams(vmem_limit_bytes=56 * 1024 * 1024),
        cost_estimate=pl.CostEstimate(flops=n * 12 * 10**8, bytes_accessed=10**7, transcendentals=0),
        name=name,
    )(side, x, d, w_qkv, gain, *extra, *after)


def swap_spans(x):
    return lax.ppermute(x, "blk", [(0, 1), (1, 0)])


def rows_dot(left, right):
    return lax.dot_general(left, right, (((0,), (0,)), ((), ())), preferred_element_type=f32)


def body(
    inputs, cotangent, lengths, groups, flip,
    w_qkv, b_query, b_value, w_out, b_out, gain_one, shift_one, gain_two, shift_two,
    w_fc, b_fc, w_proj, b_proj,
):
    place = jnp.bitwise_xor(lax.axis_index("blk"), flip[0])
    klen = jnp.minimum(lengths[0] - place * SP, SP)
    place_s = place.reshape(1).astype(jnp.int32)
    klen_s = klen.reshape(1).astype(jnp.int32)
    x_b = inputs[0, 0]
    up_b = cotangent[0, 0]
    xr_b = swap_spans(x_b)

    normed, qkv = qkv_call(x_b, w_qkv, b_query, b_value, gain_one, shift_one, 3, (), "own_qkv")
    c = col(0)
    tall = pl.BlockSpec((1, 128, SP), lambda j, *_: (j, 0, 0))
    od, ld = call(
        diag_fwd, place_s, klen_s, (qkv, qkv, qkv), [c, col(6), col(12)],
        [S((NP, 128, SP), f32), S((NP, 8, SP), f32)], [tall, ROW],
    )

    d_act = tdot(up_b, w_proj).astype(bf16)
    normed_r, kvr = qkv_call(xr_b, w_qkv, b_query, b_value, gain_one, shift_one, 2, (ld, d_act), "other_kv")
    attended, lse = call(
        cross_fwd, place_s, klen_s, (qkv, kvr, kvr, od, ld), [c, c, col(6), tall, ROW],
        [S((SP, W), bf16), S((NP, 8, SP), f32)], [c, ROW],
    )

    outputs, activ, grad_pre, normed_two, grad_att, grad_attended, sums, grad_b_fc = block_call(
        klen_s, x_b, attended, up_b, d_act, w_out, w_fc, w_proj, b_out, gain_two, shift_two, b_proj, b_fc
    )
    me = my_id()
    keeps, sends = grads_call(me, normed_two, grad_pre, activ, up_b, attended, grad_att)
    acc = pltpu.VMEM((128, SP), f32)
    flops = 8 * 10**9
    dqx = dkvr = delta = dqkv = None

    def cross_piece(at, pairs, dep):
        nonlocal dqx, dkvr, delta
        dqx, dkvr, delta = call(
            cross_bwd, place_s, klen_s, (qkv, kvr, kvr, grad_attended, attended, lse),
            [col(at), col(at), col(6 + at), col(at), col(at), row(at)],
            [S((SP, W), f32), S((2, SP, W), bf16), S((NP, 8, SP), f32)],
            [col(at), cols(2, at), row(at)], [acc], pairs=pairs,
            into={0: dqx, 1: dkvr, 2: delta} if at else None, after=dep, flops=flops * pairs,
        )

    def diag_piece(at, pairs, dep):
        nonlocal dqkv
        (dqkv,) = call(
            diag_bwd, place_s, klen_s, (qkv, qkv, qkv, grad_attended, lse, delta, dqx),
            [col(at), col(6 + at), col(12 + at), col(at), row(at), row(at), col(at)],
            [S((3, SP, W), bf16)], [cols(3, at)], [acc], pairs=pairs,
            into={0: dqkv} if at else None, after=dep, flops=flops * pairs // 2,
        )

    arrays = lambda state: [a for a, _ in state]
    gain = gain_one
    side = (1 - lax.axis_index("blk")).astype(jnp.int32).reshape(1)
    cross_piece(0, 1, keeps)
    state = core_step(keeps, sends)
    cross_piece(1, 3, arrays(state))
    state = low_step(state, 0)
    cross_piece(4, 2, arrays(state))
    part_r, sums_r = input_call(side, xr_b, dkvr, w_qkv, gain, (), (), "other_span")
    returned = lax.all_gather(part_r, "blk", axis=0, tiled=False)
    state = low_step(state, 1)
    state = low_step(state, 2)
    diag_piece(0, 3, arrays(state) + [part_r])
    early_sum = last_step(state, [dqkv])
    diag_piece(3, 3, [early_sum])
    early = unpack_early(gather_all(early_sum))

    state = core_step(*late_call(me, normed, normed_r, dqkv, dkvr, []))
    input_grad, sums_o = input_call(
        side, x_b, dqkv, w_qkv, gain, (returned, grad_att), arrays(state), "input_grad"
    )
    state = low_step(state, 0, [sums_o])
    state = low_step(state, 1)
    state = low_step(state, 2)
    state = low_step(state, 3)
    late = unpack_late(me, *spread_parts(outer_sum(arrays(state))), [early[0]])

    member = (groups[0] == jnp.arange(2, dtype=jnp.int32)).astype(f32)
    squares = jnp.concatenate([jnp.sum(sums[4:7], 1), klen.astype(f32)[None]])
    sums_one = sums_o + sums_r
    small = jnp.concatenate([
        sums_one[0], sums_one[1], sums[2], sums_one[2], sums_one[3], sums[0], sums[1], grad_b_fc[0], sums[3],
        (member[:, None] * squares[None, :]).reshape(-1), jnp.zeros((1016,), f32),
    ])
    small = sum_small(small.reshape(80, 128)).reshape(-1)
    sizes = [W] * 7 + [4 * W, W]
    pieces = []
    at = 0
    for size in sizes:
        pieces.append(small[at : at + size])
        at += size
    table = small[at : at + 8].reshape(2, 4)
    group_rms = jnp.sqrt(table[:, :3] / (table[:, 3:] * W))
    g_bq, g_bv, g_bo, g_g1, g_s1, g_g2, g_s2, g_bfc, g_bp = pieces
    return (
        outputs[None, None], input_grad[None, None], late, g_bq, g_bv, early[2], g_bo, g_g1, g_s1, g_g2, g_s2,
        early[0], g_bfc, early[1].reshape(4 * W, W), g_bp, group_rms,
    )


def solution(mesh):
    span = P("dp", "blk", None, None)
    return jax.shard_map(
        body,
        mesh=mesh,
        in_specs=(span, span, P("dp"), P("dp"), P("dp")) + (P(),) * 13,
        out_specs=(span, span) + (P(),) * 14,
        check_vma=False,
    )
```

```python
import jax
import jax.numpy as jnp
from jax import lax
from jax.experimental import pallas as pl
from jax.experimental.pallas import tpu as pltpu
from jax.sharding import PartitionSpec as P

SP = 1024
W = 768
NP = 6
EPS = 1e-05
NEG=-1e30
f32=jnp.float32; bf16=jnp.bfloat16
def tdot(a,b): return lax.dot_general(a,b,(((1,),(1,)),((),())),preferred_element_type=f32)
def dot(a,b): return jnp.dot(a,b,preferred_element_type=f32)
def head_masks():
    lane=lax.broadcasted_iota(jnp.int32,(1,128),1)
    return [lane<64, lane>=64]
def softmax_t(s):
    m=jnp.max(s,0,keepdims=True)
    p=jnp.exp(s-m)
    l=jnp.sum(p,0,keepdims=True)
    return m,l,p.astype(bf16)
DQ=256
def diag_fwd(place_ref, klen_ref, q_ref,k_ref,v_ref,o_ref,l_ref):
    hm=head_masks(); klen=klen_ref[0]
    q=q_ref[...]*jnp.asarray(0.125,bf16)
    vt=v_ref[...].T
    z=jnp.zeros((),bf16)
    tiles=[(qi,h) for qi in range(SP//DQ) for h in range(2)]
    kpos=lax.broadcasted_iota(jnp.int32,(SP,1),0)
    low=jnp.where(kpos<klen,kpos,SP)
    def scores(t):
        qi,h=t; n=(qi+1)*DQ
        ok=(qi*DQ+lax.broadcasted_iota(jnp.int32,(n,DQ),1))>=low[:n]
        return jnp.where(ok,tdot(k_ref[:n],jnp.where(hm[h],q[qi*DQ:n],z)),NEG)
    def finish(t,m,l,p):
        qi,h=t; n=(qi+1)*DQ; sl=slice(qi*DQ,n)
        acc=dot(vt[h*64:(h+1)*64,:n],p)
        o_ref[0,h*64:(h+1)*64,sl]=acc*(1.0/l)
        l_ref[0,h:h+1,sl]=m+jnp.log(l)
    pipeline(tiles,scores,softmax_t,finish)
def pipeline(tiles,scores,mid,finish,depth=2):
    s=scores(tiles[0]); pend=None
    for i,t in enumerate(tiles):
        sn=scores(tiles[i+1]) if i+1<len(tiles) else None
        r=mid(s) if not isinstance(s,tuple) else mid(t,*s)
        if depth==2:
            if pend: finish(*pend)
            pend=(t,)+r
        else: finish(t,*r)
        s=sn
    if pend: finish(*pend)
CQ=512
def cross_fwd(place_ref, klen_ref, q_ref,k_ref,v_ref,od_ref,ld_ref,o_ref,l_ref):
    hm=head_masks()
    @pl.when(place_ref[0]==1)
    def _():
        q=q_ref[...]*jnp.asarray(0.125,bf16)
        vt=v_ref[...].T
        z=jnp.zeros((),bf16)
        tiles=[(qi,h) for qi in range(SP//CQ) for h in range(2)]
        res={}
        def scores(t):
            qi,h=t
            return tdot(k_ref[...],jnp.where(hm[h],q[qi*CQ:(qi+1)*CQ],z))
        def finish(t,m,l,p):
            qi,h=t; sl=slice(qi*CQ,(qi+1)*CQ)
            acc=dot(vt[h*64:(h+1)*64],p)
            ld=ld_ref[0,h:h+1,sl]
            lx=m+jnp.log(l)
            mx=jnp.maximum(ld,lx)
            ed=jnp.exp(ld-mx); ex=jnp.exp(lx-mx); tot=ed+ex
            l_ref[0,h:h+1,sl]=mx+jnp.log(tot)
            res[t]=od_ref[0,h*64:(h+1)*64,sl]*(ed/tot)+acc*(ex/(tot*l))
            if h==1: o_ref[sl]=jnp.concatenate([res[(qi,0)],res[(qi,1)]],0).T.astype(bf16)
        pipeline(tiles,scores,softmax_t,finish)
    @pl.when(place_ref[0]==0)
    def _():
        o_ref[...]=od_ref[0].T.astype(bf16)
        l_ref[...]=ld_ref[...]
KB=256
def bwd_prep(q_ref,do_ref,hm):
    q=q_ref[...]*jnp.asarray(0.125,bf16)
    z=jnp.zeros((),bf16)
    do=do_ref[...]
    return [jnp.where(hm[h],q,z) for h in range(2)],[jnp.where(hm[h],do,z) for h in range(2)]
def bwd_tiles(k_ref,v_ref,qm,dm,lrow,drow,put,dqt,start,mask,KB):
    tiles=[(kb,h) for kb in range(SP//KB) for h in range(2)]
    acc={}
    kts={}
    def scores(t):
        kb,h=t; ks=slice(kb*KB,(kb+1)*KB); q0=start(kb)
        return tdot(k_ref[ks],qm[h][q0:]),tdot(v_ref[ks],dm[h][q0:])
    def mid(t,s,dp):
        kb,h=t; q0=start(kb)
        p=jnp.exp(s-lrow(h)[:,q0:])
        if mask is not None: p=jnp.where(mask(kb),p,0.0)
        ds=p*(dp-drow(h)[:,q0:])
        return p.astype(bf16),ds.astype(bf16)
    def finish(t,p,ds):
        kb,h=t; ks=slice(kb*KB,(kb+1)*KB); q0=start(kb)
        if h==0: kts[kb]=k_ref[ks].T
        a=dot(p,dm[h][q0:]); b=dot(ds,qm[h][q0:])
        if h==0: acc[kb]=(a,b)
        else:
            put(ks,(acc[kb][1]+b).astype(bf16),(acc[kb][0]+a).astype(bf16))
        c=dot(kts[kb][h*64:(h+1)*64],ds)
        if kb==0: dqt[h*64:(h+1)*64]=c
        else: dqt[h*64:(h+1)*64,q0:]+=c
    pipeline(tiles,scores,mid,finish)
def cross_bwd(place_ref, klen_ref, q_ref,k_ref,v_ref,do_ref,o_ref,l_ref,dq_ref,dkv_ref,dl_ref,dqt):
    hm=head_masks()
    prod=do_ref[...].astype(f32)*o_ref[...].astype(f32)
    t=prod.T
    dl_ref[0,0:1]=jnp.sum(t[:64],0,keepdims=True); dl_ref[0,1:2]=jnp.sum(t[64:],0,keepdims=True)
    @pl.when(place_ref[0]==1)
    def _():
        def put(ks,dk,dv):
            dkv_ref[0,ks]=dk
            dkv_ref[1,ks]=dv
        qm,dm=bwd_prep(q_ref,do_ref,hm)
        bwd_tiles(k_ref,v_ref,qm,dm,lambda h:l_ref[0,h:h+1],lambda h:dl_ref[0,h:h+1],put,dqt,lambda kb:0,None,512)
        dq_ref[...]=dqt[...].T*0.125
    @pl.when(place_ref[0]==0)
    def _():
        dkv_ref[...]=jnp.zeros_like(dkv_ref); dq_ref[...]=jnp.zeros_like(dq_ref)
def diag_bwd(place_ref, klen_ref, q_ref,k_ref,v_ref,do_ref,l_ref,dl_ref,dqx_ref,out_ref,dqt):
    hm=head_masks(); klen=klen_ref[0]
    qm,dm=bwd_prep(q_ref,do_ref,hm)
    def put(ks,dk,dv):
        out_ref[1,ks]=dk
        out_ref[2,ks]=dv
    kpos=lax.broadcasted_iota(jnp.int32,(SP,1),0)
    low=jnp.where(kpos<klen,kpos,SP)
    def mask(kb):
        q0=kb*KB
        return q0+lax.broadcasted_iota(jnp.int32,(KB,SP-q0),1)>=low[q0:q0+KB]
    bwd_tiles(k_ref,v_ref,qm,dm,lambda h:l_ref[0,h:h+1],lambda h:dl_ref[0,h:h+1],put,dqt,lambda kb:kb*KB,mask,KB)
    out_ref[0]=(dqt[...].T*0.125+dqx_ref[...]).astype(bf16)
S=jax.ShapeDtypeStruct
def col(base,rows=SP): return pl.BlockSpec((rows,128),lambda j,*_:(0,base+j))
def cols(n,base): return pl.BlockSpec((n,SP,128),lambda j,*_:(0,0,base+j))
def row(base): return pl.BlockSpec((1,8,SP),lambda j,*_:(base+j,0,0))
ROW=row(0)
def call(fn,place,klen,ins,in_specs,outs,out_specs,scratch=(),pairs=NP,into=None,after=(),flops=0,trans=0):
    into=into or {}
    extra=list(into.items())
    n=2+len(ins)
    m=len(extra)
    skip=n+m+len(after)
    def kern(*refs): return fn(*refs[:n],*refs[skip:])
    specs=list(in_specs)+[pl.BlockSpec(memory_space=pl.ANY)]*(m+len(after))
    return pl.pallas_call(kern,
        grid_spec=pltpu.PrefetchScalarGridSpec(num_scalar_prefetch=2,grid=(pairs,),in_specs=specs,out_specs=out_specs,scratch_shapes=list(scratch)),
        out_shape=outs,
        input_output_aliases={n+i:o for i,(o,_) in enumerate(extra)},
        compiler_params=pltpu.CompilerParams(vmem_limit_bytes=50*1024*1024,dimension_semantics=("arbitrary",)),
        cost_estimate=pl.CostEstimate(flops=flops,bytes_accessed=pairs*10**4,transcendentals=trans),
        name=fn.__name__,
    )(place,klen,*ins,*[x for _,x in extra],*after)


BITS = {"c": ("dp", 1), "y": ("dp", 2), "u": ("dp", 4), "v": ("dp", 8), "x": ("blk", 1)}
LOW = "xyuv"
ORDERS = ("xyuv", "yuxv", "uxyv")
RB = 48


def swap(a, bit):
    axis, step = BITS[bit] if isinstance(bit, str) else ("dp", bit)
    return lax.ppermute(a, axis, [(i, i ^ step) for i in range(lax.axis_size(axis))])


def outer_steps():
    size = lax.axis_size("dp")
    return [1 << k for k in range(4, 16) if (1 << k) < size]


def my_id():
    place = 0
    for bit in "c" + LOW:
        axis, step = BITS[bit]
        place = 2 * place + (lax.axis_index(axis) // step) % 2
    return place.astype(jnp.int32).reshape(1)


def add(a, b):
    return (a.astype(f32) + b.astype(f32)).astype(bf16)


def core_step(keeps, sends):
    state = []
    for keep, send in zip(keeps, sends):
        a = add(keep, swap(send, "c"))
        state.append((a.reshape((2,) * 4 + a.shape[1:]), LOW))
    return state


def low_step(state, step, after=None):
    waiting = []
    for (a, bits), order in zip(state, ORDERS):
        at = bits.index(order[step])
        keep, send = lax.index_in_dim(a, 0, at, False), lax.index_in_dim(a, 1, at, False)
        waiting.append((keep, swap(send, order[step]), bits.replace(order[step], "")))
    if after is not None:
        flat = lambda a: a.reshape(-1, a.shape[-1])
        sums = sum_kernel([(flat(keep), flat(got)) for keep, got, _ in waiting], after, "step_sum")
        return [(a.reshape(keep.shape), bits) for a, (keep, _, bits) in zip(sums, waiting)]
    return [(add(keep, got), bits) for keep, got, bits in waiting]


def sum_kernel(pairs, after, name):
    n = len(pairs)

    def kern(*refs):
        for i in range(n):
            a, b = refs[i][...], refs[n + i][...]
            refs[i - n][...] = (a.astype(f32) + b.astype(f32)).astype(a.dtype)

    vmem = pl.BlockSpec(memory_space=pltpu.VMEM)
    return pl.pallas_call(
        kern,
        in_specs=[vmem] * (2 * n) + [pl.BlockSpec(memory_space=pl.ANY)] * len(after),
        out_specs=[vmem] * n,
        out_shape=[S(a.shape, a.dtype) for a, _ in pairs],
        name=name,
    )(*[a for a, _ in pairs], *[b for _, b in pairs], *after)


def last_step(state, after):
    keep = jnp.stack([a[0] for a, _ in state])
    got = swap(jnp.stack([a[1] for a, _ in state]), ORDERS[0][3])
    (total,) = sum_kernel([(keep, got)], after, "last_sum")
    for step in outer_steps():
        total = add(total, swap(total, step))
    return total


def outer_sum(blocks):
    for step in outer_steps():
        blocks = [add(a, swap(a, step)) for a in blocks]
    return blocks


def reduce_parts(keeps, sends):
    state = core_step(keeps, sends)
    for step in range(4):
        state = low_step(state, step)
    return outer_sum([a for a, _ in state])


def spread_parts(blocks):
    state = [a[None] for a in blocks]
    for step in (3, 2, 1, 0):
        state = [jnp.concatenate([a, swap(a, o[step])], 0) for a, o in zip(state, ORDERS)]
    return state, [swap(a, "c") for a in state]


def sum_small(a):
    for bit in "c" + LOW:
        a = a + swap(a, bit)
    for step in outer_steps():
        a = a + swap(a, step)
    return a


def low_index(p, order):
    r = 0
    for bit in order:
        r = 2 * r + (p // (1 << (3 - LOW.index(bit)))) % 2
    return r


def gather_all(blocks):
    a = lax.all_gather(blocks, ("dp", "blk"), axis=0, tiled=False)
    return a[:32]


def device_of(block):
    c, x, y, u, v = [(block // (1 << (4 - i))) % 2 for i in range(5)]
    return (v * 8 + u * 4 + y * 2 + c) * 2 + x


def unpack_early(gathered):
    rows = 4

    def kern(*refs):
        ins, (fc, proj, out) = refs[: 2 * rows], refs[2 * rows :]
        for core in range(2):
            for r in range(rows):
                a = ins[core * rows + r]
                at = slice(r * RB, (r + 1) * RB)
                fc[at, core * 1536 : core * 1536 + 1152] = a[0, 0].astype(f32)
                fc[at, core * 1536 + 1152 : (core + 1) * 1536] = a[0, 1, :, :384].astype(f32)
                proj[core, 2 * r * RB : (2 * r + 1) * RB] = a[0, 1, :, 384:].astype(f32)
                proj[core, (2 * r + 1) * RB : (2 * r + 2) * RB] = a[0, 2, :, :768].astype(f32)
                out[at, core * 384 : (core + 1) * 384] = a[0, 2, :, 768:].astype(f32)

    block = (1,) + gathered.shape[1:]
    return pl.pallas_call(
        kern,
        grid=(16 // rows,),
        in_specs=[
            pl.BlockSpec(block, lambda b, core=core, r=r: (device_of(core * 16 + b * rows + r), 0, 0, 0))
            for core in range(2) for r in range(rows)
        ],
        out_specs=[
            pl.BlockSpec((rows * RB, 4 * W), lambda b: (b, 0)),
            pl.BlockSpec((2, 2 * rows * RB, W), lambda b: (0, b, 0)),
            pl.BlockSpec((rows * RB, W), lambda b: (b, 0)),
        ],
        out_shape=[S((W, 4 * W), f32), S((2, 2 * W, W), f32), S((W, W), f32)],
        compiler_params=pltpu.CompilerParams(vmem_limit_bytes=56 * 1024 * 1024),
        cost_estimate=pl.CostEstimate(flops=0, bytes_accessed=3 * gathered.size * 2, transcendentals=0),
        name="unpack_early",
    )(*[gathered] * (2 * rows))


def unpack_late(me, mine, other, after):
    n = len(mine)
    rows = 8
    lanes = mine[0].shape[2]

    def kern(me_ref, *refs):
        own, far, out = refs[:n], refs[n : 2 * n], refs[-1]
        core, low = me_ref[0] // 16, me_ref[0] % 16
        step = pl.program_id(0)

        def fill(half, ins):
            for r in range(rows):
                place = (step * rows + r) ^ low
                for part in range(n):
                    at = (half * n + part) * lanes
                    out[r * RB : (r + 1) * RB, at : at + lanes] = ins[part][low_index(place, ORDERS[part])].astype(f32)

        for half in range(2):
            @pl.when(core == half)
            def _():
                fill(half, own)

            @pl.when(core != half)
            def _():
                fill(half, far)

    whole = pl.BlockSpec(mine[0].shape, lambda b, *_: (0, 0, 0))
    return pl.pallas_call(
        kern,
        grid_spec=pltpu.PrefetchScalarGridSpec(
            num_scalar_prefetch=1, grid=(16 // rows,), in_specs=[whole] * (2 * n) + [pl.BlockSpec(memory_space=pl.ANY)] * len(after),
            out_specs=pl.BlockSpec((rows * RB, 3 * W), lambda b, *_: (b, 0)),
        ),
        out_shape=S((W, 3 * W), f32),
        compiler_params=pltpu.CompilerParams(vmem_limit_bytes=56 * 1024 * 1024),
        cost_estimate=pl.CostEstimate(flops=0, bytes_accessed=10**7, transcendentals=0),
        name="unpack_late",
    )(me, *mine, *other, *after)


MR = 256
QR = 512
FC = 1536
C0 = 0.7978845608028654
C1 = C0 * 0.044715


def rowmean(a):
    return jnp.sum(a, -1, keepdims=True) * (1.0 / W)


def block_kernel(
    klen_ref, x_ref, att_ref, up_ref, d_act_ref, w_out_ref, w_fc_ref, w_proj_ref, b_out_ref, gain_ref, shift_ref, b_proj_ref, b_fc_ref,
    y_ref, act_ref, pre_ref, mid_ref, gatt_ref, do_ref, sums_ref, bsum_ref,
):
    step = pl.program_id(0)

    @pl.when(step == 0)
    def _():
        sums_ref[...] = jnp.zeros_like(sums_ref)
        bsum_ref[...] = jnp.zeros_like(bsum_ref)

    up = up_ref[...].astype(f32)
    branch_att = dot(att_ref[...], w_out_ref[...]) + b_out_ref[...][None]
    middle = x_ref[...].astype(f32) + branch_att
    centered = middle - rowmean(middle)
    inv = lax.rsqrt(rowmean(centered * centered) + EPS)
    x_hat = centered * inv
    gain = gain_ref[...][None]
    normed = (x_hat * gain + shift_ref[...][None]).astype(bf16)
    mid_ref[...] = normed
    chunks = range(4 * W // FC)
    sl = lambda c: slice(c * FC, (c + 1) * FC)

    def first(c):
        return dot(normed, w_fc_ref[:, sl(c)])

    mlp = None
    back = None
    ahead = first(0)
    for c in chunks:
        u = ahead
        if c + 1 < len(chunks):
            ahead = first(c + 1)
        u = u + b_fc_ref[sl(c)][None]
        v = u * u
        h = 0.5 + 0.5 * jnp.tanh(u * (C0 + C1 * v))
        z = (u * h).astype(bf16)
        d = d_act_ref[:, sl(c)].astype(f32) * (h + (u * (2 * C0 + 6 * C1 * v)) * (h * (1.0 - h)))
        bsum_ref[0:1, sl(c)] += jnp.sum(d, 0, keepdims=True)
        d = d.astype(bf16)
        act_ref[:, sl(c)] = z
        pre_ref[:, sl(c)] = d
        a = dot(z, w_proj_ref[sl(c)])
        b = tdot(d, w_fc_ref[:, sl(c)])
        mlp = a if mlp is None else mlp + a
        back = b if back is None else back + b
    branch_mlp = mlp + b_proj_ref[...][None]
    out = middle + branch_mlp
    y_ref[...] = out.astype(bf16)
    scaled = back * gain
    grad = up + inv * (scaled - rowmean(scaled) - x_hat * rowmean(scaled * x_hat))
    gatt = grad.astype(bf16)
    gatt_ref[...] = gatt
    do_ref[...] = tdot(gatt, w_out_ref[...]).astype(bf16)
    valid = step * MR + lax.broadcasted_iota(jnp.int32, (MR, 1), 0) < klen_ref[0]
    total = lambda a: jnp.sum(a, 0, keepdims=True)
    kept = lambda a: total(jnp.where(valid, a * a, 0.0))
    sums_ref[...] += jnp.concatenate(
        [total(back * x_hat), total(back), total(grad), total(up), kept(out), kept(branch_att), kept(branch_mlp),
         jnp.zeros((1, W), f32)], 0,
    )


def block_call(klen, x, att, up, d_act, w_out, w_fc, w_proj, b_out, gain, shift, b_proj, b_fc):
    once = pl.Buffered(1)
    rows = lambda width: pl.BlockSpec((MR, width), lambda i, *_: (i, 0))
    whole = lambda shape: pl.BlockSpec(shape, lambda i, *_: (0, 0), pipeline_mode=once)
    const = lambda shape: pl.BlockSpec(shape, lambda i, *_: (0, 0))
    line = lambda size: pl.BlockSpec((size,), lambda i, *_: (0,))
    return pl.pallas_call(
        block_kernel,
        grid_spec=pltpu.PrefetchScalarGridSpec(
            num_scalar_prefetch=1,
            grid=(SP // MR,),
            in_specs=[rows(W)] * 3 + [rows(4 * W), whole((W, W)), whole((W, 4 * W)), whole((4 * W, W)), line(W), line(W), line(W), line(W), line(4 * W)],
            out_specs=[rows(W), rows(4 * W), rows(4 * W), rows(W), rows(W), rows(W), const((8, W)), const((1, 4 * W))],
        ),
        out_shape=[
            S((SP, W), bf16), S((SP, 4 * W), bf16), S((SP, 4 * W), bf16), S((SP, W), bf16),
            S((SP, W), bf16), S((SP, W), bf16), S((8, W), f32), S((1, 4 * W), f32),
        ],
        compiler_params=pltpu.CompilerParams(vmem_limit_bytes=56 * 1024 * 1024),
        cost_estimate=pl.CostEstimate(flops=17 * 10**9, bytes_accessed=41 * 10**6, transcendentals=3 * 10**6),
        name="block_mlp",
    )(klen, x, att, up, d_act, w_out, w_fc, w_proj, b_out, gain, shift, b_proj, b_fc)


def grads_kernel(
    me_ref, mid_ref, pre_ref, act_ref, up_hbm, att_hbm, gatt_hbm, k0, k1, k2, s0, s1, s2, mid_t, up_ref, att_ref, gatt_ref, sems
):
    step = pl.program_id(0)
    core, low = me_ref[0] // 16, me_ref[0] % 16

    copies = [
        pltpu.make_async_copy(source, target, sems.at[i])
        for i, (source, target) in enumerate(((up_hbm, up_ref), (att_hbm, att_ref), (gatt_hbm, gatt_ref)))
    ]

    @pl.when(step == 0)
    def _():
        for copy in copies:
            copy.start()
        mid_t[...] = mid_ref[...].T

    @pl.when(step == 4)
    def _():
        for copy in copies:
            copy.wait()

    def by_core(half, fill, keep, send):
        @pl.when(half == core)
        def _():
            fill(*keep)

        @pl.when(half != core)
        def _():
            fill(*send)

    @pl.when(step < 4)
    def _():
        tile = dot(mid_t[...], pre_ref[...]).astype(bf16)

        def left(one):
            for i in range(16):
                one[i ^ low, :, :768] = tile[i * RB : (i + 1) * RB]

        def right(one, two):
            for i in range(16):
                one[i ^ low, :, 768:] = tile[i * RB : (i + 1) * RB, :384]
                two[i ^ low, :, :384] = tile[i * RB : (i + 1) * RB, 384:]

        @pl.when(step % 2 == 0)
        def _():
            by_core(step // 2, left, (k0,), (s0,))

        @pl.when(step % 2 == 1)
        def _():
            by_core(step // 2, right, (k0, k1), (s0, s1))

    @pl.when((step >= 4) & (step < 8))
    def _():
        tile = rows_dot(act_ref[...], up_ref[...]).astype(bf16)
        first = (step - 4) % 2 * 8

        def fill(one, two):
            for i in range(8):
                at = (first + i) ^ low
                one[at, :, 384:] = tile[2 * i * RB : (2 * i + 1) * RB]
                two[at, :, :768] = tile[(2 * i + 1) * RB : (2 * i + 2) * RB]

        by_core((step - 4) // 2, fill, (k1, k2), (s1, s2))

    @pl.when(step == 8)
    def _():
        tile = rows_dot(att_ref[...], gatt_ref[...]).astype(bf16)

        def fill(one, two):
            for i in range(16):
                one[i ^ low, :, 768:] = tile[i * RB : (i + 1) * RB, :384]
                two[i ^ low, :, 768:] = tile[i * RB : (i + 1) * RB, 384:]

        by_core(0, fill, (k2, s2), (s2, k2))


def grads_call(me, mid, pre, act, up, att, gatt):
    clip = lambda i, lo, hi: jnp.clip(i, lo, hi) - lo
    whole = pl.BlockSpec((SP, W), lambda i, *_: (0, 0))
    part = pl.BlockSpec((16, RB, 1152), lambda i, *_: (0, 0, 0))
    res = pl.pallas_call(
        grads_kernel,
        grid_spec=pltpu.PrefetchScalarGridSpec(
            num_scalar_prefetch=1,
            grid=(9,),
            in_specs=[
                whole,
                pl.BlockSpec((SP, W), lambda i, *_: (0, clip(i, 0, 3))),
                pl.BlockSpec((SP, W), lambda i, *_: (0, clip(i, 4, 7))),
            ] + [pl.BlockSpec(memory_space=pl.ANY)] * 3,
            out_specs=[part] * 6,
            scratch_shapes=[pltpu.VMEM((W, SP), bf16)] + [pltpu.VMEM((SP, W), bf16)] * 3 + [pltpu.SemaphoreType.DMA((3,))],
        ),
        out_shape=[S((16, RB, 1152), bf16)] * 6,
        compiler_params=pltpu.CompilerParams(vmem_limit_bytes=56 * 1024 * 1024),
        cost_estimate=pl.CostEstimate(flops=11 * 10**9, bytes_accessed=30 * 10**6, transcendentals=0),
        name="block_grads",
    )(me, mid, pre, act, up, att, gatt)
    return res[:3], res[3:]


def late_kernel(me_ref, a_ref, ar_ref, d_ref, dr_ref, k0, k1, k2, s0, s1, s2, a_t, ar_t):
    step = pl.program_id(0)
    core, low = me_ref[0] // 16, me_ref[0] % 16

    def put(keep, send, tile):
        def fill(ref):
            for i in range(16):
                ref[i ^ low] = tile[i * RB : (i + 1) * RB]

        return lambda half: (
            pl.when(core == half)(lambda: fill(keep)),
            pl.when(core != half)(lambda: fill(send)),
        )

    @pl.when(step == 0)
    def _():
        a_t[...] = a_ref[...].T
        ar_t[...] = ar_ref[...].T
        tile = dot(a_t[...], d_ref[0]).astype(bf16)
        put(k0, s0, tile[:, :384])(0)
        put(k1, s1, tile[:, 384:])(0)

    @pl.when(step == 1)
    def _():
        tile = (dot(a_t[...], d_ref[0]) + dot(ar_t[...], dr_ref[0])).astype(bf16)
        put(k2, s2, tile[:, :384])(0)
        put(k0, s0, tile[:, 384:])(1)

    @pl.when(step == 2)
    def _():
        tile = (dot(a_t[...], d_ref[0]) + dot(ar_t[...], dr_ref[0])).astype(bf16)
        put(k1, s1, tile[:, :384])(1)
        put(k2, s2, tile[:, 384:])(1)


def late_call(me, a, ar, d, dr, after):
    def kern(*refs):
        return late_kernel(*refs[:5], *refs[5 + len(after) :])

    whole = pl.BlockSpec((SP, W), lambda i, *_: (0, 0))
    part = pl.BlockSpec((16, RB, 384), lambda i, *_: (0, 0, 0))
    res = pl.pallas_call(
        kern,
        grid_spec=pltpu.PrefetchScalarGridSpec(
            num_scalar_prefetch=1,
            grid=(3,),
            in_specs=[
                whole,
                whole,
                pl.BlockSpec((1, SP, W), lambda i, *_: (i, 0, 0)),
                pl.BlockSpec((1, SP, W), lambda i, *_: (jnp.maximum(i - 1, 0), 0, 0)),
            ] + [pl.BlockSpec(memory_space=pl.ANY)] * len(after),
            out_specs=[part] * 6,
            scratch_shapes=[pltpu.VMEM((W, SP), bf16)] * 2,
        ),
        out_shape=[S((16, RB, 384), bf16)] * 6,
        compiler_params=pltpu.CompilerParams(vmem_limit_bytes=56 * 1024 * 1024),
        cost_estimate=pl.CostEstimate(flops=6 * 10**9, bytes_accessed=14 * 10**6, transcendentals=0),
        name="late_grads",
    )(me, a, ar, d, dr, *after)
    return res[:3], res[3:]


def qkv_call(x, w_qkv, b_query, b_value, gain, shift, n, after, name):
    def kern(x_ref, w_ref, bq_ref, bv_ref, gain_ref, shift_ref, *refs):
        a_ref, out_ref = refs[len(after) :]
        a = (norm_one(x_ref)[0] * gain_ref[...][None] + shift_ref[...][None]).astype(bf16)
        a_ref[...] = a
        if n == 3:
            out_ref[:, :W] = (dot(a, w_ref[:, :W]) + bq_ref[...][None]).astype(bf16)
        out_ref[:, (n - 2) * W : (n - 1) * W] = dot(a, w_ref[:, W : 2 * W]).astype(bf16)
        out_ref[:, (n - 1) * W :] = (dot(a, w_ref[:, 2 * W :]) + bv_ref[...][None]).astype(bf16)

    rows = lambda width: pl.BlockSpec((QR, width), lambda i: (i, 0))
    return pl.pallas_call(
        kern,
        grid=(SP // QR,),
        in_specs=[
            rows(W),
            pl.BlockSpec((W, 3 * W), lambda i: (0, 0)),
        ] + [pl.BlockSpec((W,), lambda i: (0,))] * 4 + [pl.BlockSpec(memory_space=pl.ANY)] * len(after),
        out_specs=[rows(W), rows(n * W)],
        out_shape=[S((SP, W), bf16), S((SP, n * W), bf16)],
        compiler_params=pltpu.CompilerParams(vmem_limit_bytes=56 * 1024 * 1024),
        cost_estimate=pl.CostEstimate(flops=n * 12 * 10**8, bytes_accessed=10**7, transcendentals=0),
        name=name,
    )(x, w_qkv, b_query, b_value, gain, shift, *after)


def norm_one(x_ref):
    x = x_ref[...].astype(f32)
    centered = x - rowmean(x)
    inv = lax.rsqrt(rowmean(centered * centered) + EPS)
    return centered * inv, inv


def input_kernel(x_ref, d_ref, w_ref, gain_ref, *refs):
    n = d_ref.shape[0]
    sums_ref = refs[-1]

    @pl.when(pl.program_id(0) == 0)
    def _():
        sums_ref[...] = jnp.zeros_like(sums_ref)

    x_hat, inv = norm_one(x_ref)
    part = None
    for i in range(n):
        a = tdot(d_ref[i], w_ref[:, (3 - n + i) * W : (4 - n + i) * W])
        part = a if part is None else part + a
    total = lambda a: jnp.sum(a.astype(f32), 0, keepdims=True)
    first = total(d_ref[0]) if n == 3 else jnp.zeros((1, W), f32)
    sums_ref[...] += jnp.concatenate(
        [first, total(d_ref[n - 1]), total(part * x_hat), total(part), jnp.zeros((4, W), f32)], 0
    )
    if n == 2:
        refs[0][...] = part.astype(bf16)
    else:
        returned_ref, gatt_ref = refs[:2]
        scaled = (part + returned_ref[0].astype(f32)) * gain_ref[...][None]
        inner = scaled - rowmean(scaled) - x_hat * rowmean(scaled * x_hat)
        refs[-2][...] = (gatt_ref[...].astype(f32) + inv * inner).astype(bf16)


def input_call(side, x, d, w_qkv, gain, extra, after, name):
    n = d.shape[0]
    rows = pl.BlockSpec((QR, W), lambda i, *_: (i, 0))
    more = [pl.BlockSpec((1, QR, W), lambda i, side_ref: (side_ref[0], i, 0)), rows] if extra else []
    skip = 5 + len(extra)

    def kern(*refs):
        return input_kernel(*refs[1:skip], *refs[skip + len(after) :])

    return pl.pallas_call(
        kern,
        grid_spec=pltpu.PrefetchScalarGridSpec(
            num_scalar_prefetch=1,
            grid=(SP // QR,),
            in_specs=[
                rows,
                pl.BlockSpec((n, QR, W), lambda i, *_: (0, i, 0)),
                pl.BlockSpec((W, 3 * W), lambda i, *_: (0, 0)),
                pl.BlockSpec((W,), lambda i, *_: (0,)),
            ] + more + [pl.BlockSpec(memory_space=pl.ANY)] * len(after),
            out_specs=[rows, pl.BlockSpec((8, W), lambda i, *_: (0, 0))],
        ),
        out_shape=[S((SP, W), bf16), S((8, W), f32)],
        compiler_params=pltpu.CompilerParams(vmem_limit_bytes=56 * 1024 * 1024),
        cost_estimate=pl.CostEstimate(flops=n * 12 * 10**8, bytes_accessed=10**7, transcendentals=0),
        name=name,
    )(side, x, d, w_qkv, gain, *extra, *after)


def swap_spans(x):
    return lax.ppermute(x, "blk", [(0, 1), (1, 0)])


def rows_dot(left, right):
    return lax.dot_general(left, right, (((0,), (0,)), ((), ())), preferred_element_type=f32)


def body(
    inputs, cotangent, lengths, groups, flip,
    w_qkv, b_query, b_value, w_out, b_out, gain_one, shift_one, gain_two, shift_two,
    w_fc, b_fc, w_proj, b_proj,
):
    place = jnp.bitwise_xor(lax.axis_index("blk"), flip[0])
    klen = jnp.minimum(lengths[0] - place * SP, SP)
    place_s = place.reshape(1).astype(jnp.int32)
    klen_s = klen.reshape(1).astype(jnp.int32)
    x_b = inputs[0, 0]
    up_b = cotangent[0, 0]
    xr_b = swap_spans(x_b)

    normed, qkv = qkv_call(x_b, w_qkv, b_query, b_value, gain_one, shift_one, 3, (), "own_qkv")
    c = col(0)
    tall = pl.BlockSpec((1, 128, SP), lambda j, *_: (j, 0, 0))
    od, ld = call(
        diag_fwd, place_s, klen_s, (qkv, qkv, qkv), [c, col(6), col(12)],
        [S((NP, 128, SP), f32), S((NP, 8, SP), f32)], [tall, ROW],
    )

    d_act = tdot(up_b, w_proj).astype(bf16)
    normed_r, kvr = qkv_call(xr_b, w_qkv, b_query, b_value, gain_one, shift_one, 2, (ld, d_act), "other_kv")
    attended, lse = call(
        cross_fwd, place_s, klen_s, (qkv, kvr, kvr, od, ld), [c, c, col(6), tall, ROW],
        [S((SP, W), bf16), S((NP, 8, SP), f32)], [c, ROW],
    )

    outputs, activ, grad_pre, normed_two, grad_att, grad_attended, sums, grad_b_fc = block_call(
        klen_s, x_b, attended, up_b, d_act, w_out, w_fc, w_proj, b_out, gain_two, shift_two, b_proj, b_fc
    )
    me = my_id()
    keeps, sends = grads_call(me, normed_two, grad_pre, activ, up_b, attended, grad_att)
    acc = pltpu.VMEM((128, SP), f32)
    flops = 8 * 10**9
    dqx = dkvr = delta = dqkv = None

    def cross_piece(at, pairs, dep):
        nonlocal dqx, dkvr, delta
        dqx, dkvr, delta = call(
            cross_bwd, place_s, klen_s, (qkv, kvr, kvr, grad_attended, attended, lse),
            [col(at), col(at), col(6 + at), col(at), col(at), row(at)],
            [S((SP, W), f32), S((2, SP, W), bf16), S((NP, 8, SP), f32)],
            [col(at), cols(2, at), row(at)], [acc], pairs=pairs,
            into={0: dqx, 1: dkvr, 2: delta} if at else None, after=dep, flops=flops * pairs,
        )

    def diag_piece(at, pairs, dep):
        nonlocal dqkv
        (dqkv,) = call(
            diag_bwd, place_s, klen_s, (qkv, qkv, qkv, grad_attended, lse, delta, dqx),
            [col(at), col(6 + at), col(12 + at), col(at), row(at), row(at), col(at)],
            [S((3, SP, W), bf16)], [cols(3, at)], [acc], pairs=pairs,
            into={0: dqkv} if at else None, after=dep, flops=flops * pairs // 2,
        )

    arrays = lambda state: [a for a, _ in state]
    gain = gain_one
    side = (1 - lax.axis_index("blk")).astype(jnp.int32).reshape(1)
    cross_piece(0, 1, keeps)
    state = core_step(keeps, sends)
    cross_piece(1, 3, arrays(state))
    state = low_step(state, 0)
    cross_piece(4, 2, arrays(state))
    part_r, sums_r = input_call(side, xr_b, dkvr, w_qkv, gain, (), (), "other_span")
    returned = lax.all_gather(part_r, "blk", axis=0, tiled=False)
    state = low_step(state, 1)
    state = low_step(state, 2)
    diag_piece(0, 3, arrays(state) + [part_r])
    early_sum = last_step(state, [dqkv])
    diag_piece(3, 3, [early_sum])
    early = unpack_early(gather_all(early_sum))

    state = core_step(*late_call(me, normed, normed_r, dqkv, dkvr, []))
    input_grad, sums_o = input_call(
        side, x_b, dqkv, w_qkv, gain, (returned, grad_att), arrays(state), "input_grad"
    )
    state = low_step(state, 0, [sums_o])
    state = low_step(state, 1)
    state = low_step(state, 2)
    state = low_step(state, 3)
    late = unpack_late(me, *spread_parts(outer_sum(arrays(state))), [early[0]])

    member = (groups[0] == jnp.arange(2, dtype=jnp.int32)).astype(f32)
    squares = jnp.concatenate([jnp.sum(sums[4:7], 1), klen.astype(f32)[None]])
    sums_one = sums_o + sums_r
    small = jnp.concatenate([
        sums_one[0], sums_one[1], sums[2], sums_one[2], sums_one[3], sums[0], sums[1], grad_b_fc[0], sums[3],
        (member[:, None] * squares[None, :]).reshape(-1), jnp.zeros((1016,), f32),
    ])
    small = sum_small(small.reshape(80, 128)).reshape(-1)
    sizes = [W] * 7 + [4 * W, W]
    pieces = []
    at = 0
    for size in sizes:
        pieces.append(small[at : at + size])
        at += size
    table = small[at : at + 8].reshape(2, 4)
    group_rms = jnp.sqrt(table[:, :3] / (table[:, 3:] * W))
    g_bq, g_bv, g_bo, g_g1, g_s1, g_g2, g_s2, g_bfc, g_bp = pieces
    return (
        outputs[None, None], input_grad[None, None], late, g_bq, g_bv, early[2], g_bo, g_g1, g_s1, g_g2, g_s2,
        early[0], g_bfc, early[1].reshape(4 * W, W), g_bp, group_rms,
    )


def solution(mesh):
    span = P("dp", "blk", None, None)
    return jax.shard_map(
        body,
        mesh=mesh,
        in_specs=(span, span, P("dp"), P("dp"), P("dp")) + (P(),) * 13,
        out_specs=(span, span) + (P(),) * 14,
        check_vma=False,
    )
```
